128 devices in a mesh: ctx: 8 (over x_hi, y), tp: 16 (over z, x_lo, core).
Axes of the slice: x: 4 (x_hi: 2, x_lo: 2; x = x_hi * 2 + x_lo), y: 4, z: 4, core: 2. Of those that a mesh axis runs over, the one named last changes fastest.
Arguments:
- moe_input: bfloat16 [1024, 6144], P('ctx', 'tp'), may hold values from -6 to 6
- grad_output: bfloat16 [1024, 6144], P('ctx', 'tp'), may hold values from -6 to 6
- expert_ids: int32 [1024, 2], P('ctx'), may hold values from 0 to 7, all different within a row; in each aligned block of 128 rows (0 to 127, 128 to 255, ...) at most 64 rows name the same one
- route_weights: float32 [1024, 2], P('ctx'), may hold values from 0.1 to 0.9
- w_gate: bfloat16 [8, 6144, 8192], P('ctx', None, 'tp'), may hold values from -0.078125 to 0.078125
- w_up: bfloat16 [8, 6144, 8192], P('ctx', None, 'tp'), may hold values from -0.078125 to 0.078125
- w_down: bfloat16 [8, 8192, 6144], P('ctx', 'tp'), may hold values from -0.0625 to 0.0625
- queries: bfloat16 [1024, 6144], P('ctx', 'tp'), may hold values from -9 to 9
- keys_values: bfloat16 [1024, 2048], P('ctx'), may hold values from -9 to 9
- out_proj: bfloat16 [6144, 6144], P('tp'), may hold values from -0.078125 to 0.078125
Outputs:
- grad_hidden: bfloat16 [1024, 6144], P('ctx', 'tp')
- grad_query: bfloat16 [1024, 6144], P('ctx', 'tp')
- grad_kv: bfloat16 [1024, 2048], P('ctx', 'tp')
- grad_out_proj_t: bfloat16 [6144, 6144], P('ctx', 'tp')
The draws below stay inside these ranges and needn't reach their ends.
Inputs may be any that keep to these rules, and one draw needn't show every extreme that they name: `expert_ids`: in the 128 tokens of one index of ctx no expert is named by more than 64 tokens, a bound that some block reaches; the two ids of a token differ.
All inputs are finite; a program needn't handle non-finite values.
Results may differ from the reference program's by a relative error of at most 0.03.
Values may be sent and summed in bfloat16 or wider, within the bound.
No kernel may reach another device: no remote copies, remote signals or barrier semaphores. Data moves between devices by JAX's collectives and lax.ppermute only.
A program may use at most 128 MiB of HBM per device.

```python
import math
import jax
import jax.numpy as jnp
import numpy as np
from jax import lax

D = 6144
HQ = 48
KVH = 8
HD = 128
FF = 8192
TOK_DEV = 128
EXPERTS = 8
CAP = 64
S = 1024
N_CTX = 8


def draw_keys_values(key, part):
    key = jax.random.fold_in(key, 11)
    raw_draw = jnp.clip(jax.random.normal(key, (S, KVH, 2, HD), jnp.float32), -6.0, 6.0)
    return raw_draw.reshape(S, KVH * 2 * HD).astype(jnp.bfloat16)


def draw_queries(key, part):
    key = jax.random.fold_in(key, 23)
    raw_draw = jnp.clip(jax.random.normal(key, (S, HQ, HD), jnp.float32), -6.0, 6.0)
    return raw_draw.reshape(S, HQ * HD).astype(jnp.bfloat16)


def shard_levels(key, dims, split, low, largest):
    loudness, own = 1.0, jax.random.fold_in(key, 6)
    for axis_at, shards_of in split:
        steps = jnp.exp(jax.random.uniform(jax.random.fold_in(own, axis_at), (shards_of,), jnp.float32, low / len(split), largest / len(split)))
        loudness = loudness * jnp.repeat(steps, dims[axis_at] // shards_of).reshape([-1 if axis == axis_at else 1 for axis in range(len(dims))])
    return loudness


def routed_block(own_key, own, number, rows, amount, top, bound, skew):
    order = jax.random.permutation(own_key, amount)
    crowded, common = load_shares(amount, rows * top, bound, skew, True), load_shares(amount, rows * top, bound, skew, False)
    places = jnp.arange(amount)

    def named(lengths, rotation):
        used = int((lengths > 0).sum())
        fixed = max(1, used // 4)
        moved = fixed + (places - fixed + rotation * (used - fixed)) % max(1, amount - fixed)
        return jnp.zeros((amount,), jnp.int32).at[order[jnp.where(places < fixed, places, moved)]].set(jnp.asarray(lengths, jnp.int32))

    lengths = jnp.where(number % 4 == 0, named(crowded, number // 4), named(common, number - number // 4 - 1))
    mixed = jax.random.permutation(jax.random.fold_in(own, 3), amount)
    donor, taker = mixed[0:amount // 2 * 2:2], mixed[1:amount // 2 * 2:2]
    room = jnp.minimum(lengths[donor] - 1, bound - lengths[taker]) // 2
    room = jnp.where((donor == order[0]) | (taker == order[0]) | (lengths[taker] == 0), 0, jnp.maximum(room, 0))
    moved = jax.random.randint(jax.random.fold_in(own, 4), (amount // 2,), 0, 1 << 20) % (room + 1)
    lengths = lengths.at[donor].add(-moved).at[taker].add(moved)
    members = jnp.searchsorted(jnp.cumsum(lengths), jnp.arange(rows * top), side="right").astype(jnp.int32)
    listing = members.reshape(top, rows).T
    listing = listing[jax.random.permutation(jax.random.fold_in(own, 1), rows)]
    rotation = jax.random.randint(jax.random.fold_in(own, 2), (rows, 1), 0, top)
    return jnp.take_along_axis(listing, (jnp.arange(top)[None, :] + rotation) % top, axis=1)


def load_shares(amount, total, bound, slope, full):
    loads = [(1 << 20) // math.isqrt(grade ** slope) + 1 for grade in range(1, amount + 1)]
    largest = bound if full else min(bound, max(-(-total // amount), total * loads[0] // sum(loads)))
    least = 1 if total - largest >= amount - 1 else 0
    holding, spare = [largest] + [least] * (amount - 1), total - largest - least * (amount - 1)
    while spare > 0:
        free = [i for i in range(1, amount) if holding[i] < largest] or [i for i in range(1, amount) if holding[i] < bound]
        whole, budget = sum([loads[i] for i in free]), spare
        for i in free:
            more = min(bound - holding[i], max(1, budget * loads[i] // whole), spare)
            holding[i] = holding[i] + more
            spare = spare - more
    return np.array(holding)


def gaussian(stream_key, shape, width, most, split=(), kind=jnp.bfloat16):
    level = shard_levels(stream_key, shape, split, -0.22, 0.18) if split else 1.0
    values = jax.random.normal(stream_key, shape, jnp.float32) * width * level
    return jnp.minimum(jnp.maximum(values, -most), most).astype(kind)


def setup_inputs(seed: int = 0) -> dict:
    splits = jax.random.split(jax.random.key(seed), 11)
    moe_input = gaussian(splits[0], (S, D), 1.0, 6.0, ((0, 8), (1, 16)))
    grad_output = gaussian(splits[1], (S, D), 1.0, 6.0, ((0, 8), (1, 16)))
    expert_ids_keys = jax.random.split(jax.random.fold_in(splits[2], 1), S // TOK_DEV)
    expert_ids_turns = jax.random.permutation(jax.random.fold_in(splits[2], 3), S // TOK_DEV)
    expert_ids = jax.vmap(lambda own, number: routed_block(jax.random.fold_in(splits[2], 2), own, number, TOK_DEV, EXPERTS, 2, CAP, 2))(expert_ids_keys, expert_ids_turns).reshape((S, 2))
    route_weights = jnp.clip(0.1 + 0.79999997 * jax.random.uniform(splits[3], (S, 2), jnp.float32) ** shard_levels(splits[3], (S, 2), ((0, 8),), -0.2, 0.2), 0.1, 0.9)
    w_gate = gaussian(splits[4], (EXPERTS, D, FF), D ** -0.5, 0.078125, ((0, 8), (2, 16)))
    w_up = gaussian(splits[5], (EXPERTS, D, FF), D ** -0.5, 0.078125, ((0, 8), (2, 16)))
    w_down = gaussian(splits[6], (EXPERTS, FF, D), FF ** -0.5, 0.0625, ((0, 8), (1, 16)))
    queries = draw_queries(jax.random.fold_in(splits[10], 71), 0)
    keys_values = draw_keys_values(jax.random.fold_in(splits[10], 71), 0)
    out_proj = gaussian(splits[9], (HQ * HD, D), (HQ * HD) ** -0.5, 0.078125, ((0, 16),))
    return {"moe_input": moe_input, "grad_output": grad_output, "expert_ids": expert_ids, "route_weights": route_weights, "w_gate": w_gate, "w_up": w_up, "w_down": w_down, "queries": queries, "keys_values": keys_values, "out_proj": out_proj}


def expert_scan(moe_input, grad_output, expert_ids, route_weights, w_gate, w_up, w_down):
    tokens = moe_input.shape[0]
    model_width = moe_input.shape[1]
    slot_rows = N_CTX * CAP
    flat_ids = expert_ids.reshape(-1).astype(jnp.int32)
    owners = (jnp.arange(2 * tokens, dtype=jnp.int32) // 2).astype(jnp.int32)
    flat_weights = route_weights.reshape(-1).astype(jnp.float32)

    def one_expert(totals, packed):
        gate_w, up_w, down_w, number = packed
        chosen = flat_ids == number
        slot_rank = (jnp.cumsum(chosen.astype(jnp.int32)) - 1).astype(jnp.int32)
        slot_pos = jnp.where(chosen, slot_rank, slot_rows).astype(jnp.int32)
        holder = jnp.zeros((slot_rows + 1,), jnp.int32).at[slot_pos].set(owners)[:slot_rows]
        route_scale = jnp.zeros((slot_rows + 1,), jnp.float32).at[slot_pos].set(flat_weights)[:slot_rows]
        x_rows = moe_input[holder]
        dy_rows = grad_output[holder]
        gate_act = jnp.dot(x_rows, gate_w, preferred_element_type=jnp.float32)
        up_act = jnp.dot(x_rows, up_w, preferred_element_type=jnp.float32)
        hidden_grad = jnp.dot(dy_rows, down_w.T, preferred_element_type=jnp.float32)
        sigmoid_g = jax.nn.sigmoid(gate_act)
        grad_gate = (hidden_grad * up_act * sigmoid_g * (1.0 + gate_act * (1.0 - sigmoid_g))).astype(jnp.bfloat16)
        grad_up = (hidden_grad * gate_act * sigmoid_g).astype(jnp.bfloat16)
        routed = jnp.dot(grad_gate, gate_w.T, preferred_element_type=jnp.float32)
        routed = routed + jnp.dot(grad_up, up_w.T, preferred_element_type=jnp.float32)
        totals = totals.at[holder].add(routed * route_scale[:, None])
        return (totals, None)
    start_sum = jnp.zeros((tokens, model_width), jnp.float32)
    numbers = jnp.arange(EXPERTS, dtype=jnp.int32)
    totals, _ = lax.scan(one_expert, start_sum, (w_gate, w_up, w_down, numbers))
    return totals

def attention_backward(queries, keys_values, out_proj, grad_hidden):
    tokens = queries.shape[0]
    inv_root = 1.0 / math.sqrt(HD)
    q_heads = queries.reshape(tokens, HQ, HD).transpose(1, 0, 2)
    kv_blocks = keys_values.reshape(tokens, KVH, 2, HD)
    key_heads = kv_blocks[:, :, 0, :].transpose(1, 0, 2)
    value_heads = kv_blocks[:, :, 1, :].transpose(1, 0, 2)
    grad_context = jnp.dot(grad_hidden, out_proj.T, preferred_element_type=jnp.float32).astype(jnp.bfloat16)
    grad_heads = grad_context.reshape(tokens, HQ, HD).transpose(1, 0, 2)
    causal = jnp.arange(tokens)[:, None] >= jnp.arange(tokens)[None, :]
    group_of = (jnp.arange(HQ, dtype=jnp.int32) // (HQ // KVH)).astype(jnp.int32)

    def one_head(packed):
        query_rows, grad_out, kv_group = packed
        key_rows = key_heads[kv_group]
        value_rows = value_heads[kv_group]
        scores = jnp.dot(query_rows, key_rows.T, preferred_element_type=jnp.float32) * inv_root
        scores = jnp.where(causal, scores, -1e+30)
        row_max = lax.optimization_barrier(jnp.max(scores, axis=1, keepdims=True))
        exp_scores = jnp.exp(scores - row_max)
        attn_prob = exp_scores / lax.optimization_barrier(jnp.sum(exp_scores, axis=1, keepdims=True))
        prob_b = attn_prob.astype(jnp.bfloat16)
        context = jnp.dot(prob_b, value_rows, preferred_element_type=jnp.float32).astype(jnp.bfloat16)
        grad_prob = jnp.dot(grad_out, value_rows.T, preferred_element_type=jnp.float32)
        row_delta = lax.optimization_barrier(jnp.sum(grad_out.astype(jnp.float32) * context.astype(jnp.float32), axis=1, keepdims=True))
        grad_score = (attn_prob * (grad_prob - row_delta)).astype(jnp.bfloat16)
        grad_q = (jnp.dot(grad_score, key_rows, preferred_element_type=jnp.float32) * inv_root).astype(jnp.bfloat16)
        grad_k = jnp.dot(grad_score.T, query_rows, preferred_element_type=jnp.float32) * inv_root
        grad_v = jnp.dot(prob_b.T, grad_out, preferred_element_type=jnp.float32)
        return (context, grad_q, grad_k, grad_v)
    contexts, grad_q, grad_k, grad_v = lax.map(one_head, (q_heads, grad_heads, group_of))
    attn_out = contexts.transpose(1, 0, 2).reshape(tokens, HQ * HD)
    grad_query = grad_q.transpose(1, 0, 2).reshape(tokens, HQ * HD)
    key_sums = grad_k.reshape(KVH, HQ // KVH, tokens, HD).sum(axis=1)
    value_sums = grad_v.reshape(KVH, HQ // KVH, tokens, HD).sum(axis=1)
    stacked = jnp.stack([key_sums, value_sums], axis=1).transpose(2, 0, 1, 3)
    grad_kv = stacked.reshape(tokens, KVH * 2 * HD).astype(jnp.bfloat16)
    grad_out_proj_t = jnp.dot(grad_hidden.T, attn_out, preferred_element_type=jnp.float32).astype(jnp.bfloat16)
    return (grad_query, grad_kv, grad_out_proj_t)

def reference(moe_input, grad_output, expert_ids, route_weights, w_gate, w_up, w_down, queries, keys_values, out_proj):
    moe_grad = expert_scan(moe_input, grad_output, expert_ids, route_weights, w_gate, w_up, w_down)
    grad_hidden = (grad_output.astype(jnp.float32) + moe_grad).astype(jnp.bfloat16)
    grad_query, grad_kv, grad_out_proj_t = attention_backward(queries, keys_values, out_proj, grad_hidden)
    return (grad_hidden, grad_query, grad_kv, grad_out_proj_t)
```

```python
import math

import jax
import jax.numpy as jnp
from jax import lax
from jax.experimental import pallas as pl
from jax.experimental.pallas import tpu as pltpu
from jax.sharding import PartitionSpec as P

HQ = 48
KVH = 8
HD = 128
Z = 4
BF16 = jnp.bfloat16
F32 = jnp.float32


def tp_move(block, dz=0, dx=0, dc=0):
    route = []
    for src in range(Z * 4):
        z, low = src // 4, src % 4
        route.append((src, ((z + dz) % Z) * 4 + (low ^ (dx * 2 + dc))))
    return lax.ppermute(block, "tp", route)


def route_tables(expert_ids, route_weights, groups, capacity):
    tokens = expert_ids.shape[0]
    flat_ids = expert_ids.reshape(-1)
    numbers = jnp.arange(groups, dtype=jnp.int32)
    hits = (flat_ids[:, None] == numbers[None, :]).astype(jnp.int32)
    earlier = jnp.cumsum(hits, axis=0) - hits
    slot_rank = jnp.sum(earlier * hits, axis=1)
    targets = (flat_ids * capacity + slot_rank).reshape(tokens, 2)
    slot_index = jnp.arange(groups * capacity, dtype=jnp.int32)[:, None]
    first_hit = slot_index == targets[None, :, 0]
    second_hit = slot_index == targets[None, :, 1]
    placing = (first_hit | second_hit).astype(BF16)
    combine = jnp.where(first_hit, route_weights[None, :, 0], 0.0) + jnp.where(
        second_hit, route_weights[None, :, 1], 0.0
    )
    return (placing, combine)


def swiglu_grads(gate_act, up_act, hidden_grad):
    sigmoid_g = jax.nn.sigmoid(gate_act)
    grad_gate = (hidden_grad * up_act * sigmoid_g * (1.0 + gate_act * (1.0 - sigmoid_g))).astype(
        BF16
    )
    grad_up = (hidden_grad * gate_act * sigmoid_g).astype(BF16)
    return (grad_gate, grad_up)


def contract_last(left, right):
    return lax.dot_general(left, right, (((1,), (1,)), ((), ())), preferred_element_type=F32)


def add_bf16(*terms):
    total = terms[0].astype(F32)
    for term in terms[1:]:
        total = total + term.astype(F32)
    return total.astype(BF16)


def routed_kernel(chunk_ref, gg_ref, gu_ref, wg_ref, wu_ref, out_ref):
    out_ref[0] = (
        contract_last(gg_ref[...], wg_ref[...]) + contract_last(gu_ref[...], wu_ref[...])
    ).astype(BF16)


def routed_chunks(chunks, grad_gate, grad_up, gate_w, up_w, width):
    count = chunks.shape[0]
    rows, hidden = grad_gate.shape
    whole = pl.BlockSpec((rows, hidden), lambda i, ids: (0, 0))
    weight = pl.BlockSpec((width, hidden), lambda i, ids: (ids[i], 0))
    return pl.pallas_call(
        routed_kernel,
        grid_spec=pltpu.PrefetchScalarGridSpec(
            num_scalar_prefetch=1,
            grid=(count,),
            in_specs=[whole, whole, weight, weight],
            out_specs=pl.BlockSpec((1, rows, width), lambda i, ids: (i, 0, 0)),
        ),
        out_shape=jax.ShapeDtypeStruct((count, rows, width), BF16),
        compiler_params=pltpu.CompilerParams(vmem_limit_bytes=24 * 2**20),
        cost_estimate=pl.CostEstimate(
            flops=4 * count * rows * width * hidden,
            bytes_accessed=count * (4 * width * hidden + 2 * rows * width) + 4 * rows * hidden,
            transcendentals=0,
        ),
    )(chunks, grad_gate, grad_up, gate_w, up_w)


def context_kernel(chunk_ref, left_ref, weight_ref, out_ref, total):
    step = pl.program_id(0)

    @pl.when(step == 0)
    def _():
        total[...] = jnp.zeros_like(total)

    total[...] += contract_last(left_ref[0], weight_ref[...])

    @pl.when(step == pl.num_programs(0) - 1)
    def _():
        out_ref[...] = total[...].astype(BF16)


def context_grad(chunks, pieces, weight):
    count, rows, width = pieces.shape
    outs = weight.shape[0]
    return pl.pallas_call(
        context_kernel,
        grid_spec=pltpu.PrefetchScalarGridSpec(
            num_scalar_prefetch=1,
            grid=(count,),
            in_specs=[
                pl.BlockSpec((1, rows, width), lambda i, ids: (i, 0, 0)),
                pl.BlockSpec((outs, width), lambda i, ids: (0, ids[i])),
            ],
            out_specs=pl.BlockSpec((rows, outs), lambda i, ids: (0, 0)),
            scratch_shapes=[pltpu.VMEM((rows, outs), F32)],
        ),
        out_shape=jax.ShapeDtypeStruct((rows, outs), BF16),
        compiler_params=pltpu.CompilerParams(vmem_limit_bytes=16 * 2**20),
        cost_estimate=pl.CostEstimate(
            flops=2 * count * rows * width * outs,
            bytes_accessed=2 * count * width * (outs + rows),
            transcendentals=0,
        ),
    )(chunks, pieces, weight)


def per_device(
    moe_input,
    grad_output,
    expert_ids,
    route_weights,
    w_gate,
    w_up,
    w_down,
    queries,
    keys_values,
    out_proj,
):
    ctx_count = lax.axis_size("ctx")
    tp_rank = lax.axis_index("tp")
    ctx_rank = lax.axis_index("ctx")
    my_z, my_x, my_core = tp_rank // 4, (tp_rank // 2) % 2, tp_rank % 2
    tokens, features = moe_input.shape
    capacity = tokens // 2
    slot_rows = ctx_count * capacity
    gate_w, up_w, down_w = w_gate[0], w_up[0], w_down[0]

    def chunk_of(dz, dx, dc):
        return ((my_z + dz) % Z) * 4 + (my_x ^ dx) * 2 + (my_core ^ dc)

    placing, combine = route_tables(expert_ids, route_weights, ctx_count, capacity)
    both = jnp.concatenate([moe_input, grad_output], axis=1)
    send = jnp.dot(placing, both, preferred_element_type=F32).astype(BF16)
    got = lax.all_to_all(
        send.reshape(ctx_count, capacity, 2 * features), "ctx", split_axis=0, concat_axis=0, tiled=True
    ).reshape(slot_rows, 2 * features)

    heads_here = queries.shape[1] // HD
    group_size = HQ // KVH
    kv_group = tp_rank * heads_here // group_size
    mine_kv = lax.dynamic_slice_in_dim(keys_values, kv_group * 2 * HD, 2 * HD, 1)
    all_kv = lax.all_gather(mine_kv, "ctx", axis=0, tiled=True)
    seq_len = all_kv.shape[0]
    key_rows, value_rows = all_kv[:, :HD], all_kv[:, HD:]
    query_heads = queries.reshape(tokens, heads_here, HD)
    inv_root = 1.0 / math.sqrt(HD)
    query_pos = ctx_rank * tokens + jnp.arange(tokens, dtype=jnp.int32)
    causal = query_pos[:, None] >= jnp.arange(seq_len, dtype=jnp.int32)[None, :]
    scores = jnp.einsum("qhd,kd->hqk", query_heads, key_rows, preferred_element_type=F32) * inv_root
    scores = jnp.where(causal[None], scores, -1e30)
    row_max = jnp.max(scores, axis=2, keepdims=True)
    exp_scores = jnp.exp(scores - row_max)
    attn_prob = exp_scores / jnp.sum(exp_scores, axis=2, keepdims=True)
    prob_b = attn_prob.astype(BF16)
    context_heads = jnp.einsum("hqk,kd->qhd", prob_b, value_rows, preferred_element_type=F32).astype(
        BF16
    )
    context = context_heads.reshape(tokens, heads_here * HD)
    all_context = lax.all_gather(context, "ctx", axis=0, tiled=True)

    got_x, got_dy = got[:, :features], got[:, features:]
    half = slot_rows // 2

    def x_term(piece, dz, dx, dc):
        start = chunk_of(-dz, dx, dc) * features
        gate_rows = lax.dynamic_slice_in_dim(gate_w, start, features, 0)
        up_rows = lax.dynamic_slice_in_dim(up_w, start, features, 0)
        return (
            jnp.dot(piece, gate_rows, preferred_element_type=F32),
            jnp.dot(piece, up_rows, preferred_element_type=F32),
        )

    def dy_term(piece, dz, dx, dc):
        start = chunk_of(-dz, dx, dc) * features
        return contract_last(piece, lax.dynamic_slice_in_dim(down_w, start, features, 1))

    dy_z = {0: got_dy, 1: tp_move(got_dy, dz=1), 3: tp_move(got_dy, dz=3)}
    x_pair = jnp.concatenate([got_x, tp_move(got_x, dx=1)], axis=0)
    dy_far = (tp_move(dy_z[1][:half], dz=1), tp_move(dy_z[3][half:], dz=3))
    dy_z[2] = jnp.concatenate(dy_far, axis=0)
    x_z = {0: x_pair, 1: tp_move(x_pair, dz=1), 3: tp_move(x_pair, dz=3)}
    dy_x = {dz: tp_move(dy_z[dz], dx=1) for dz in (0, 1, 3, 2)}
    x_far = (tp_move(x_z[1][:slot_rows], dz=1), tp_move(x_z[3][slot_rows:], dz=3))
    x_z[2] = jnp.concatenate(x_far, axis=0)

    gate_act = up_act = hidden_grad = None
    for dz in (0, 1, 3, 2):
        for dx in (0, 1):
            piece = (dy_z, dy_x)[dx][dz]
            other = tp_move(piece, dc=1)
            term = dy_term(piece, dz, dx, 0) + dy_term(other, dz, dx, 1)
            hidden_grad = term if hidden_grad is None else hidden_grad + term
        other = tp_move(x_z[dz], dc=1)
        for dc, pair in ((0, x_z[dz]), (1, other)):
            for dx in (0, 1):
                piece = pair[dx * slot_rows : (dx + 1) * slot_rows]
                gate_term, up_term = x_term(piece, dz, dx, dc)
                gate_act = gate_term if gate_act is None else gate_act + gate_term
                up_act = up_term if up_act is None else up_act + up_term
    grad_gate, grad_up = swiglu_grads(gate_act, up_act, hidden_grad)

    pair_sum = {}
    for group in ((2,), (1, 3), (0,)):
        places = [(dz, dx) for dz in group for dx in (0, 1)]
        away = jnp.stack([chunk_of(dz, dx, 1) for dz, dx in places])
        stay = jnp.stack([chunk_of(dz, dx, 0) for dz, dx in places])
        sent = routed_chunks(away, grad_gate, grad_up, gate_w, up_w, features)
        arrived = tp_move(sent, dc=1)
        kept = routed_chunks(stay, grad_gate, grad_up, gate_w, up_w, features)
        for i, place in enumerate(places):
            pair_sum[place] = (kept[i], arrived[i])

    def first(dz, dx):
        kept, arrived = pair_sum[dz, dx]
        return add_bf16(kept[:half], arrived[:half])

    def second(dz, dx):
        kept, arrived = pair_sum[dz, dx]
        return add_bf16(kept[half:], arrived[half:])

    def sum_along_z(own):
        cut = own[2].shape[0] // 2
        up_far = tp_move(own[2][:cut], dz=1)
        down_far = tp_move(own[2][cut:], dz=3)
        up = jnp.concatenate([add_bf16(own[1][:cut], up_far), own[1][cut:]], axis=0)
        down = jnp.concatenate([own[3][:cut], add_bf16(own[3][cut:], down_far)], axis=0)
        return own[0], tp_move(up, dz=1), tp_move(down, dz=3)

    along_z = {
        dz: jnp.concatenate([second(dz, 0), second(dz, 1)], axis=1) for dz in (2, 1, 3, 0)
    }
    second_sum = add_bf16(*sum_along_z(along_z))
    second_sum = add_bf16(second_sum[:, :features], tp_move(second_sum[:, features:], dx=1))
    along_x = {}
    for group in ((2,), (1, 3), (0,)):
        crossed = tp_move(jnp.concatenate([first(dz, 1) for dz in group], axis=0), dx=1)
        for i, dz in enumerate(group):
            along_x[dz] = add_bf16(first(dz, 0), crossed[i * half : (i + 1) * half])
    first_sum = add_bf16(*sum_along_z(along_x))
    own_slice = jnp.concatenate([first_sum, second_sum], axis=0)

    returned = lax.all_to_all(
        own_slice.reshape(ctx_count, capacity, features), "ctx", split_axis=0, concat_axis=0, tiled=True
    ).reshape(slot_rows, features)
    moe_part = lax.dot_general(
        combine,
        returned.astype(F32),
        (((0,), (0,)), ((), ())),
        precision=lax.Precision.HIGHEST,
        preferred_element_type=F32,
    )
    grad_hidden = (grad_output.astype(F32) + moe_part).astype(BF16)

    cut = tokens // 2
    low, high = grad_hidden[:cut], grad_hidden[cut:]
    low_pair = jnp.stack([low, tp_move(low, dx=1)])
    high_z = jnp.stack([high] + [tp_move(high, dz=dz) for dz in (1, 2, 3)])
    low_all = jnp.stack([low_pair] + [tp_move(low_pair, dz=dz) for dz in (1, 2, 3)])
    high_all = jnp.stack([high_z, tp_move(high_z, dx=1)], axis=1)
    same_core = jnp.concatenate([low_all, high_all], axis=2)
    other_core = tp_move(same_core, dc=1)
    hidden_pieces = jnp.stack([same_core, other_core]).reshape(Z * 4, tokens, features)
    hidden_chunks = jnp.stack(
        [chunk_of(-dz, dx, dc) for dc in (0, 1) for dz in range(Z) for dx in (0, 1)]
    )
    grad_context = context_grad(hidden_chunks, hidden_pieces, out_proj)

    swapped = jnp.where(my_x == 0, same_core, same_core[:, ::-1])
    ordered = jnp.stack([swapped[0], swapped[3], swapped[2], swapped[1]])
    ordered = lax.dynamic_slice_in_dim(
        jnp.concatenate([ordered, ordered], axis=0), (Z - my_z) % Z, Z, 0
    )
    column_own = lax.all_to_all(
        ordered.reshape(ctx_count, tokens, features), "ctx", split_axis=0, concat_axis=0, tiled=True
    ).reshape(seq_len, features)
    column_other = tp_move(column_own, dc=1)

    grad_heads = grad_context.reshape(tokens, heads_here, HD)
    grad_prob = jnp.einsum("qhd,kd->hqk", grad_heads, value_rows, preferred_element_type=F32)
    row_delta = jnp.sum(grad_heads.astype(F32) * context_heads.astype(F32), axis=2)
    grad_score = (attn_prob * (grad_prob - row_delta.T[:, :, None])).astype(BF16)
    grad_query = (
        jnp.einsum("hqk,kd->qhd", grad_score, key_rows, preferred_element_type=F32) * inv_root
    ).astype(BF16)
    grad_query = grad_query.reshape(tokens, heads_here * HD)
    key_term = (
        jnp.einsum("hqk,qhd->kd", grad_score, query_heads, preferred_element_type=F32) * inv_root
    )
    value_term = jnp.einsum("hqk,qhd->kd", prob_b, grad_heads, preferred_element_type=F32)
    kept_term = jnp.where(my_core == 0, key_term, value_term)
    sent_term = jnp.where(my_core == 0, value_term, key_term).astype(BF16)
    pair_term = (kept_term + tp_move(sent_term, dc=1).astype(F32)).astype(BF16)
    kv_blocks = lax.all_to_all(
        pair_term.reshape(ctx_count, tokens, HD), "ctx", split_axis=0, concat_axis=0, tiled=True
    )
    grad_kv = jnp.sum(kv_blocks.astype(F32), axis=0).astype(BF16)

    def over_tokens(left):
        return lax.dot_general(
            left, all_context, (((0,), (0,)), ((), ())), preferred_element_type=F32
        ).astype(BF16)

    own_rows, other_rows = over_tokens(column_own), over_tokens(column_other)
    grad_out_proj_t = jnp.concatenate(
        [
            jnp.where(my_core == 0, own_rows, other_rows),
            jnp.where(my_core == 0, other_rows, own_rows),
        ],
        axis=0,
    )
    return (grad_hidden, grad_query, grad_kv, grad_out_proj_t)


def solution(mesh):
    in_specs = (
        P("ctx", "tp"),
        P("ctx", "tp"),
        P("ctx", None),
        P("ctx", None),
        P("ctx", None, "tp"),
        P("ctx", None, "tp"),
        P("ctx", "tp", None),
        P("ctx", "tp"),
        P("ctx", None),
        P("tp", None),
    )
    out_specs = (P("ctx", "tp"), P("ctx", "tp"), P("ctx", "tp"), P("ctx", "tp"))
    return jax.shard_map(
        per_device, mesh=mesh, in_specs=in_specs, out_specs=out_specs, check_vma=False
    )
```

```python
import math

import jax
import jax.numpy as jnp
from jax import lax
from jax.experimental import pallas as pl
from jax.experimental.pallas import tpu as pltpu
from jax.sharding import PartitionSpec as P

HQ = 48
KVH = 8
HD = 128
Z = 4
BF16 = jnp.bfloat16
F32 = jnp.float32


def tp_move(block, dz=0, dx=0, dc=0):
    route = []
    for src in range(Z * 4):
        z, low = src // 4, src % 4
        route.append((src, ((z + dz) % Z) * 4 + (low ^ (dx * 2 + dc))))
    return lax.ppermute(block, "tp", route)


def core_move(block, zero, one):
    route = []
    for src in range(Z * 4):
        z, low = src // 4, src % 4
        dz, dx = (zero, one)[src % 2]
        route.append((src, ((z + dz) % Z) * 4 + (low ^ (dx * 2))))
    return lax.ppermute(block, "tp", route)


def double_ctx(held, bit):
    route = [(c, c ^ (1 << bit)) for c in range(lax.axis_size("ctx"))]
    came = lax.ppermute(held, "ctx", route)
    upper = (lax.axis_index("ctx") >> bit) & 1 == 1
    axis = 0 if bit == 2 else 1
    return jnp.stack([jnp.where(upper, came, held), jnp.where(upper, held, came)], axis=axis)


def gather_y(held):
    held = double_ctx(double_ctx(held, 0), 1)
    return held.reshape(-1, *held.shape[4:])


def route_tables(expert_ids, route_weights, groups, capacity):
    tokens = expert_ids.shape[0]
    flat_ids = expert_ids.reshape(-1)
    numbers = jnp.arange(groups, dtype=jnp.int32)
    hits = (flat_ids[:, None] == numbers[None, :]).astype(jnp.int32)
    earlier = jnp.cumsum(hits, axis=0) - hits
    slot_rank = jnp.sum(earlier * hits, axis=1)
    targets = (flat_ids * capacity + slot_rank).reshape(tokens, 2)
    slot_index = jnp.arange(groups * capacity, dtype=jnp.int32)[:, None]
    first_hit = slot_index == targets[None, :, 0]
    second_hit = slot_index == targets[None, :, 1]
    placing = (first_hit | second_hit).astype(BF16)
    combine = jnp.where(first_hit, route_weights[None, :, 0], 0.0) + jnp.where(
        second_hit, route_weights[None, :, 1], 0.0
    )
    return (placing, combine)


def swiglu_grads(gate_act, up_act, hidden_grad):
    sigmoid_g = jax.nn.sigmoid(gate_act)
    grad_gate = (hidden_grad * up_act * sigmoid_g * (1.0 + gate_act * (1.0 - sigmoid_g))).astype(
        BF16
    )
    grad_up = (hidden_grad * gate_act * sigmoid_g).astype(BF16)
    return (grad_gate, grad_up)


def contract_last(left, right):
    return lax.dot_general(left, right, (((1,), (1,)), ((), ())), preferred_element_type=F32)


def add_bf16(*terms):
    total = terms[0].astype(F32)
    for term in terms[1:]:
        total = total + term.astype(F32)
    return total.astype(BF16)


def context_kernel(ids_ref, own_ref, other_ref, weight_ref, out_ref, total):
    step = pl.program_id(0)
    width = own_ref.shape[-1]
    first_core = ids_ref[Z] == 0

    @pl.when(step == 0)
    def _():
        total[...] = jnp.zeros_like(total)

    for x in (0, 1):
        own, other = own_ref[0, x], other_ref[0, x]
        for core, piece in (
            (0, jnp.where(first_core, own, other)),
            (1, jnp.where(first_core, other, own)),
        ):
            start = (x * 2 + core) * width
            total[...] += contract_last(piece, weight_ref[:, start : start + width])

    @pl.when(step == pl.num_programs(0) - 1)
    def _():
        out_ref[...] = total[...].astype(BF16)


def context_grad(ids, own, other, weight):
    count, _, rows, width = own.shape
    outs = weight.shape[0]
    pieces = pl.BlockSpec((1, 2, rows, width), lambda i, ids: (i, 0, 0, 0))
    return pl.pallas_call(
        context_kernel,
        grid_spec=pltpu.PrefetchScalarGridSpec(
            num_scalar_prefetch=1,
            grid=(count,),
            in_specs=[pieces, pieces, pl.BlockSpec((outs, 4 * width), lambda i, ids: (0, ids[i]))],
            out_specs=pl.BlockSpec((rows, outs), lambda i, ids: (0, 0)),
            scratch_shapes=[pltpu.VMEM((rows, outs), F32)],
        ),
        out_shape=jax.ShapeDtypeStruct((rows, outs), BF16),
        compiler_params=pltpu.CompilerParams(vmem_limit_bytes=8 * 2**20),
        cost_estimate=pl.CostEstimate(
            flops=8 * count * rows * width * outs,
            bytes_accessed=8 * count * width * (outs + rows),
            transcendentals=0,
        ),
    )(ids, own, other, weight)


def per_device(
    moe_input,
    grad_output,
    expert_ids,
    route_weights,
    w_gate,
    w_up,
    w_down,
    queries,
    keys_values,
    out_proj,
):
    ctx_count = lax.axis_size("ctx")
    tp_rank = lax.axis_index("tp")
    ctx_rank = lax.axis_index("ctx")
    my_z, my_x, my_core = tp_rank // 4, (tp_rank // 2) % 2, tp_rank % 2
    tokens, features = moe_input.shape
    capacity = tokens // 2
    slot_rows = ctx_count * capacity
    gate_w, up_w, down_w = w_gate[0], w_up[0], w_down[0]

    def chunk_of(dz, dx, dc):
        return ((my_z + dz) % Z) * 4 + (my_x ^ dx) * 2 + (my_core ^ dc)

    placing, combine = route_tables(expert_ids, route_weights, ctx_count, capacity)
    first_core = my_core == 0

    def in_core_order(own, other, axis):
        return jnp.concatenate(
            [jnp.where(first_core, own, other), jnp.where(first_core, other, own)], axis=axis
        )

    came = tp_move(jnp.where(first_core, moe_input, grad_output), dc=1)
    carried = in_core_order(jnp.where(first_core, grad_output, moe_input), came, 1)
    send = jnp.dot(placing, carried, preferred_element_type=F32).astype(BF16)
    got = lax.all_to_all(
        send.reshape(ctx_count, capacity, 2 * features), "ctx", split_axis=0, concat_axis=0, tiled=True
    ).reshape(slot_rows, 2 * features)

    heads_here = queries.shape[1] // HD
    group_size = HQ // KVH
    kv_group = tp_rank * heads_here // group_size
    mine_kv = lax.dynamic_slice_in_dim(keys_values, kv_group * 2 * HD, 2 * HD, 1)
    two_kv, got = lax.optimization_barrier((double_ctx(mine_kv, 2), got))
    seq_len = ctx_count * tokens
    query_heads = queries.reshape(tokens, heads_here, HD)
    inv_root = 1.0 / math.sqrt(HD)

    def attention_forward(all_kv):
        key_rows, value_rows = all_kv[:, :HD], all_kv[:, HD:]
        query_pos = ctx_rank * tokens + jnp.arange(tokens, dtype=jnp.int32)
        causal = query_pos[:, None] >= jnp.arange(seq_len, dtype=jnp.int32)[None, :]
        scores = (
            jnp.einsum("qhd,kd->hqk", query_heads, key_rows, preferred_element_type=F32) * inv_root
        )
        scores = jnp.where(causal[None], scores, -1e30)
        row_max = jnp.max(scores, axis=2, keepdims=True)
        exp_scores = jnp.exp(scores - row_max)
        attn_prob = exp_scores / jnp.sum(exp_scores, axis=2, keepdims=True)
        prob_b = attn_prob.astype(BF16)
        context_heads = jnp.einsum(
            "hqk,kd->qhd", prob_b, value_rows, preferred_element_type=F32
        ).astype(BF16)
        return context_heads, attn_prob, prob_b

    half, width = slot_rows // 2, 2 * features
    hop_1 = core_move(got, (1, 0), (0, 1))
    hop_2 = core_move(got, (3, 0), (1, 0))
    hop_3 = core_move(got, (0, 1), (3, 0))
    got_crossed, hop_3 = lax.optimization_barrier((tp_move(got, dc=1), hop_3))
    two_kv, hop_1 = lax.optimization_barrier((two_kv, hop_1))
    all_kv = gather_y(two_kv)
    far_low = core_move(jnp.where(first_core, hop_1[:half], hop_2[:half]), (1, 0), (1, 0))
    far_high = core_move(jnp.where(first_core, hop_2[half:], hop_3[half:]), (3, 0), (3, 0))
    hop_6 = core_move(hop_1, (0, 1), (1, 0))
    hop_7 = core_move(jnp.where(first_core, hop_2, hop_1), (0, 1), (3, 0))
    context_heads, attn_prob, prob_b = attention_forward(all_kv)
    context = context_heads.reshape(tokens, heads_here * HD)
    far = jnp.concatenate([far_low, far_high], axis=0)
    cross_low = core_move(jnp.where(first_core, far_low, hop_6[:half]), (0, 1), (1, 0))
    cross_high = core_move(jnp.where(first_core, far_high, hop_7[half:]), (0, 1), (3, 0))
    far_cross = jnp.concatenate([cross_low, cross_high], axis=0)
    far_cross, context = lax.optimization_barrier((far_cross, context))
    all_context = gather_y(double_ctx(context, 2))

    arrivals = (
        (got, (0, 0), (0, 0)),
        (hop_1, (3, 0), (0, 1)),
        (hop_2, (1, 0), (3, 0)),
        (hop_3, (0, 1), (1, 0)),
        (far, (2, 0), (2, 0)),
        (hop_6, (3, 1), (3, 1)),
        (hop_7, (1, 1), (1, 1)),
        (far_cross, (2, 1), (2, 1)),
    )
    gate_act = up_act = hidden_grad = 0.0
    for block, dy_from, x_from in arrivals:
        held = block
        if block is hop_1 or block is hop_2 or block is hop_3:
            held, _ = lax.optimization_barrier((block, far_low))
        crossed = got_crossed if block is got else tp_move(held, dc=1)
        x_rows = jnp.where(first_core, crossed, block)
        dy_rows = jnp.where(first_core, block, crossed)
        x_start = (chunk_of(*x_from, 0) // 2) * width
        dy_start = (chunk_of(*dy_from, 0) // 2) * width
        gate_rows = lax.dynamic_slice_in_dim(gate_w, x_start, width, 0)
        up_rows = lax.dynamic_slice_in_dim(up_w, x_start, width, 0)
        down_cols = lax.dynamic_slice_in_dim(down_w, dy_start, width, 1)
        gate_act = gate_act + jnp.dot(x_rows, gate_rows, preferred_element_type=F32)
        up_act = up_act + jnp.dot(x_rows, up_rows, preferred_element_type=F32)
        hidden_grad = hidden_grad + contract_last(dy_rows, down_cols)
    grad_gate, grad_up = swiglu_grads(gate_act, up_act, hidden_grad)

    def routed(dz, core_0, core_1, after):
        start = ((my_z + dz) % Z) * 2 * width
        if after is not None:
            start, after = lax.optimization_barrier((start, after))
        gate_rows = lax.dynamic_slice_in_dim(gate_w, start, 2 * width, 0)
        up_rows = lax.dynamic_slice_in_dim(up_w, start, 2 * width, 0)
        gate_half = jnp.where(first_core, grad_gate[core_0], grad_gate[core_1])
        up_half = jnp.where(first_core, grad_up[core_0], grad_up[core_1])
        result = (contract_last(gate_half, gate_rows) + contract_last(up_half, up_rows)).astype(BF16)
        return result, after

    lower, upper = slice(None, half), slice(half, None)
    order = (2, 1, 3, 0)
    sent, kept, after = {}, {}, None
    for i, dz in enumerate(order):
        sent[dz], done = routed(dz, upper, lower, after)
        if i:
            sent[order[i - 1]] = done
        after = sent[dz]
    near, cross = {}, {}
    for dz in order:
        kept[dz], _ = routed(dz, lower, upper, after)
        own = add_bf16(kept[dz], tp_move(sent[dz], dc=1))
        low_x, high_x = own[:, :width], own[:, width:]
        near[dz] = jnp.where(my_x == 0, low_x, high_x)
        cross[dz] = jnp.where(my_x == 0, high_x, low_x)

    cut = half // 2

    def stack_for(zero, one):
        return jnp.where(first_core, jnp.stack(zero), jnp.stack(one))

    def low(rows):
        return rows[:cut]

    def high(rows):
        return rows[cut:]

    def both(rows):
        return (low(rows), high(rows))

    sum_1 = core_move(stack_for(both(cross[2]), (low(near[2]), low(cross[2]))), (0, 1), (1, 0))
    sum_2 = core_move(stack_for(both(cross[1]), (high(near[2]), high(cross[2]))), (0, 1), (3, 0))
    sum_3 = core_move(stack_for(both(cross[3]), (high(near[1]), high(cross[1]))), (0, 1), (1, 0))
    sum_4 = core_move(stack_for(both(cross[0]), (low(near[3]), low(cross[3]))), (0, 1), (3, 0))
    over_2 = [add_bf16(low(near[2]), sum_1[0]), add_bf16(high(near[2]), sum_1[1])]
    over_1 = [add_bf16(low(near[1]), sum_2[0]), add_bf16(high(near[1]), sum_2[1])]
    over_3 = [add_bf16(low(near[3]), sum_3[0]), add_bf16(high(near[3]), sum_3[1])]
    down = [add_bf16(high(near[3]), sum_2[0]), add_bf16(high(cross[3]), sum_2[1])]
    up = [add_bf16(low(near[1]), sum_1[0]), add_bf16(low(cross[1]), sum_1[1])]
    sum_5 = core_move(stack_for((over_2[0], over_1[1]), down), (1, 0), (3, 0))
    sum_6 = core_move(stack_for((over_2[1], over_3[0]), up), (3, 0), (1, 0))
    z_near = [add_bf16(low(near[0]), sum_4[0], sum_6[0]), add_bf16(high(near[0]), sum_3[0], sum_5[0])]
    z_cross = [
        add_bf16(low(cross[0]), sum_4[1], sum_6[1]),
        add_bf16(high(cross[0]), sum_3[1], sum_5[1]),
    ]
    sum_7 = core_move(jnp.where(first_core, add_bf16(over_1[0], sum_5[0]), z_cross[0]), (1, 0), (0, 1))
    sum_8 = core_move(jnp.where(first_core, add_bf16(over_3[1], sum_6[0]), z_cross[1]), (3, 0), (0, 1))
    zero_low = add_bf16(low(near[0]), sum_4[0], sum_6[1], sum_7)
    zero_high = add_bf16(high(near[0]), sum_4[1], sum_5[1], sum_8)
    one_low, one_high = add_bf16(z_near[0], sum_7), add_bf16(z_near[1], sum_8)
    total = jnp.concatenate(
        [jnp.where(first_core, zero_low, one_low), jnp.where(first_core, zero_high, one_high)], axis=0
    )
    total, all_context = lax.optimization_barrier((total, all_context))
    left, right = total[:, :features], total[:, features:]
    came = tp_move(jnp.where(first_core, right, left), dc=1)
    own_slice = in_core_order(jnp.where(first_core, left, right), came, 0)

    returned = lax.all_to_all(
        own_slice.reshape(ctx_count, capacity, features), "ctx", split_axis=0, concat_axis=0, tiled=True
    ).reshape(slot_rows, features)
    moe_part = lax.dot_general(
        combine,
        returned.astype(F32),
        (((0,), (0,)), ((), ())),
        precision=lax.Precision.HIGHEST,
        preferred_element_type=F32,
    )
    grad_hidden = (grad_output.astype(F32) + moe_part).astype(BF16)

    cut = tokens // 2
    one_half, other_half = grad_hidden[:cut], grad_hidden[cut:]
    low_pair = jnp.stack([one_half, tp_move(one_half, dx=1)])
    high_z = jnp.stack([other_half] + [tp_move(other_half, dz=dz) for dz in (1, 2, 3)])
    low_all = jnp.stack([low_pair] + [tp_move(low_pair, dz=dz) for dz in (1, 2, 3)])
    high_all = jnp.stack([high_z, tp_move(high_z, dx=1)], axis=1)
    same_core = jnp.concatenate([low_all, high_all], axis=2)
    swapped = jnp.where(my_x == 0, same_core, same_core[:, ::-1])
    ordered = jnp.stack([swapped[0], swapped[3], swapped[2], swapped[1]])
    ids = jnp.stack([(my_z + i) % Z for i in range(Z)] + [my_core])
    grad_context = context_grad(ids, ordered, tp_move(ordered, dc=1), out_proj)

    by_owner = jnp.where(my_z % 2 == 1, jnp.roll(ordered, 1, axis=0), ordered)
    by_owner = jnp.where(my_z >= 2, jnp.roll(by_owner, 2, axis=0), by_owner)
    column_own = lax.all_to_all(
        by_owner.reshape(ctx_count, tokens, features), "ctx", split_axis=0, concat_axis=0, tiled=True
    ).reshape(seq_len, features)

    key_rows, value_rows = all_kv[:, :HD], all_kv[:, HD:]
    grad_heads = grad_context.reshape(tokens, heads_here, HD)
    grad_prob = jnp.einsum("qhd,kd->hqk", grad_heads, value_rows, preferred_element_type=F32)
    row_delta = jnp.sum(grad_heads.astype(F32) * context_heads.astype(F32), axis=2)
    grad_score = (attn_prob * (grad_prob - row_delta.T[:, :, None])).astype(BF16)
    grad_query = (
        jnp.einsum("hqk,kd->qhd", grad_score, key_rows, preferred_element_type=F32) * inv_root
    ).astype(BF16)
    grad_query = grad_query.reshape(tokens, heads_here * HD)
    key_term = (
        jnp.einsum("hqk,qhd->kd", grad_score, query_heads, preferred_element_type=F32) * inv_root
    )
    value_term = jnp.einsum("hqk,qhd->kd", prob_b, grad_heads, preferred_element_type=F32)
    kept_term = jnp.where(my_core == 0, key_term, value_term)
    sent_term = jnp.where(my_core == 0, value_term, key_term).astype(BF16)
    pair_term = (kept_term + tp_move(sent_term, dc=1).astype(F32)).astype(BF16)
    pair_term, column_own = lax.optimization_barrier((pair_term, column_own))
    column_other = tp_move(column_own, dc=1)
    kv_blocks = lax.all_to_all(
        pair_term.reshape(ctx_count, tokens, HD), "ctx", split_axis=0, concat_axis=0, tiled=True
    )

    def over_tokens(left):
        return lax.dot_general(
            left, all_context, (((0,), (0,)), ((), ())), preferred_element_type=F32
        ).astype(BF16)

    kv_blocks, own_rows = lax.optimization_barrier((kv_blocks, over_tokens(column_own)))
    grad_kv = jnp.sum(kv_blocks.astype(F32), axis=0).astype(BF16)
    grad_out_proj_t = in_core_order(own_rows, over_tokens(column_other), 0)
    return (grad_hidden, grad_query, grad_kv, grad_out_proj_t)


def solution(mesh):
    in_specs = (
        P("ctx", "tp"),
        P("ctx", "tp"),
        P("ctx", None),
        P("ctx", None),
        P("ctx", None, "tp"),
        P("ctx", None, "tp"),
        P("ctx", "tp", None),
        P("ctx", "tp"),
        P("ctx", None),
        P("tp", None),
    )
    out_specs = (P("ctx", "tp"), P("ctx", "tp"), P("ctx", "tp"), P("ctx", "tp"))
    return jax.shard_map(
        per_device, mesh=mesh, in_specs=in_specs, out_specs=out_specs, check_vma=False
    )
```

```python
import math

import jax
import jax.numpy as jnp
from jax import lax
from jax.experimental import pallas as pl
from jax.experimental.pallas import tpu as pltpu
from jax.sharding import PartitionSpec as P

HQ = 48
KVH = 8
HD = 128
Z = 4
BF16 = jnp.bfloat16
F32 = jnp.float32


def tp_move(block, dz=0, dx=0, dc=0):
    route = []
    for src in range(Z * 4):
        z, low = src // 4, src % 4
        route.append((src, ((z + dz) % Z) * 4 + (low ^ (dx * 2 + dc))))
    return lax.ppermute(block, "tp", route)


def core_move(block, zero, one):
    route = []
    for src in range(Z * 4):
        z, low = src // 4, src % 4
        dz, dx = (zero, one)[src % 2]
        route.append((src, ((z + dz) % Z) * 4 + (low ^ (dx * 2))))
    return lax.ppermute(block, "tp", route)


def double_ctx(held, bit):
    route = [(c, c ^ (1 << bit)) for c in range(lax.axis_size("ctx"))]
    came = lax.ppermute(held, "ctx", route)
    upper = (lax.axis_index("ctx") >> bit) & 1 == 1
    axis = 0 if bit == 2 else 1
    return jnp.stack([jnp.where(upper, came, held), jnp.where(upper, held, came)], axis=axis)


def gather_y(held):
    held = double_ctx(double_ctx(held, 0), 1)
    return held.reshape(-1, *held.shape[4:])


def route_tables(expert_ids, route_weights, groups, capacity):
    tokens = expert_ids.shape[0]
    flat_ids = expert_ids.reshape(-1)
    numbers = jnp.arange(groups, dtype=jnp.int32)
    hits = (flat_ids[:, None] == numbers[None, :]).astype(jnp.int32)
    earlier = jnp.cumsum(hits, axis=0) - hits
    slot_rank = jnp.sum(earlier * hits, axis=1)
    targets = (flat_ids * capacity + slot_rank).reshape(tokens, 2)
    slot_index = jnp.arange(groups * capacity, dtype=jnp.int32)[:, None]
    first_hit = slot_index == targets[None, :, 0]
    second_hit = slot_index == targets[None, :, 1]
    placing = (first_hit | second_hit).astype(BF16)
    combine = jnp.where(first_hit, route_weights[None, :, 0], 0.0) + jnp.where(
        second_hit, route_weights[None, :, 1], 0.0
    )
    return (placing, combine)


def swiglu_grads(gate_act, up_act, hidden_grad):
    sigmoid_g = jax.nn.sigmoid(gate_act)
    grad_gate = (hidden_grad * up_act * sigmoid_g * (1.0 + gate_act * (1.0 - sigmoid_g))).astype(
        BF16
    )
    grad_up = (hidden_grad * gate_act * sigmoid_g).astype(BF16)
    return (grad_gate, grad_up)


def contract_last(left, right):
    return lax.dot_general(left, right, (((1,), (1,)), ((), ())), preferred_element_type=F32)


def add_bf16(*terms):
    total = terms[0].astype(F32)
    for term in terms[1:]:
        total = total + term.astype(F32)
    return total.astype(BF16)


def context_kernel(ids_ref, own_ref, other_ref, weight_ref, out_ref, total):
    step = pl.program_id(0)
    width = own_ref.shape[-1]
    first_core = ids_ref[Z] == 0

    @pl.when(step == 0)
    def _():
        total[...] = jnp.zeros_like(total)

    for x in (0, 1):
        own, other = own_ref[0, x], other_ref[0, x]
        for core, piece in (
            (0, jnp.where(first_core, own, other)),
            (1, jnp.where(first_core, other, own)),
        ):
            start = (x * 2 + core) * width
            total[...] += contract_last(piece, weight_ref[:, start : start + width])

    @pl.when(step == pl.num_programs(0) - 1)
    def _():
        out_ref[...] = total[...].astype(BF16)


def context_grad(ids, own, other, weight):
    count, _, rows, width = own.shape
    outs = weight.shape[0]
    pieces = pl.BlockSpec((1, 2, rows, width), lambda i, ids: (i, 0, 0, 0))
    return pl.pallas_call(
        context_kernel,
        grid_spec=pltpu.PrefetchScalarGridSpec(
            num_scalar_prefetch=1,
            grid=(count,),
            in_specs=[pieces, pieces, pl.BlockSpec((outs, 4 * width), lambda i, ids: (0, ids[i]))],
            out_specs=pl.BlockSpec((rows, outs), lambda i, ids: (0, 0)),
            scratch_shapes=[pltpu.VMEM((rows, outs), F32)],
        ),
        out_shape=jax.ShapeDtypeStruct((rows, outs), BF16),
        compiler_params=pltpu.CompilerParams(vmem_limit_bytes=8 * 2**20),
        cost_estimate=pl.CostEstimate(
            flops=8 * count * rows * width * outs,
            bytes_accessed=8 * count * width * (outs + rows),
            transcendentals=0,
        ),
    )(ids, own, other, weight)


def per_device(
    moe_input,
    grad_output,
    expert_ids,
    route_weights,
    w_gate,
    w_up,
    w_down,
    queries,
    keys_values,
    out_proj,
):
    ctx_count = lax.axis_size("ctx")
    tp_rank = lax.axis_index("tp")
    ctx_rank = lax.axis_index("ctx")
    my_z, my_x, my_core = tp_rank // 4, (tp_rank // 2) % 2, tp_rank % 2
    tokens, features = moe_input.shape
    capacity = tokens // 2
    slot_rows = ctx_count * capacity
    gate_w, up_w, down_w = w_gate[0], w_up[0], w_down[0]

    def chunk_of(dz, dx, dc):
        return ((my_z + dz) % Z) * 4 + (my_x ^ dx) * 2 + (my_core ^ dc)

    placing, combine = route_tables(expert_ids, route_weights, ctx_count, capacity)
    first_core = my_core == 0

    def in_core_order(own, other, axis):
        return jnp.concatenate(
            [jnp.where(first_core, own, other), jnp.where(first_core, other, own)], axis=axis
        )

    came = tp_move(jnp.where(first_core, moe_input, grad_output), dc=1)
    carried = in_core_order(jnp.where(first_core, grad_output, moe_input), came, 1)
    send = jnp.dot(placing, carried, preferred_element_type=F32).astype(BF16)
    got = lax.all_to_all(
        send.reshape(ctx_count, capacity, 2 * features), "ctx", split_axis=0, concat_axis=0, tiled=True
    ).reshape(slot_rows, 2 * features)

    heads_here = queries.shape[1] // HD
    group_size = HQ // KVH
    kv_group = tp_rank * heads_here // group_size
    mine_kv = lax.dynamic_slice_in_dim(keys_values, kv_group * 2 * HD, 2 * HD, 1)
    two_kv, got = lax.optimization_barrier((double_ctx(mine_kv, 2), got))
    seq_len = ctx_count * tokens
    query_heads = queries.reshape(tokens, heads_here, HD)
    inv_root = 1.0 / math.sqrt(HD)

    def attention_forward(all_kv):
        key_rows, value_rows = all_kv[:, :HD], all_kv[:, HD:]
        query_pos = ctx_rank * tokens + jnp.arange(tokens, dtype=jnp.int32)
        causal = query_pos[:, None] >= jnp.arange(seq_len, dtype=jnp.int32)[None, :]
        scores = (
            jnp.einsum("qhd,kd->hqk", query_heads, key_rows, preferred_element_type=F32) * inv_root
        )
        scores = jnp.where(causal[None], scores, -1e30)
        row_max = jnp.max(scores, axis=2, keepdims=True)
        exp_scores = jnp.exp(scores - row_max)
        attn_prob = exp_scores / jnp.sum(exp_scores, axis=2, keepdims=True)
        prob_b = attn_prob.astype(BF16)
        context_heads = jnp.einsum(
            "hqk,kd->qhd", prob_b, value_rows, preferred_element_type=F32
        ).astype(BF16)
        return context_heads, attn_prob, prob_b

    half, width = slot_rows // 2, 2 * features
    hop_1 = core_move(got, (1, 0), (0, 1))
    hop_2 = core_move(got, (3, 0), (1, 0))
    hop_3 = core_move(got, (0, 1), (3, 0))
    far_low = core_move(jnp.where(first_core, hop_1[:half], hop_2[:half]), (1, 0), (1, 0))
    far_high = core_move(jnp.where(first_core, hop_2[half:], hop_3[half:]), (3, 0), (3, 0))
    hop_6 = core_move(hop_1, (0, 1), (1, 0))
    hop_7 = core_move(jnp.where(first_core, hop_2, hop_1), (0, 1), (3, 0))
    far = jnp.concatenate([far_low, far_high], axis=0)
    cross_low = core_move(jnp.where(first_core, far_low, hop_6[:half]), (0, 1), (1, 0))
    cross_high = core_move(jnp.where(first_core, far_high, hop_7[half:]), (0, 1), (3, 0))
    far_cross = jnp.concatenate([cross_low, cross_high], axis=0)

    arrivals = (
        (got, (0, 0), (0, 0)),
        (hop_1, (3, 0), (0, 1)),
        (hop_2, (1, 0), (3, 0)),
        (hop_3, (0, 1), (1, 0)),
        (far, (2, 0), (2, 0)),
        (hop_6, (3, 1), (3, 1)),
        (hop_7, (1, 1), (1, 1)),
        (far_cross, (2, 1), (2, 1)),
    )
    gate_act = up_act = hidden_grad = 0.0
    for block, dy_from, x_from in arrivals:
        crossed = tp_move(block, dc=1)
        x_rows = jnp.where(first_core, crossed, block)
        dy_rows = jnp.where(first_core, block, crossed)
        x_start = (chunk_of(*x_from, 0) // 2) * width
        dy_start = (chunk_of(*dy_from, 0) // 2) * width
        gate_rows = lax.dynamic_slice_in_dim(gate_w, x_start, width, 0)
        up_rows = lax.dynamic_slice_in_dim(up_w, x_start, width, 0)
        down_cols = lax.dynamic_slice_in_dim(down_w, dy_start, width, 1)
        gate_act = gate_act + jnp.dot(x_rows, gate_rows, preferred_element_type=F32)
        up_act = up_act + jnp.dot(x_rows, up_rows, preferred_element_type=F32)
        hidden_grad = hidden_grad + contract_last(dy_rows, down_cols)
    grad_gate, grad_up = swiglu_grads(gate_act, up_act, hidden_grad)

    two_kv, grad_gate = lax.optimization_barrier((two_kv, grad_gate))
    all_kv = gather_y(two_kv)
    context_heads, attn_prob, prob_b = attention_forward(all_kv)
    context = context_heads.reshape(tokens, heads_here * HD)

    def routed(core_0, core_1):
        gate_half = jnp.where(first_core, grad_gate[core_0], grad_gate[core_1])
        up_half = jnp.where(first_core, grad_up[core_0], grad_up[core_1])
        return (contract_last(gate_w, gate_half) + contract_last(up_w, up_half)).astype(BF16)

    lower, upper = slice(None, half), slice(half, None)
    sent = routed(upper, lower)
    arrived = tp_move(sent, dc=1)
    grad_gate, sent = lax.optimization_barrier((grad_gate, sent))
    own = add_bf16(routed(lower, upper), arrived)

    def chip_rows(dz, dx):
        return lax.dynamic_slice_in_dim(own, (chunk_of(dz, dx, 0) // 2) * width, width, 0)

    near = {dz: chip_rows(dz, 0) for dz in range(Z)}
    cross = {dz: chip_rows(dz, 1) for dz in range(Z)}
    cut = features

    def stack_for(zero, one):
        return jnp.where(first_core, jnp.stack(zero), jnp.stack(one))

    def low(rows):
        return rows[:cut]

    def high(rows):
        return rows[cut:]

    def both(rows):
        return (low(rows), high(rows))

    sum_1 = core_move(stack_for(both(cross[2]), (low(near[2]), low(cross[2]))), (0, 1), (1, 0))
    sum_2 = core_move(stack_for(both(cross[1]), (high(near[2]), high(cross[2]))), (0, 1), (3, 0))
    sum_3 = core_move(stack_for(both(cross[3]), (high(near[1]), high(cross[1]))), (0, 1), (1, 0))
    sum_4 = core_move(stack_for(both(cross[0]), (low(near[3]), low(cross[3]))), (0, 1), (3, 0))
    over_2 = [add_bf16(low(near[2]), sum_1[0]), add_bf16(high(near[2]), sum_1[1])]
    over_1 = [add_bf16(low(near[1]), sum_2[0]), add_bf16(high(near[1]), sum_2[1])]
    over_3 = [add_bf16(low(near[3]), sum_3[0]), add_bf16(high(near[3]), sum_3[1])]
    down = [add_bf16(high(near[3]), sum_2[0]), add_bf16(high(cross[3]), sum_2[1])]
    up = [add_bf16(low(near[1]), sum_1[0]), add_bf16(low(cross[1]), sum_1[1])]
    sum_5 = core_move(stack_for((over_2[0], over_1[1]), down), (1, 0), (3, 0))
    sum_6 = core_move(stack_for((over_2[1], over_3[0]), up), (3, 0), (1, 0))
    z_near = [add_bf16(low(near[0]), sum_4[0], sum_6[0]), add_bf16(high(near[0]), sum_3[0], sum_5[0])]
    z_cross = [
        add_bf16(low(cross[0]), sum_4[1], sum_6[1]),
        add_bf16(high(cross[0]), sum_3[1], sum_5[1]),
    ]
    sum_7 = core_move(jnp.where(first_core, add_bf16(over_1[0], sum_5[0]), z_cross[0]), (1, 0), (0, 1))
    sum_8 = core_move(jnp.where(first_core, add_bf16(over_3[1], sum_6[0]), z_cross[1]), (3, 0), (0, 1))
    zero_low = add_bf16(low(near[0]), sum_4[0], sum_6[1], sum_7)
    zero_high = add_bf16(high(near[0]), sum_4[1], sum_5[1], sum_8)
    one_low, one_high = add_bf16(z_near[0], sum_7), add_bf16(z_near[1], sum_8)
    total = jnp.concatenate(
        [jnp.where(first_core, zero_low, one_low), jnp.where(first_core, zero_high, one_high)], axis=0
    )
    total, context = lax.optimization_barrier((total, context))
    all_context = gather_y(double_ctx(context, 2))
    left, right = total[:features], total[features:]
    came = tp_move(jnp.where(first_core, right, left), dc=1)
    own_slice = in_core_order(jnp.where(first_core, left, right), came, 1).T

    returned = lax.all_to_all(
        own_slice.reshape(ctx_count, capacity, features), "ctx", split_axis=0, concat_axis=0, tiled=True
    ).reshape(slot_rows, features)
    returned, all_context = lax.optimization_barrier((returned, all_context))
    moe_part = lax.dot_general(
        combine,
        returned.astype(F32),
        (((0,), (0,)), ((), ())),
        precision=lax.Precision.HIGHEST,
        preferred_element_type=F32,
    )
    grad_hidden = (grad_output.astype(F32) + moe_part).astype(BF16)

    one_half, other_half = grad_hidden[: tokens // 2], grad_hidden[tokens // 2 :]
    low_pair = jnp.stack([one_half, tp_move(one_half, dx=1)])
    high_z = jnp.stack([other_half] + [tp_move(other_half, dz=dz) for dz in (1, 2, 3)])
    low_all = jnp.stack([low_pair] + [tp_move(low_pair, dz=dz) for dz in (1, 2, 3)])
    high_all = jnp.stack([high_z, tp_move(high_z, dx=1)], axis=1)
    same_core = jnp.concatenate([low_all, high_all], axis=2)
    swapped = jnp.where(my_x == 0, same_core, same_core[:, ::-1])
    ordered = jnp.stack([swapped[0], swapped[3], swapped[2], swapped[1]])
    ids = jnp.stack([(my_z + i) % Z for i in range(Z)] + [my_core])
    grad_context = context_grad(ids, ordered, tp_move(ordered, dc=1), out_proj)

    by_owner = jnp.where(my_z % 2 == 1, jnp.roll(ordered, 1, axis=0), ordered)
    by_owner = jnp.where(my_z >= 2, jnp.roll(by_owner, 2, axis=0), by_owner)
    column_own = lax.all_to_all(
        by_owner.reshape(ctx_count, tokens, features), "ctx", split_axis=0, concat_axis=0, tiled=True
    ).reshape(seq_len, features)

    key_rows, value_rows = all_kv[:, :HD], all_kv[:, HD:]
    grad_heads = grad_context.reshape(tokens, heads_here, HD)
    grad_prob = jnp.einsum("qhd,kd->hqk", grad_heads, value_rows, preferred_element_type=F32)
    row_delta = jnp.sum(grad_heads.astype(F32) * context_heads.astype(F32), axis=2)
    grad_score = (attn_prob * (grad_prob - row_delta.T[:, :, None])).astype(BF16)
    grad_query = (
        jnp.einsum("hqk,kd->qhd", grad_score, key_rows, preferred_element_type=F32) * inv_root
    ).astype(BF16)
    grad_query = grad_query.reshape(tokens, heads_here * HD)
    key_term = (
        jnp.einsum("hqk,qhd->kd", grad_score, query_heads, preferred_element_type=F32) * inv_root
    )
    value_term = jnp.einsum("hqk,qhd->kd", prob_b, grad_heads, preferred_element_type=F32)
    kept_term = jnp.where(my_core == 0, key_term, value_term)
    sent_term = jnp.where(my_core == 0, value_term, key_term).astype(BF16)
    pair_term = (kept_term + tp_move(sent_term, dc=1).astype(F32)).astype(BF16)
    pair_term, column_own = lax.optimization_barrier((pair_term, column_own))
    column_other = tp_move(column_own, dc=1)
    kv_blocks = lax.all_to_all(
        pair_term.reshape(ctx_count, tokens, HD), "ctx", split_axis=0, concat_axis=0, tiled=True
    )

    def over_tokens(left):
        return lax.dot_general(
            left, all_context, (((0,), (0,)), ((), ())), preferred_element_type=F32
        ).astype(BF16)

    kv_blocks, own_rows = lax.optimization_barrier((kv_blocks, over_tokens(column_own)))
    grad_kv = jnp.sum(kv_blocks.astype(F32), axis=0).astype(BF16)
    grad_out_proj_t = in_core_order(own_rows, over_tokens(column_other), 0)
    return (grad_hidden, grad_query, grad_kv, grad_out_proj_t)


def solution(mesh):
    in_specs = (
        P("ctx", "tp"),
        P("ctx", "tp"),
        P("ctx", None),
        P("ctx", None),
        P("ctx", None, "tp"),
        P("ctx", None, "tp"),
        P("ctx", "tp", None),
        P("ctx", "tp"),
        P("ctx", None),
        P("tp", None),
    )
    out_specs = (P("ctx", "tp"), P("ctx", "tp"), P("ctx", "tp"), P("ctx", "tp"))
    return jax.shard_map(
        per_device, mesh=mesh, in_specs=in_specs, out_specs=out_specs, check_vma=False
    )
```

```python
import math

import jax
import jax.numpy as jnp
from jax import lax
from jax.experimental import pallas as pl
from jax.experimental.pallas import tpu as pltpu
from jax.sharding import PartitionSpec as P

HQ = 48
KVH = 8
HD = 128
Z = 4
BF16 = jnp.bfloat16
F32 = jnp.float32


def tp_move(block, dz=0, dx=0, dc=0):
    route = []
    for src in range(Z * 4):
        z, low = src // 4, src % 4
        route.append((src, ((z + dz) % Z) * 4 + (low ^ (dx * 2 + dc))))
    return lax.ppermute(block, "tp", route)


def core_move(block, zero, one):
    route = []
    for src in range(Z * 4):
        z, low = src // 4, src % 4
        dz, dx = (zero, one)[src % 2]
        route.append((src, ((z + dz) % Z) * 4 + (low ^ (dx * 2))))
    return lax.ppermute(block, "tp", route)


def x_pair(block):
    rank, count = lax.axis_index("ctx"), lax.axis_size("ctx")
    came = lax.ppermute(block, "ctx", [(c, c ^ 4) for c in range(count)])
    return jnp.stack([jnp.where(rank >= 4, came, block), jnp.where(rank >= 4, block, came)])


def y_moves(block):
    return [block] + [
        lax.ppermute(block, "ctx", [(c, c // 4 * 4 + (c + dy) % 4) for c in range(lax.axis_size("ctx"))])
        for dy in (3, 2, 1)
    ]


def rolled(blocks, shift, axis):
    blocks = jnp.where(shift % 2 == 1, jnp.roll(blocks, 1, axis=axis), blocks)
    return jnp.where(shift >= 2, jnp.roll(blocks, 2, axis=axis), blocks)


def in_ctx_order(moved):
    blocks = rolled(jnp.stack(moved, axis=1), lax.axis_index("ctx") % 4, 1)
    return blocks.reshape(-1, *blocks.shape[3:])


def route_tables(expert_ids, route_weights, groups, capacity):
    tokens = expert_ids.shape[0]
    flat_ids = expert_ids.reshape(-1)
    numbers = jnp.arange(groups, dtype=jnp.int32)
    hits = (flat_ids[:, None] == numbers[None, :]).astype(jnp.int32)
    earlier = jnp.cumsum(hits, axis=0) - hits
    slot_rank = jnp.sum(earlier * hits, axis=1)
    targets = (flat_ids * capacity + slot_rank).reshape(tokens, 2)
    slot_index = jnp.arange(groups * capacity, dtype=jnp.int32)[:, None]
    first_hit = slot_index == targets[None, :, 0]
    second_hit = slot_index == targets[None, :, 1]
    placing = (first_hit | second_hit).astype(BF16)
    combine = jnp.where(first_hit, route_weights[None, :, 0], 0.0) + jnp.where(
        second_hit, route_weights[None, :, 1], 0.0
    )
    return (placing, combine)


def swiglu_grads(gate_act, up_act, hidden_grad):
    sigmoid_g = jax.nn.sigmoid(gate_act)
    grad_gate = (hidden_grad * up_act * sigmoid_g * (1.0 + gate_act * (1.0 - sigmoid_g))).astype(
        BF16
    )
    grad_up = (hidden_grad * gate_act * sigmoid_g).astype(BF16)
    return (grad_gate, grad_up)


def contract_last(left, right):
    return lax.dot_general(left, right, (((1,), (1,)), ((), ())), preferred_element_type=F32)


def add_bf16(*terms):
    total = terms[0].astype(F32)
    for term in terms[1:]:
        total = total + term.astype(F32)
    return total.astype(BF16)


def context_kernel(ids_ref, pieces_ref, first_ref, second_ref, before_ref, out_ref, total):
    step = pl.program_id(0)

    @pl.when(step == 0)
    def _():
        total[...] = before_ref[...]

    total[...] += contract_last(pieces_ref[0, 0], first_ref[...]) + contract_last(
        pieces_ref[0, 1], second_ref[...]
    )

    @pl.when(step == pl.num_programs(0) - 1)
    def _():
        out_ref[...] = total[...].astype(out_ref.dtype)


def context_grad(ids, pieces, weight, before, dtype):
    count, _, rows, width = pieces.shape
    outs = weight.shape[0]
    whole = pl.BlockSpec((rows, outs), lambda i, ids: (0, 0))
    return pl.pallas_call(
        context_kernel,
        grid_spec=pltpu.PrefetchScalarGridSpec(
            num_scalar_prefetch=1,
            grid=(count,),
            in_specs=[
                pl.BlockSpec((1, 2, rows, width), lambda i, ids: (i, 0, 0, 0)),
                pl.BlockSpec((outs, width), lambda i, ids: (0, ids[i])),
                pl.BlockSpec((outs, width), lambda i, ids: (0, ids[i + count])),
                whole,
            ],
            out_specs=whole,
            scratch_shapes=[pltpu.VMEM((rows, outs), F32)],
        ),
        out_shape=jax.ShapeDtypeStruct((rows, outs), dtype),
        compiler_params=pltpu.CompilerParams(vmem_limit_bytes=8 * 2**20),
        cost_estimate=pl.CostEstimate(
            flops=4 * count * rows * width * outs,
            bytes_accessed=4 * count * width * (outs + rows),
            transcendentals=0,
        ),
    )(ids, pieces, weight, weight, before)


def per_device(
    moe_input,
    grad_output,
    expert_ids,
    route_weights,
    w_gate,
    w_up,
    w_down,
    queries,
    keys_values,
    out_proj,
):
    ctx_count = lax.axis_size("ctx")
    tp_rank = lax.axis_index("tp")
    ctx_rank = lax.axis_index("ctx")
    my_z, my_x, my_core = tp_rank // 4, (tp_rank // 2) % 2, tp_rank % 2
    tokens, features = moe_input.shape
    capacity = tokens // 2
    slot_rows = ctx_count * capacity
    gate_w, up_w, down_w = w_gate[0], w_up[0], w_down[0]

    def chunk_of(dz, dx, dc):
        return ((my_z + dz) % Z) * 4 + (my_x ^ dx) * 2 + (my_core ^ dc)

    placing, combine = route_tables(expert_ids, route_weights, ctx_count, capacity)
    first_core = my_core == 0

    def in_core_order(own, other, axis):
        return jnp.concatenate(
            [jnp.where(first_core, own, other), jnp.where(first_core, other, own)], axis=axis
        )

    came = tp_move(jnp.where(first_core, moe_input, grad_output), dc=1)
    carried = in_core_order(jnp.where(first_core, grad_output, moe_input), came, 1)
    send = jnp.dot(placing, carried, preferred_element_type=F32).astype(BF16)
    got = lax.all_to_all(
        send.reshape(ctx_count, capacity, 2 * features), "ctx", split_axis=0, concat_axis=0, tiled=True
    ).reshape(slot_rows, 2 * features)

    heads_here = queries.shape[1] // HD
    group_size = HQ // KVH
    kv_group = tp_rank * heads_here // group_size
    mine_kv = lax.dynamic_slice_in_dim(keys_values, kv_group * 2 * HD, 2 * HD, 1)
    moved_kv, got = lax.optimization_barrier((y_moves(x_pair(mine_kv)), got))
    all_kv = in_ctx_order(moved_kv)
    seq_len = ctx_count * tokens
    query_heads = queries.reshape(tokens, heads_here, HD)
    inv_root = 1.0 / math.sqrt(HD)

    def attention_forward(all_kv):
        key_rows, value_rows = all_kv[:, :HD], all_kv[:, HD:]
        query_pos = ctx_rank * tokens + jnp.arange(tokens, dtype=jnp.int32)
        causal = query_pos[:, None] >= jnp.arange(seq_len, dtype=jnp.int32)[None, :]
        scores = (
            jnp.einsum("qhd,kd->hqk", query_heads, key_rows, preferred_element_type=F32) * inv_root
        )
        scores = jnp.where(causal[None], scores, -1e30)
        row_max = jnp.max(scores, axis=2, keepdims=True)
        exp_scores = jnp.exp(scores - row_max)
        attn_prob = exp_scores / jnp.sum(exp_scores, axis=2, keepdims=True)
        prob_b = attn_prob.astype(BF16)
        context_heads = jnp.einsum(
            "hqk,kd->qhd", prob_b, value_rows, preferred_element_type=F32
        ).astype(BF16)
        return context_heads, attn_prob, prob_b

    half, width = slot_rows // 2, 2 * features
    hop_1 = core_move(got, (1, 0), (0, 1))
    hop_2 = core_move(got, (3, 0), (1, 0))
    hop_3 = core_move(got, (0, 1), (3, 0))
    context_heads, attn_prob, prob_b = attention_forward(all_kv)
    context = context_heads.reshape(tokens, heads_here * HD)
    hop_3, context = lax.optimization_barrier((hop_3, context))
    far_low = core_move(jnp.where(first_core, hop_1[:half], hop_2[:half]), (1, 0), (1, 0))
    far_high = core_move(jnp.where(first_core, hop_2[half:], hop_3[half:]), (3, 0), (3, 0))
    hop_6 = core_move(hop_1, (0, 1), (1, 0))
    hop_7 = core_move(jnp.where(first_core, hop_2, hop_1), (0, 1), (3, 0))
    far = jnp.concatenate([far_low, far_high], axis=0)
    cross_low = core_move(jnp.where(first_core, far_low, hop_6[:half]), (0, 1), (1, 0))
    cross_high = core_move(jnp.where(first_core, far_high, hop_7[half:]), (0, 1), (3, 0))
    far_cross = jnp.concatenate([cross_low, cross_high], axis=0)

    arrivals = (
        (got, (0, 0), (0, 0)),
        (hop_1, (3, 0), (0, 1)),
        (hop_2, (1, 0), (3, 0)),
        (hop_3, (0, 1), (1, 0)),
        (far, (2, 0), (2, 0)),
        (hop_6, (3, 1), (3, 1)),
        (hop_7, (1, 1), (1, 1)),
        (far_cross, (2, 1), (2, 1)),
    )
    gate_act = up_act = hidden_grad = 0.0
    for block, dy_from, x_from in arrivals:
        crossed = tp_move(block, dc=1)
        x_rows = jnp.where(first_core, crossed, block)
        dy_rows = jnp.where(first_core, block, crossed)
        x_start = (chunk_of(*x_from, 0) // 2) * width
        dy_start = (chunk_of(*dy_from, 0) // 2) * width
        gate_rows = lax.dynamic_slice_in_dim(gate_w, x_start, width, 0)
        up_rows = lax.dynamic_slice_in_dim(up_w, x_start, width, 0)
        down_cols = lax.dynamic_slice_in_dim(down_w, dy_start, width, 1)
        gate_act = gate_act + jnp.dot(x_rows, gate_rows, preferred_element_type=F32)
        up_act = up_act + jnp.dot(x_rows, up_rows, preferred_element_type=F32)
        hidden_grad = hidden_grad + contract_last(dy_rows, down_cols)
    grad_gate, grad_up = swiglu_grads(gate_act, up_act, hidden_grad)

    def routed(core_0, core_1):
        gate_half = jnp.where(first_core, grad_gate[core_0], grad_gate[core_1])
        up_half = jnp.where(first_core, grad_up[core_0], grad_up[core_1])
        return (contract_last(gate_w, gate_half) + contract_last(up_w, up_half)).astype(BF16)

    lower, upper = slice(None, half), slice(half, None)
    sent = routed(upper, lower)
    arrived, moved_context = lax.optimization_barrier((tp_move(sent, dc=1), y_moves(x_pair(context))))
    all_context = in_ctx_order(moved_context)
    grad_gate, sent = lax.optimization_barrier((grad_gate, sent))
    own = add_bf16(routed(lower, upper), arrived)

    def chip_rows(dz, dx):
        return lax.dynamic_slice_in_dim(own, (chunk_of(dz, dx, 0) // 2) * width, width, 0)

    near = {dz: chip_rows(dz, 0) for dz in range(Z)}
    cross = {dz: chip_rows(dz, 1) for dz in range(Z)}
    cut = features

    def stack_for(zero, one):
        return jnp.where(first_core, jnp.stack(zero), jnp.stack(one))

    def low(rows):
        return rows[:cut]

    def high(rows):
        return rows[cut:]

    def both(rows):
        return (low(rows), high(rows))

    sum_1 = core_move(stack_for(both(cross[2]), (low(near[2]), low(cross[2]))), (0, 1), (1, 0))
    sum_2 = core_move(stack_for(both(cross[1]), (high(near[2]), high(cross[2]))), (0, 1), (3, 0))
    sum_3 = core_move(stack_for(both(cross[3]), (high(near[1]), high(cross[1]))), (0, 1), (1, 0))
    sum_4 = core_move(stack_for(both(cross[0]), (low(near[3]), low(cross[3]))), (0, 1), (3, 0))
    over_2 = [add_bf16(low(near[2]), sum_1[0]), add_bf16(high(near[2]), sum_1[1])]
    over_1 = [add_bf16(low(near[1]), sum_2[0]), add_bf16(high(near[1]), sum_2[1])]
    over_3 = [add_bf16(low(near[3]), sum_3[0]), add_bf16(high(near[3]), sum_3[1])]
    down = [add_bf16(high(near[3]), sum_2[0]), add_bf16(high(cross[3]), sum_2[1])]
    up = [add_bf16(low(near[1]), sum_1[0]), add_bf16(low(cross[1]), sum_1[1])]
    sum_5 = core_move(stack_for((over_2[0], over_1[1]), down), (1, 0), (3, 0))
    sum_6 = core_move(stack_for((over_2[1], over_3[0]), up), (3, 0), (1, 0))
    z_near = [add_bf16(low(near[0]), sum_4[0], sum_6[0]), add_bf16(high(near[0]), sum_3[0], sum_5[0])]
    z_cross = [
        add_bf16(low(cross[0]), sum_4[1], sum_6[1]),
        add_bf16(high(cross[0]), sum_3[1], sum_5[1]),
    ]
    sum_7 = core_move(jnp.where(first_core, add_bf16(over_1[0], sum_5[0]), z_cross[0]), (1, 0), (0, 1))
    sum_8 = core_move(jnp.where(first_core, add_bf16(over_3[1], sum_6[0]), z_cross[1]), (3, 0), (0, 1))
    zero_low = add_bf16(low(near[0]), sum_4[0], sum_6[1], sum_7)
    zero_high = add_bf16(high(near[0]), sum_4[1], sum_5[1], sum_8)
    one_low, one_high = add_bf16(z_near[0], sum_7), add_bf16(z_near[1], sum_8)
    total = jnp.concatenate(
        [jnp.where(first_core, zero_low, one_low), jnp.where(first_core, zero_high, one_high)], axis=0
    )
    left, right = total[:features], total[features:]
    came = tp_move(jnp.where(first_core, right, left), dc=1)
    own_slice = in_core_order(jnp.where(first_core, left, right), came, 1).T

    returned = lax.all_to_all(
        own_slice.reshape(ctx_count, capacity, features), "ctx", split_axis=0, concat_axis=0, tiled=True
    ).reshape(slot_rows, features)
    moe_part = lax.dot_general(
        combine,
        returned.astype(F32),
        (((0,), (0,)), ((), ())),
        precision=lax.Precision.HIGHEST,
        preferred_element_type=F32,
    )
    grad_hidden = (grad_output.astype(F32) + moe_part).astype(BF16)

    one_half, other_half = grad_hidden[: tokens // 2], grad_hidden[tokens // 2 :]
    low_pair = jnp.stack([one_half, tp_move(one_half, dx=1)])
    high_z = jnp.stack([other_half] + [tp_move(other_half, dz=dz) for dz in (1, 2, 3)])
    low_all = jnp.stack([low_pair] + [tp_move(low_pair, dz=dz) for dz in (1, 2, 3)])
    high_all = jnp.stack([high_z, tp_move(high_z, dx=1)], axis=1)
    same_core = jnp.concatenate([low_all, high_all], axis=2)
    swapped = jnp.where(my_x == 0, same_core, same_core[:, ::-1])
    ordered = jnp.stack([swapped[0], swapped[3], swapped[2], swapped[1]])
    ids = jnp.stack([(my_z + i) % Z * 4 + x * 2 for x in (0, 1) for i in range(Z)])
    grad_context = context_grad(
        ids + my_core, ordered, out_proj, jnp.zeros((tokens, features), F32), F32
    )
    grad_context = context_grad(
        ids + 1 - my_core, tp_move(ordered, dc=1), out_proj, grad_context, BF16
    )

    by_owner = rolled(ordered, my_z, 0)
    column_own = lax.all_to_all(
        by_owner.reshape(ctx_count, tokens, features), "ctx", split_axis=0, concat_axis=0, tiled=True
    ).reshape(seq_len, features)

    key_rows, value_rows = all_kv[:, :HD], all_kv[:, HD:]
    grad_heads = grad_context.reshape(tokens, heads_here, HD)
    grad_prob = jnp.einsum("qhd,kd->hqk", grad_heads, value_rows, preferred_element_type=F32)
    row_delta = jnp.sum(grad_heads.astype(F32) * context_heads.astype(F32), axis=2)
    grad_score = (attn_prob * (grad_prob - row_delta.T[:, :, None])).astype(BF16)
    grad_query = (
        jnp.einsum("hqk,kd->qhd", grad_score, key_rows, preferred_element_type=F32) * inv_root
    ).astype(BF16)
    grad_query = grad_query.reshape(tokens, heads_here * HD)
    key_term = (
        jnp.einsum("hqk,qhd->kd", grad_score, query_heads, preferred_element_type=F32) * inv_root
    )
    value_term = jnp.einsum("hqk,qhd->kd", prob_b, grad_heads, preferred_element_type=F32)
    kept_term = jnp.where(my_core == 0, key_term, value_term)
    sent_term = jnp.where(my_core == 0, value_term, key_term).astype(BF16)
    pair_term = (kept_term + tp_move(sent_term, dc=1).astype(F32)).astype(BF16)
    pair_term, column_own = lax.optimization_barrier((pair_term, column_own))
    column_other = tp_move(column_own, dc=1)
    kv_blocks = lax.all_to_all(
        pair_term.reshape(ctx_count, tokens, HD), "ctx", split_axis=0, concat_axis=0, tiled=True
    )

    def over_tokens(left):
        return lax.dot_general(
            left, all_context, (((0,), (0,)), ((), ())), preferred_element_type=F32
        ).astype(BF16)

    kv_blocks, own_rows = lax.optimization_barrier((kv_blocks, over_tokens(column_own)))
    grad_kv = jnp.sum(kv_blocks.astype(F32), axis=0).astype(BF16)
    grad_out_proj_t = in_core_order(own_rows, over_tokens(column_other), 0)
    return (grad_hidden, grad_query, grad_kv, grad_out_proj_t)


def solution(mesh):
    in_specs = (
        P("ctx", "tp"),
        P("ctx", "tp"),
        P("ctx", None),
        P("ctx", None),
        P("ctx", None, "tp"),
        P("ctx", None, "tp"),
        P("ctx", "tp", None),
        P("ctx", "tp"),
        P("ctx", None),
        P("tp", None),
    )
    out_specs = (P("ctx", "tp"), P("ctx", "tp"), P("ctx", "tp"), P("ctx", "tp"))
    return jax.shard_map(
        per_device, mesh=mesh, in_specs=in_specs, out_specs=out_specs, check_vma=False
    )
```

```python
import math

import jax
import jax.numpy as jnp
from jax import lax
from jax.experimental import pallas as pl
from jax.experimental.pallas import tpu as pltpu
from jax.sharding import PartitionSpec as P

HQ = 48
KVH = 8
HD = 128
Z = 4
BF16 = jnp.bfloat16
F32 = jnp.float32


def tp_move(block, dz=0, dx=0, dc=0):
    route = []
    for src in range(Z * 4):
        z, low = src // 4, src % 4
        route.append((src, ((z + dz) % Z) * 4 + (low ^ (dx * 2 + dc))))
    return lax.ppermute(block, "tp", route)


def core_move(block, zero, one):
    route = []
    for src in range(Z * 4):
        z, low = src // 4, src % 4
        dz, dx = (zero, one)[src % 2]
        route.append((src, ((z + dz) % Z) * 4 + (low ^ (dx * 2))))
    return lax.ppermute(block, "tp", route)


def double_ctx(held, bit):
    route = [(c, c ^ (1 << bit)) for c in range(lax.axis_size("ctx"))]
    came = lax.ppermute(held, "ctx", route)
    upper = (lax.axis_index("ctx") >> bit) & 1 == 1
    axis = 0 if bit == 2 else 1
    return jnp.stack([jnp.where(upper, came, held), jnp.where(upper, held, came)], axis=axis)


def rolled(blocks, shift, axis):
    blocks = jnp.where(shift % 2 == 1, jnp.roll(blocks, 1, axis=axis), blocks)
    return jnp.where(shift >= 2, jnp.roll(blocks, 2, axis=axis), blocks)


def route_tables(expert_ids, route_weights, groups, capacity):
    tokens = expert_ids.shape[0]
    flat_ids = expert_ids.reshape(-1)
    numbers = jnp.arange(groups, dtype=jnp.int32)
    hits = (flat_ids[:, None] == numbers[None, :]).astype(jnp.int32)
    earlier = jnp.cumsum(hits, axis=0) - hits
    slot_rank = jnp.sum(earlier * hits, axis=1)
    targets = (flat_ids * capacity + slot_rank).reshape(tokens, 2)
    slot_index = jnp.arange(groups * capacity, dtype=jnp.int32)[:, None]
    first_hit = slot_index == targets[None, :, 0]
    second_hit = slot_index == targets[None, :, 1]
    placing = (first_hit | second_hit).astype(BF16)
    combine = jnp.where(first_hit, route_weights[None, :, 0], 0.0) + jnp.where(
        second_hit, route_weights[None, :, 1], 0.0
    )
    return (placing, combine)


def swiglu_grads(gate_act, up_act, hidden_grad):
    sigmoid_g = jax.nn.sigmoid(gate_act)
    grad_gate = (hidden_grad * up_act * sigmoid_g * (1.0 + gate_act * (1.0 - sigmoid_g))).astype(
        BF16
    )
    grad_up = (hidden_grad * gate_act * sigmoid_g).astype(BF16)
    return (grad_gate, grad_up)


def contract_last(left, right):
    return lax.dot_general(left, right, (((1,), (1,)), ((), ())), preferred_element_type=F32)


def add_bf16(*terms):
    total = terms[0].astype(F32)
    for term in terms[1:]:
        total = total + term.astype(F32)
    return total.astype(BF16)


def context_kernel(ids_ref, pieces_ref, first_ref, second_ref, before_ref, out_ref, total):
    step = pl.program_id(0)

    @pl.when(step == 0)
    def _():
        total[...] = before_ref[...]

    total[...] += contract_last(pieces_ref[0, 0], first_ref[...]) + contract_last(
        pieces_ref[0, 1], second_ref[...]
    )

    @pl.when(step == pl.num_programs(0) - 1)
    def _():
        out_ref[...] = total[...].astype(out_ref.dtype)


def context_grad(ids, pieces, weight, before, dtype):
    count, _, rows, width = pieces.shape
    outs = weight.shape[0]
    whole = pl.BlockSpec((rows, outs), lambda i, ids: (0, 0))
    return pl.pallas_call(
        context_kernel,
        grid_spec=pltpu.PrefetchScalarGridSpec(
            num_scalar_prefetch=1,
            grid=(count,),
            in_specs=[
                pl.BlockSpec((1, 2, rows, width), lambda i, ids: (i, 0, 0, 0)),
                pl.BlockSpec((outs, width), lambda i, ids: (0, ids[i])),
                pl.BlockSpec((outs, width), lambda i, ids: (0, ids[i + count])),
                whole,
            ],
            out_specs=whole,
            scratch_shapes=[pltpu.VMEM((rows, outs), F32)],
        ),
        out_shape=jax.ShapeDtypeStruct((rows, outs), dtype),
        compiler_params=pltpu.CompilerParams(vmem_limit_bytes=8 * 2**20),
        cost_estimate=pl.CostEstimate(
            flops=4 * count * rows * width * outs,
            bytes_accessed=4 * count * width * (outs + rows),
            transcendentals=0,
        ),
    )(ids, pieces, weight, weight, before)


def per_device(
    moe_input,
    grad_output,
    expert_ids,
    route_weights,
    w_gate,
    w_up,
    w_down,
    queries,
    keys_values,
    out_proj,
):
    ctx_count = lax.axis_size("ctx")
    tp_rank = lax.axis_index("tp")
    ctx_rank = lax.axis_index("ctx")
    my_z, my_x, my_core = tp_rank // 4, (tp_rank // 2) % 2, tp_rank % 2
    tokens, features = moe_input.shape
    capacity = tokens // 2
    slot_rows = ctx_count * capacity
    gate_w, up_w, down_w = w_gate[0], w_up[0], w_down[0]

    def chunk_of(dz, dx, dc):
        return ((my_z + dz) % Z) * 4 + (my_x ^ dx) * 2 + (my_core ^ dc)

    placing, combine = route_tables(expert_ids, route_weights, ctx_count, capacity)
    first_core = my_core == 0

    def in_core_order(own, other, axis):
        return jnp.concatenate(
            [jnp.where(first_core, own, other), jnp.where(first_core, other, own)], axis=axis
        )

    came = tp_move(jnp.where(first_core, moe_input, grad_output), dc=1)
    carried = in_core_order(jnp.where(first_core, grad_output, moe_input), came, 1)
    send = jnp.dot(placing, carried, preferred_element_type=F32).astype(BF16)
    got = lax.all_to_all(
        send.reshape(ctx_count, capacity, 2 * features), "ctx", split_axis=0, concat_axis=0, tiled=True
    ).reshape(slot_rows, 2 * features)

    heads_here = queries.shape[1] // HD
    group_size = HQ // KVH
    kv_group = tp_rank * heads_here // group_size
    mine_kv = lax.dynamic_slice_in_dim(keys_values, kv_group * 2 * HD, 2 * HD, 1)
    part_kv, got = lax.optimization_barrier((double_ctx(double_ctx(mine_kv, 2), 0), got))
    all_kv = double_ctx(part_kv, 1).reshape(-1, 2 * HD)
    seq_len = ctx_count * tokens
    query_heads = queries.reshape(tokens, heads_here, HD)
    inv_root = 1.0 / math.sqrt(HD)

    def attention_forward(all_kv):
        key_rows, value_rows = all_kv[:, :HD], all_kv[:, HD:]
        query_pos = ctx_rank * tokens + jnp.arange(tokens, dtype=jnp.int32)
        causal = query_pos[:, None] >= jnp.arange(seq_len, dtype=jnp.int32)[None, :]
        scores = (
            jnp.einsum("qhd,kd->hqk", query_heads, key_rows, preferred_element_type=F32) * inv_root
        )
        scores = jnp.where(causal[None], scores, -1e30)
        row_max = jnp.max(scores, axis=2, keepdims=True)
        exp_scores = jnp.exp(scores - row_max)
        attn_prob = exp_scores / jnp.sum(exp_scores, axis=2, keepdims=True)
        prob_b = attn_prob.astype(BF16)
        context_heads = jnp.einsum(
            "hqk,kd->qhd", prob_b, value_rows, preferred_element_type=F32
        ).astype(BF16)
        return context_heads, attn_prob, prob_b

    half, width = slot_rows // 2, 2 * features
    hop_1 = core_move(got, (1, 0), (0, 1))
    hop_2 = core_move(got, (3, 0), (1, 0))
    hop_3 = core_move(got, (0, 1), (3, 0))
    hop_3, all_kv = lax.optimization_barrier((hop_3, all_kv))
    context_heads, attn_prob, prob_b = attention_forward(all_kv)
    context = context_heads.reshape(tokens, heads_here * HD)
    far_low = core_move(jnp.where(first_core, hop_1[:half], hop_2[:half]), (1, 0), (1, 0))
    far_high = core_move(jnp.where(first_core, hop_2[half:], hop_3[half:]), (3, 0), (3, 0))
    hop_6 = core_move(hop_1, (0, 1), (1, 0))
    hop_7 = core_move(jnp.where(first_core, hop_2, hop_1), (0, 1), (3, 0))
    hop_6, context = lax.optimization_barrier((hop_6, context))
    far = jnp.concatenate([far_low, far_high], axis=0)
    cross_low = core_move(jnp.where(first_core, far_low, hop_6[:half]), (0, 1), (1, 0))
    cross_high = core_move(jnp.where(first_core, far_high, hop_7[half:]), (0, 1), (3, 0))
    far_cross = jnp.concatenate([cross_low, cross_high], axis=0)

    arrivals = (
        (got, (0, 0), (0, 0)),
        (hop_1, (3, 0), (0, 1)),
        (hop_2, (1, 0), (3, 0)),
        (hop_3, (0, 1), (1, 0)),
        (far, (2, 0), (2, 0)),
        (hop_6, (3, 1), (3, 1)),
        (hop_7, (1, 1), (1, 1)),
        (far_cross, (2, 1), (2, 1)),
    )
    gate_act = up_act = hidden_grad = 0.0
    for block, dy_from, x_from in arrivals:
        crossed = tp_move(block, dc=1)
        x_rows = jnp.where(first_core, crossed, block)
        dy_rows = jnp.where(first_core, block, crossed)
        x_start = (chunk_of(*x_from, 0) // 2) * width
        dy_start = (chunk_of(*dy_from, 0) // 2) * width
        gate_rows = lax.dynamic_slice_in_dim(gate_w, x_start, width, 0)
        up_rows = lax.dynamic_slice_in_dim(up_w, x_start, width, 0)
        down_cols = lax.dynamic_slice_in_dim(down_w, dy_start, width, 1)
        gate_act = gate_act + jnp.dot(x_rows, gate_rows, preferred_element_type=F32)
        up_act = up_act + jnp.dot(x_rows, up_rows, preferred_element_type=F32)
        hidden_grad = hidden_grad + contract_last(dy_rows, down_cols)
    grad_gate, grad_up = swiglu_grads(gate_act, up_act, hidden_grad)

    def routed(core_0, core_1):
        gate_half = jnp.where(first_core, grad_gate[core_0], grad_gate[core_1])
        up_half = jnp.where(first_core, grad_up[core_0], grad_up[core_1])
        return (contract_last(gate_w, gate_half) + contract_last(up_w, up_half)).astype(BF16)

    lower, upper = slice(None, half), slice(half, None)
    sent = routed(upper, lower)
    arrived = tp_move(sent, dc=1)
    grad_gate, sent = lax.optimization_barrier((grad_gate, sent))
    kept = routed(lower, upper)

    cut = features

    def stack_for(zero, one):
        return jnp.where(first_core, jnp.stack(zero), jnp.stack(one))

    def low(rows):
        return rows[:cut]

    def high(rows):
        return rows[cut:]

    def both(rows):
        return (low(rows), high(rows))

    near, cross, loads = {}, {}, []
    for dz in (2, 1, 3, 0):

        def chip_rows(dx):
            start = (chunk_of(dz, dx, 0) // 2) * width
            return add_bf16(
                lax.dynamic_slice_in_dim(kept, start, width, 0),
                lax.dynamic_slice_in_dim(arrived, start, width, 0),
            )

        near[dz], cross[dz], kept = lax.optimization_barrier((chip_rows(0), chip_rows(1), kept))
        if dz == 2:
            load = stack_for(both(cross[2]), (low(near[2]), low(cross[2])))
        elif dz == 1:
            continue
        elif dz == 3:
            load = stack_for((high(cross[1]), low(cross[3])), (high(near[2]), high(cross[2])))
        else:
            load = stack_for(both(cross[0]), (low(near[3]), low(cross[3])))
        load, kept = lax.optimization_barrier((load, kept))
        loads.append(load)
        if dz == 3:
            load = stack_for((low(cross[1]), high(cross[3])), (high(near[1]), high(cross[1])))
            load, kept = lax.optimization_barrier((load, kept))
            loads.append(load)
    sum_1 = core_move(loads[0], (0, 1), (1, 0))
    sum_1, context = lax.optimization_barrier((sum_1, context))
    part_context = double_ctx(context, 2)
    sum_2 = core_move(loads[1], (0, 1), (3, 0))
    sum_3 = core_move(loads[2], (0, 1), (1, 0))
    sum_4 = core_move(loads[3], (0, 1), (3, 0))
    over_2 = [add_bf16(low(near[2]), sum_1[0]), add_bf16(high(near[2]), sum_1[1])]
    over_1 = [None, add_bf16(high(near[1]), sum_2[0])]
    over_3 = [add_bf16(low(near[3]), sum_2[1]), None]
    down = [add_bf16(high(near[3]), sum_2[0]), add_bf16(high(cross[3]), sum_2[1])]
    up = [add_bf16(low(near[1]), sum_1[0]), add_bf16(low(cross[1]), sum_1[1])]
    load_5 = stack_for((over_2[0], over_1[1]), down)
    load_6 = stack_for((over_2[1], over_3[0]), up)
    sum_3, sum_4, _, _ = lax.optimization_barrier((sum_3, sum_4, load_5, load_6))
    sum_5 = core_move(load_5, (1, 0), (3, 0))
    sum_5, part_context = lax.optimization_barrier((sum_5, part_context))
    sum_6 = core_move(load_6, (3, 0), (1, 0))
    over_1[0] = add_bf16(low(near[1]), sum_3[0])
    over_3[1] = add_bf16(high(near[3]), sum_3[1])
    z_near = [add_bf16(low(near[0]), sum_4[0], sum_6[0]), add_bf16(high(near[0]), sum_3[0], sum_5[0])]
    z_cross = [
        add_bf16(low(cross[0]), sum_4[1], sum_6[1]),
        add_bf16(high(cross[0]), sum_3[1], sum_5[1]),
    ]
    sum_7 = core_move(jnp.where(first_core, add_bf16(over_1[0], sum_5[0]), z_cross[0]), (1, 0), (0, 1))
    sum_8 = core_move(jnp.where(first_core, add_bf16(over_3[1], sum_6[0]), z_cross[1]), (3, 0), (0, 1))
    zero_low = add_bf16(low(near[0]), sum_4[0], sum_6[1], sum_7)
    zero_high = add_bf16(high(near[0]), sum_4[1], sum_5[1], sum_8)
    one_low, one_high = add_bf16(z_near[0], sum_7), add_bf16(z_near[1], sum_8)
    total = jnp.concatenate(
        [jnp.where(first_core, zero_low, one_low), jnp.where(first_core, zero_high, one_high)], axis=0
    )
    left, right = total[:features], total[features:]
    came = tp_move(jnp.where(first_core, right, left), dc=1)
    own_slice = in_core_order(jnp.where(first_core, left, right), came, 1).T

    returned = lax.all_to_all(
        own_slice.reshape(ctx_count, capacity, features), "ctx", split_axis=0, concat_axis=0, tiled=True
    ).reshape(slot_rows, features)
    part_context = double_ctx(double_ctx(part_context, 0), 1)
    returned, part_context = lax.optimization_barrier((returned, part_context))
    all_context = part_context.reshape(-1, heads_here * HD)
    moe_part = lax.dot_general(
        combine,
        returned.astype(F32),
        (((0,), (0,)), ((), ())),
        precision=lax.Precision.HIGHEST,
        preferred_element_type=F32,
    )
    grad_hidden = (grad_output.astype(F32) + moe_part).astype(BF16)

    one_half, other_half = grad_hidden[: tokens // 2], grad_hidden[tokens // 2 :]
    low_pair = jnp.stack([one_half, tp_move(one_half, dx=1)])
    high_z = jnp.stack([other_half] + [tp_move(other_half, dz=dz) for dz in (1, 2, 3)])
    low_all = jnp.stack([low_pair] + [tp_move(low_pair, dz=dz) for dz in (1, 2, 3)])
    high_all = jnp.stack([high_z, tp_move(high_z, dx=1)], axis=1)
    same_core = jnp.concatenate([low_all, high_all], axis=2)
    swapped = jnp.where(my_x == 0, same_core, same_core[:, ::-1])
    ordered = jnp.stack([swapped[0], swapped[3], swapped[2], swapped[1]])
    ids = jnp.stack([(my_z + i) % Z * 4 + x * 2 for x in (0, 1) for i in range(Z)])
    grad_context = context_grad(
        ids + my_core, ordered, out_proj, jnp.zeros((tokens, features), F32), F32
    )
    grad_context = context_grad(
        ids + 1 - my_core, tp_move(ordered, dc=1), out_proj, grad_context, BF16
    )

    by_owner = rolled(ordered, my_z, 0)
    column_own = lax.all_to_all(
        by_owner.reshape(ctx_count, tokens, features), "ctx", split_axis=0, concat_axis=0, tiled=True
    ).reshape(seq_len, features)

    key_rows, value_rows = all_kv[:, :HD], all_kv[:, HD:]
    grad_heads = grad_context.reshape(tokens, heads_here, HD)
    grad_prob = jnp.einsum("qhd,kd->hqk", grad_heads, value_rows, preferred_element_type=F32)
    row_delta = jnp.sum(grad_heads.astype(F32) * context_heads.astype(F32), axis=2)
    grad_score = (attn_prob * (grad_prob - row_delta.T[:, :, None])).astype(BF16)
    grad_query = (
        jnp.einsum("hqk,kd->qhd", grad_score, key_rows, preferred_element_type=F32) * inv_root
    ).astype(BF16)
    grad_query = grad_query.reshape(tokens, heads_here * HD)
    key_term = (
        jnp.einsum("hqk,qhd->kd", grad_score, query_heads, preferred_element_type=F32) * inv_root
    )
    value_term = jnp.einsum("hqk,qhd->kd", prob_b, grad_heads, preferred_element_type=F32)
    kept_term = jnp.where(my_core == 0, key_term, value_term)
    sent_term = jnp.where(my_core == 0, value_term, key_term).astype(BF16)
    pair_term = (kept_term + tp_move(sent_term, dc=1).astype(F32)).astype(BF16)
    pair_term, column_own = lax.optimization_barrier((pair_term, column_own))
    column_other = tp_move(column_own, dc=1)
    kv_blocks = lax.all_to_all(
        pair_term.reshape(ctx_count, tokens, HD), "ctx", split_axis=0, concat_axis=0, tiled=True
    )

    def over_tokens(left):
        return lax.dot_general(
            left, all_context, (((0,), (0,)), ((), ())), preferred_element_type=F32
        ).astype(BF16)

    kv_blocks, own_rows = lax.optimization_barrier((kv_blocks, over_tokens(column_own)))
    grad_kv = jnp.sum(kv_blocks.astype(F32), axis=0).astype(BF16)
    grad_out_proj_t = in_core_order(own_rows, over_tokens(column_other), 0)
    return (grad_hidden, grad_query, grad_kv, grad_out_proj_t)


def solution(mesh):
    in_specs = (
        P("ctx", "tp"),
        P("ctx", "tp"),
        P("ctx", None),
        P("ctx", None),
        P("ctx", None, "tp"),
        P("ctx", None, "tp"),
        P("ctx", "tp", None),
        P("ctx", "tp"),
        P("ctx", None),
        P("tp", None),
    )
    out_specs = (P("ctx", "tp"), P("ctx", "tp"), P("ctx", "tp"), P("ctx", "tp"))
    return jax.shard_map(
        per_device, mesh=mesh, in_specs=in_specs, out_specs=out_specs, check_vma=False
    )
```

```python
import math

import jax
import jax.numpy as jnp
from jax import lax
from jax.experimental import pallas as pl
from jax.experimental.pallas import tpu as pltpu
from jax.sharding import PartitionSpec as P

HQ = 48
KVH = 8
HD = 128
Z = 4
BF16 = jnp.bfloat16
F32 = jnp.float32


def tp_move(block, dz=0, dx=0, dc=0):
    route = []
    for src in range(Z * 4):
        z, low = src // 4, src % 4
        route.append((src, ((z + dz) % Z) * 4 + (low ^ (dx * 2 + dc))))
    return lax.ppermute(block, "tp", route)


def core_move(block, zero, one):
    route = []
    for src in range(Z * 4):
        z, low = src // 4, src % 4
        dz, dx = (zero, one)[src % 2]
        route.append((src, ((z + dz) % Z) * 4 + (low ^ (dx * 2))))
    return lax.ppermute(block, "tp", route)


def double_ctx(held, bit):
    route = [(c, c ^ (1 << bit)) for c in range(lax.axis_size("ctx"))]
    came = lax.ppermute(held, "ctx", route)
    upper = (lax.axis_index("ctx") >> bit) & 1 == 1
    axis = 0 if bit == 2 else 1
    return jnp.stack([jnp.where(upper, came, held), jnp.where(upper, held, came)], axis=axis)


def rolled(blocks, shift, axis):
    blocks = jnp.where(shift % 2 == 1, jnp.roll(blocks, 1, axis=axis), blocks)
    return jnp.where(shift >= 2, jnp.roll(blocks, 2, axis=axis), blocks)


def route_tables(expert_ids, route_weights, groups, capacity):
    tokens = expert_ids.shape[0]
    flat_ids = expert_ids.reshape(-1)
    numbers = jnp.arange(groups, dtype=jnp.int32)
    hits = (flat_ids[:, None] == numbers[None, :]).astype(jnp.int32)
    earlier = jnp.cumsum(hits, axis=0) - hits
    slot_rank = jnp.sum(earlier * hits, axis=1)
    targets = (flat_ids * capacity + slot_rank).reshape(tokens, 2)
    slot_index = jnp.arange(groups * capacity, dtype=jnp.int32)[:, None]
    first_hit = slot_index == targets[None, :, 0]
    second_hit = slot_index == targets[None, :, 1]
    placing = (first_hit | second_hit).astype(BF16)
    combine = jnp.where(first_hit, route_weights[None, :, 0], 0.0) + jnp.where(
        second_hit, route_weights[None, :, 1], 0.0
    )
    return (placing, combine)


def swiglu_grads(gate_act, up_act, hidden_grad):
    sigmoid_g = jax.nn.sigmoid(gate_act)
    grad_gate = (hidden_grad * up_act * sigmoid_g * (1.0 + gate_act * (1.0 - sigmoid_g))).astype(
        BF16
    )
    grad_up = (hidden_grad * gate_act * sigmoid_g).astype(BF16)
    return (grad_gate, grad_up)


def contract_last(left, right):
    return lax.dot_general(left, right, (((1,), (1,)), ((), ())), preferred_element_type=F32)


def add_bf16(*terms):
    total = terms[0].astype(F32)
    for term in terms[1:]:
        total = total + term.astype(F32)
    return total.astype(BF16)


def context_kernel(ids_ref, pieces_ref, first_ref, second_ref, before_ref, out_ref, total):
    step = pl.program_id(0)

    @pl.when(step == 0)
    def _():
        total[...] = before_ref[...]

    total[...] += contract_last(pieces_ref[0, 0], first_ref[...]) + contract_last(
        pieces_ref[0, 1], second_ref[...]
    )

    @pl.when(step == pl.num_programs(0) - 1)
    def _():
        out_ref[...] = total[...].astype(out_ref.dtype)


def context_grad(ids, pieces, weight, before, dtype):
    count, _, rows, width = pieces.shape
    outs = weight.shape[0]
    whole = pl.BlockSpec((rows, outs), lambda i, ids: (0, 0))
    return pl.pallas_call(
        context_kernel,
        grid_spec=pltpu.PrefetchScalarGridSpec(
            num_scalar_prefetch=1,
            grid=(count,),
            in_specs=[
                pl.BlockSpec((1, 2, rows, width), lambda i, ids: (i, 0, 0, 0)),
                pl.BlockSpec((outs, width), lambda i, ids: (0, ids[i])),
                pl.BlockSpec((outs, width), lambda i, ids: (0, ids[i + count])),
                whole,
            ],
            out_specs=whole,
            scratch_shapes=[pltpu.VMEM((rows, outs), F32)],
        ),
        out_shape=jax.ShapeDtypeStruct((rows, outs), dtype),
        compiler_params=pltpu.CompilerParams(vmem_limit_bytes=8 * 2**20),
        cost_estimate=pl.CostEstimate(
            flops=4 * count * rows * width * outs,
            bytes_accessed=4 * count * width * (outs + rows),
            transcendentals=0,
        ),
    )(ids, pieces, weight, weight, before)


def per_device(
    moe_input,
    grad_output,
    expert_ids,
    route_weights,
    w_gate,
    w_up,
    w_down,
    queries,
    keys_values,
    out_proj,
):
    ctx_count = lax.axis_size("ctx")
    tp_rank = lax.axis_index("tp")
    ctx_rank = lax.axis_index("ctx")
    my_z, my_x, my_core = tp_rank // 4, (tp_rank // 2) % 2, tp_rank % 2
    tokens, features = moe_input.shape
    capacity = tokens // 2
    slot_rows = ctx_count * capacity
    gate_w, up_w, down_w = w_gate[0], w_up[0], w_down[0]

    def chunk_of(dz, dx, dc):
        return ((my_z + dz) % Z) * 4 + (my_x ^ dx) * 2 + (my_core ^ dc)

    placing, combine = route_tables(expert_ids, route_weights, ctx_count, capacity)
    first_core = my_core == 0

    def in_core_order(own, other, axis):
        return jnp.concatenate(
            [jnp.where(first_core, own, other), jnp.where(first_core, other, own)], axis=axis
        )

    came = tp_move(jnp.where(first_core, moe_input, grad_output), dc=1)
    carried = in_core_order(jnp.where(first_core, grad_output, moe_input), came, 1)
    send = jnp.dot(placing, carried, preferred_element_type=F32).astype(BF16)
    got = lax.all_to_all(
        send.reshape(ctx_count, capacity, 2 * features), "ctx", split_axis=0, concat_axis=0, tiled=True
    ).reshape(slot_rows, 2 * features)

    heads_here = queries.shape[1] // HD
    group_size = HQ // KVH
    kv_group = tp_rank * heads_here // group_size
    mine_kv = lax.dynamic_slice_in_dim(keys_values, kv_group * 2 * HD, 2 * HD, 1)
    part_kv, got = lax.optimization_barrier((double_ctx(mine_kv, 2), got))
    all_kv = double_ctx(double_ctx(part_kv, 0), 1).reshape(-1, 2 * HD)
    seq_len = ctx_count * tokens
    query_heads = queries.reshape(tokens, heads_here, HD)
    inv_root = 1.0 / math.sqrt(HD)

    def attention_forward(all_kv):
        key_rows, value_rows = all_kv[:, :HD], all_kv[:, HD:]
        query_pos = ctx_rank * tokens + jnp.arange(tokens, dtype=jnp.int32)
        causal = query_pos[:, None] >= jnp.arange(seq_len, dtype=jnp.int32)[None, :]
        scores = (
            jnp.einsum("qhd,kd->hqk", query_heads, key_rows, preferred_element_type=F32) * inv_root
        )
        scores = jnp.where(causal[None], scores, -1e30)
        row_max = jnp.max(scores, axis=2, keepdims=True)
        exp_scores = jnp.exp(scores - row_max)
        attn_prob = exp_scores / jnp.sum(exp_scores, axis=2, keepdims=True)
        prob_b = attn_prob.astype(BF16)
        context_heads = jnp.einsum(
            "hqk,kd->qhd", prob_b, value_rows, preferred_element_type=F32
        ).astype(BF16)
        return context_heads, attn_prob, prob_b

    half, width = slot_rows // 2, 2 * features
    hop_1 = core_move(got, (1, 0), (0, 1))
    hop_2 = core_move(got, (3, 0), (1, 0))
    hop_3 = core_move(got, (0, 1), (3, 0))
    hop_3, all_kv = lax.optimization_barrier((hop_3, all_kv))
    context_heads, attn_prob, prob_b = attention_forward(all_kv)
    context = context_heads.reshape(tokens, heads_here * HD)
    far_low = core_move(jnp.where(first_core, hop_1[:half], hop_2[:half]), (1, 0), (1, 0))
    far_high = core_move(jnp.where(first_core, hop_2[half:], hop_3[half:]), (3, 0), (3, 0))
    hop_6 = core_move(hop_1, (0, 1), (1, 0))
    hop_7 = core_move(jnp.where(first_core, hop_2, hop_1), (0, 1), (3, 0))
    hop_6, context = lax.optimization_barrier((hop_6, context))
    far = jnp.concatenate([far_low, far_high], axis=0)
    cross_low = core_move(jnp.where(first_core, far_low, hop_6[:half]), (0, 1), (1, 0))
    cross_high = core_move(jnp.where(first_core, far_high, hop_7[half:]), (0, 1), (3, 0))
    far_cross = jnp.concatenate([cross_low, cross_high], axis=0)

    arrivals = (
        (got, (0, 0), (0, 0)),
        (hop_1, (3, 0), (0, 1)),
        (hop_2, (1, 0), (3, 0)),
        (hop_3, (0, 1), (1, 0)),
        (far, (2, 0), (2, 0)),
        (hop_6, (3, 1), (3, 1)),
        (hop_7, (1, 1), (1, 1)),
        (far_cross, (2, 1), (2, 1)),
    )
    gate_act = up_act = hidden_grad = 0.0
    for block, dy_from, x_from in arrivals:
        crossed = tp_move(block, dc=1)
        x_rows = jnp.where(first_core, crossed, block)
        dy_rows = jnp.where(first_core, block, crossed)
        x_start = (chunk_of(*x_from, 0) // 2) * width
        dy_start = (chunk_of(*dy_from, 0) // 2) * width
        gate_rows = lax.dynamic_slice_in_dim(gate_w, x_start, width, 0)
        up_rows = lax.dynamic_slice_in_dim(up_w, x_start, width, 0)
        down_cols = lax.dynamic_slice_in_dim(down_w, dy_start, width, 1)
        gate_act = gate_act + jnp.dot(x_rows, gate_rows, preferred_element_type=F32)
        up_act = up_act + jnp.dot(x_rows, up_rows, preferred_element_type=F32)
        hidden_grad = hidden_grad + contract_last(dy_rows, down_cols)
    grad_gate, grad_up = swiglu_grads(gate_act, up_act, hidden_grad)

    def routed(dz, core_0, core_1, after):
        start, _ = lax.optimization_barrier((((my_z + dz) % Z) * 2 * width, after))
        gate_rows = lax.dynamic_slice_in_dim(gate_w, start, 2 * width, 0)
        up_rows = lax.dynamic_slice_in_dim(up_w, start, 2 * width, 0)
        gate_half = jnp.where(first_core, grad_gate[core_0], grad_gate[core_1])
        up_half = jnp.where(first_core, grad_up[core_0], grad_up[core_1])
        return (contract_last(gate_rows, gate_half) + contract_last(up_rows, up_half)).astype(BF16)

    lower, upper = slice(None, half), slice(half, None)
    order = (2, 1, 3, 0)
    sent, after = {}, grad_gate
    for dz in order:
        sent[dz] = after = routed(dz, upper, lower, after)

    cut = features

    def stack_for(zero, one):
        return jnp.where(first_core, jnp.stack(zero), jnp.stack(one))

    def low(rows):
        return rows[:cut]

    def high(rows):
        return rows[cut:]

    def both(rows):
        return (low(rows), high(rows))

    near, cross, loads = {}, {}, []
    for dz in order:
        own = add_bf16(routed(dz, lower, upper, after), tp_move(sent[dz], dc=1))
        low_x, high_x = own[:width], own[width:]
        near[dz] = jnp.where(my_x == 0, low_x, high_x)
        cross[dz] = jnp.where(my_x == 0, high_x, low_x)
        if dz == 2:
            loads.append(stack_for(both(cross[2]), (low(near[2]), low(cross[2]))))
        elif dz == 3:
            loads.append(stack_for((high(cross[1]), low(cross[3])), (high(near[2]), high(cross[2]))))
            loads.append(stack_for((low(cross[1]), high(cross[3])), (high(near[1]), high(cross[1]))))
        elif dz == 0:
            loads.append(stack_for(both(cross[0]), (low(near[3]), low(cross[3]))))
        after = near[1] if dz == 1 else loads[-1]
    sum_1 = core_move(loads[0], (0, 1), (1, 0))
    sum_1, context = lax.optimization_barrier((sum_1, context))
    part_context = double_ctx(context, 2)
    sum_2 = core_move(loads[1], (0, 1), (3, 0))
    sum_3 = core_move(loads[2], (0, 1), (1, 0))
    sum_4 = core_move(loads[3], (0, 1), (3, 0))
    over_2 = [add_bf16(low(near[2]), sum_1[0]), add_bf16(high(near[2]), sum_1[1])]
    over_1 = [None, add_bf16(high(near[1]), sum_2[0])]
    over_3 = [add_bf16(low(near[3]), sum_2[1]), None]
    down = [add_bf16(high(near[3]), sum_2[0]), add_bf16(high(cross[3]), sum_2[1])]
    up = [add_bf16(low(near[1]), sum_1[0]), add_bf16(low(cross[1]), sum_1[1])]
    load_5 = stack_for((over_2[0], over_1[1]), down)
    load_6 = stack_for((over_2[1], over_3[0]), up)
    sum_3, sum_4, _, _ = lax.optimization_barrier((sum_3, sum_4, load_5, load_6))
    sum_5 = core_move(load_5, (1, 0), (3, 0))
    sum_5, part_context = lax.optimization_barrier((sum_5, part_context))
    sum_6 = core_move(load_6, (3, 0), (1, 0))
    over_1[0] = add_bf16(low(near[1]), sum_3[0])
    over_3[1] = add_bf16(high(near[3]), sum_3[1])
    z_near = [add_bf16(low(near[0]), sum_4[0], sum_6[0]), add_bf16(high(near[0]), sum_3[0], sum_5[0])]
    z_cross = [
        add_bf16(low(cross[0]), sum_4[1], sum_6[1]),
        add_bf16(high(cross[0]), sum_3[1], sum_5[1]),
    ]
    sum_7 = core_move(jnp.where(first_core, add_bf16(over_1[0], sum_5[0]), z_cross[0]), (1, 0), (0, 1))
    sum_8 = core_move(jnp.where(first_core, add_bf16(over_3[1], sum_6[0]), z_cross[1]), (3, 0), (0, 1))
    zero_low = add_bf16(low(near[0]), sum_4[0], sum_6[1], sum_7)
    zero_high = add_bf16(high(near[0]), sum_4[1], sum_5[1], sum_8)
    one_low, one_high = add_bf16(z_near[0], sum_7), add_bf16(z_near[1], sum_8)
    total = jnp.concatenate(
        [jnp.where(first_core, zero_low, one_low), jnp.where(first_core, zero_high, one_high)], axis=0
    )
    left, right = total[:features], total[features:]
    came = tp_move(jnp.where(first_core, right, left), dc=1)
    own_slice = in_core_order(jnp.where(first_core, left, right), came, 1).T

    returned = lax.all_to_all(
        own_slice.reshape(ctx_count, capacity, features), "ctx", split_axis=0, concat_axis=0, tiled=True
    ).reshape(slot_rows, features)
    part_context = double_ctx(double_ctx(part_context, 0), 1)
    returned, part_context = lax.optimization_barrier((returned, part_context))
    all_context = part_context.reshape(-1, heads_here * HD)
    moe_part = lax.dot_general(
        combine,
        returned.astype(F32),
        (((0,), (0,)), ((), ())),
        precision=lax.Precision.HIGHEST,
        preferred_element_type=F32,
    )
    grad_hidden = (grad_output.astype(F32) + moe_part).astype(BF16)

    one_half, other_half = grad_hidden[: tokens // 2], grad_hidden[tokens // 2 :]
    low_pair = jnp.stack([one_half, tp_move(one_half, dx=1)])
    high_z = jnp.stack([other_half] + [tp_move(other_half, dz=dz) for dz in (1, 2, 3)])
    low_all = jnp.stack([low_pair] + [tp_move(low_pair, dz=dz) for dz in (1, 2, 3)])
    high_all = jnp.stack([high_z, tp_move(high_z, dx=1)], axis=1)
    same_core = jnp.concatenate([low_all, high_all], axis=2)
    swapped = jnp.where(my_x == 0, same_core, same_core[:, ::-1])
    ordered = jnp.stack([swapped[0], swapped[3], swapped[2], swapped[1]])
    ids = jnp.stack([(my_z + i) % Z * 4 + x * 2 for x in (0, 1) for i in range(Z)])
    grad_context = context_grad(
        ids + my_core, ordered, out_proj, jnp.zeros((tokens, features), F32), F32
    )
    grad_context = context_grad(
        ids + 1 - my_core, tp_move(ordered, dc=1), out_proj, grad_context, BF16
    )

    by_owner = rolled(ordered, my_z, 0)
    column_own = lax.all_to_all(
        by_owner.reshape(ctx_count, tokens, features), "ctx", split_axis=0, concat_axis=0, tiled=True
    ).reshape(seq_len, features)

    key_rows, value_rows = all_kv[:, :HD], all_kv[:, HD:]
    grad_heads = grad_context.reshape(tokens, heads_here, HD)
    grad_prob = jnp.einsum("qhd,kd->hqk", grad_heads, value_rows, preferred_element_type=F32)
    row_delta = jnp.sum(grad_heads.astype(F32) * context_heads.astype(F32), axis=2)
    grad_score = (attn_prob * (grad_prob - row_delta.T[:, :, None])).astype(BF16)
    grad_query = (
        jnp.einsum("hqk,kd->qhd", grad_score, key_rows, preferred_element_type=F32) * inv_root
    ).astype(BF16)
    grad_query = grad_query.reshape(tokens, heads_here * HD)
    key_term = (
        jnp.einsum("hqk,qhd->kd", grad_score, query_heads, preferred_element_type=F32) * inv_root
    )
    value_term = jnp.einsum("hqk,qhd->kd", prob_b, grad_heads, preferred_element_type=F32)
    kept_term = jnp.where(my_core == 0, key_term, value_term)
    sent_term = jnp.where(my_core == 0, value_term, key_term).astype(BF16)
    pair_term = (kept_term + tp_move(sent_term, dc=1).astype(F32)).astype(BF16)
    pair_term, column_own = lax.optimization_barrier((pair_term, column_own))
    column_other = tp_move(column_own, dc=1)
    kv_blocks = lax.all_to_all(
        pair_term.reshape(ctx_count, tokens, HD), "ctx", split_axis=0, concat_axis=0, tiled=True
    )

    def over_tokens(left):
        return lax.dot_general(
            left, all_context, (((0,), (0,)), ((), ())), preferred_element_type=F32
        ).astype(BF16)

    grad_out_proj_t = in_core_order(over_tokens(column_own), over_tokens(column_other), 0)
    kv_blocks, grad_out_proj_t = lax.optimization_barrier((kv_blocks, grad_out_proj_t))
    grad_kv = jnp.sum(kv_blocks.astype(F32), axis=0).astype(BF16)
    return (grad_hidden, grad_query, grad_kv, grad_out_proj_t)


def solution(mesh):
    in_specs = (
        P("ctx", "tp"),
        P("ctx", "tp"),
        P("ctx", None),
        P("ctx", None),
        P("ctx", None, "tp"),
        P("ctx", None, "tp"),
        P("ctx", "tp", None),
        P("ctx", "tp"),
        P("ctx", None),
        P("tp", None),
    )
    out_specs = (P("ctx", "tp"), P("ctx", "tp"), P("ctx", "tp"), P("ctx", "tp"))
    return jax.shard_map(
        per_device, mesh=mesh, in_specs=in_specs, out_specs=out_specs, check_vma=False
    )
```

```python
import math

import jax
import jax.numpy as jnp
from jax import lax
from jax.experimental import pallas as pl
from jax.experimental.pallas import tpu as pltpu
from jax.sharding import PartitionSpec as P

HQ = 48
KVH = 8
HD = 128
Z = 4
BF16 = jnp.bfloat16
F32 = jnp.float32


def tp_move(block, dz=0, dx=0, dc=0):
    route = []
    for src in range(Z * 4):
        z, low = src // 4, src % 4
        route.append((src, ((z + dz) % Z) * 4 + (low ^ (dx * 2 + dc))))
    return lax.ppermute(block, "tp", route)


def core_move(block, zero, one):
    route = []
    for src in range(Z * 4):
        z, low = src // 4, src % 4
        dz, dx = (zero, one)[src % 2]
        route.append((src, ((z + dz) % Z) * 4 + (low ^ (dx * 2))))
    return lax.ppermute(block, "tp", route)


def double_ctx(held, bit):
    route = [(c, c ^ (1 << bit)) for c in range(lax.axis_size("ctx"))]
    came = lax.ppermute(held, "ctx", route)
    upper = (lax.axis_index("ctx") >> bit) & 1 == 1
    axis = 0 if bit == 2 else 1
    return jnp.stack([jnp.where(upper, came, held), jnp.where(upper, held, came)], axis=axis)


def rolled(blocks, shift, axis):
    blocks = jnp.where(shift % 2 == 1, jnp.roll(blocks, 1, axis=axis), blocks)
    return jnp.where(shift >= 2, jnp.roll(blocks, 2, axis=axis), blocks)


def route_tables(expert_ids, route_weights, groups, capacity):
    tokens = expert_ids.shape[0]
    flat_ids = expert_ids.reshape(-1)
    numbers = jnp.arange(groups, dtype=jnp.int32)
    hits = (flat_ids[:, None] == numbers[None, :]).astype(jnp.int32)
    earlier = jnp.cumsum(hits, axis=0) - hits
    slot_rank = jnp.sum(earlier * hits, axis=1)
    targets = (flat_ids * capacity + slot_rank).reshape(tokens, 2)
    slot_index = jnp.arange(groups * capacity, dtype=jnp.int32)[:, None]
    first_hit = slot_index == targets[None, :, 0]
    second_hit = slot_index == targets[None, :, 1]
    placing = (first_hit | second_hit).astype(BF16)
    combine = jnp.where(first_hit, route_weights[None, :, 0], 0.0) + jnp.where(
        second_hit, route_weights[None, :, 1], 0.0
    )
    return (placing, combine)


def swiglu_grads(gate_act, up_act, hidden_grad):
    sigmoid_g = jax.nn.sigmoid(gate_act)
    grad_gate = (hidden_grad * up_act * sigmoid_g * (1.0 + gate_act * (1.0 - sigmoid_g))).astype(
        BF16
    )
    grad_up = (hidden_grad * gate_act * sigmoid_g).astype(BF16)
    return (grad_gate, grad_up)


def contract_last(left, right):
    return lax.dot_general(left, right, (((1,), (1,)), ((), ())), preferred_element_type=F32)


def add_bf16(*terms):
    total = terms[0].astype(F32)
    for term in terms[1:]:
        total = total + term.astype(F32)
    return total.astype(BF16)


def context_kernel(ids_ref, pieces_ref, first_ref, second_ref, before_ref, out_ref, total):
    step = pl.program_id(0)

    @pl.when(step == 0)
    def _():
        total[...] = before_ref[...]

    total[...] += contract_last(pieces_ref[0, 0], first_ref[...]) + contract_last(
        pieces_ref[0, 1], second_ref[...]
    )

    @pl.when(step == pl.num_programs(0) - 1)
    def _():
        out_ref[...] = total[...].astype(out_ref.dtype)


def context_grad(ids, pieces, weight, before, dtype):
    count, _, rows, width = pieces.shape
    outs = weight.shape[0]
    whole = pl.BlockSpec((rows, outs), lambda i, ids: (0, 0))
    return pl.pallas_call(
        context_kernel,
        grid_spec=pltpu.PrefetchScalarGridSpec(
            num_scalar_prefetch=1,
            grid=(count,),
            in_specs=[
                pl.BlockSpec((1, 2, rows, width), lambda i, ids: (i, 0, 0, 0)),
                pl.BlockSpec((outs, width), lambda i, ids: (0, ids[i])),
                pl.BlockSpec((outs, width), lambda i, ids: (0, ids[i + count])),
                whole,
            ],
            out_specs=whole,
            scratch_shapes=[pltpu.VMEM((rows, outs), F32)],
        ),
        out_shape=jax.ShapeDtypeStruct((rows, outs), dtype),
        compiler_params=pltpu.CompilerParams(vmem_limit_bytes=8 * 2**20),
        cost_estimate=pl.CostEstimate(
            flops=4 * count * rows * width * outs,
            bytes_accessed=4 * count * width * (outs + rows),
            transcendentals=0,
        ),
    )(ids, pieces, weight, weight, before)


def per_device(
    moe_input,
    grad_output,
    expert_ids,
    route_weights,
    w_gate,
    w_up,
    w_down,
    queries,
    keys_values,
    out_proj,
):
    ctx_count = lax.axis_size("ctx")
    tp_rank = lax.axis_index("tp")
    ctx_rank = lax.axis_index("ctx")
    my_z, my_x, my_core = tp_rank // 4, (tp_rank // 2) % 2, tp_rank % 2
    tokens, features = moe_input.shape
    capacity = tokens // 2
    slot_rows = ctx_count * capacity
    gate_w, up_w, down_w = w_gate[0], w_up[0], w_down[0]

    def chunk_of(dz, dx, dc):
        return ((my_z + dz) % Z) * 4 + (my_x ^ dx) * 2 + (my_core ^ dc)

    placing, combine = route_tables(expert_ids, route_weights, ctx_count, capacity)
    first_core = my_core == 0

    def in_core_order(own, other, axis):
        return jnp.concatenate(
            [jnp.where(first_core, own, other), jnp.where(first_core, other, own)], axis=axis
        )

    came = tp_move(jnp.where(first_core, moe_input, grad_output), dc=1)
    carried = in_core_order(jnp.where(first_core, grad_output, moe_input), came, 1)
    send = jnp.dot(placing, carried, preferred_element_type=F32).astype(BF16)
    got = lax.all_to_all(
        send.reshape(ctx_count, capacity, 2 * features), "ctx", split_axis=0, concat_axis=0, tiled=True
    ).reshape(slot_rows, 2 * features)

    heads_here = queries.shape[1] // HD
    group_size = HQ // KVH
    kv_group = tp_rank * heads_here // group_size
    mine_kv = lax.dynamic_slice_in_dim(keys_values, kv_group * 2 * HD, 2 * HD, 1)
    part_kv, got = lax.optimization_barrier((double_ctx(mine_kv, 2), got))
    all_kv = double_ctx(double_ctx(part_kv, 0), 1).reshape(-1, 2 * HD)
    seq_len = ctx_count * tokens
    query_heads = queries.reshape(tokens, heads_here, HD)
    inv_root = 1.0 / math.sqrt(HD)

    def attention_forward(all_kv):
        key_rows, value_rows = all_kv[:, :HD], all_kv[:, HD:]
        query_pos = ctx_rank * tokens + jnp.arange(tokens, dtype=jnp.int32)
        causal = query_pos[:, None] >= jnp.arange(seq_len, dtype=jnp.int32)[None, :]
        scores = (
            jnp.einsum("qhd,kd->hqk", query_heads, key_rows, preferred_element_type=F32) * inv_root
        )
        scores = jnp.where(causal[None], scores, -1e30)
        row_max = jnp.max(scores, axis=2, keepdims=True)
        exp_scores = jnp.exp(scores - row_max)
        attn_prob = exp_scores / jnp.sum(exp_scores, axis=2, keepdims=True)
        prob_b = attn_prob.astype(BF16)
        context_heads = jnp.einsum(
            "hqk,kd->qhd", prob_b, value_rows, preferred_element_type=F32
        ).astype(BF16)
        return context_heads, attn_prob, prob_b

    half, width = slot_rows // 2, 2 * features
    hop_1 = core_move(got, (1, 0), (0, 1))
    hop_2 = core_move(got, (3, 0), (1, 0))
    hop_3 = core_move(got, (0, 1), (3, 0))
    hop_3, all_kv = lax.optimization_barrier((hop_3, all_kv))
    context_heads, attn_prob, prob_b = attention_forward(all_kv)
    context = context_heads.reshape(tokens, heads_here * HD)
    far_low = core_move(jnp.where(first_core, hop_1[:half], hop_2[:half]), (1, 0), (1, 0))
    far_high = core_move(jnp.where(first_core, hop_2[half:], hop_3[half:]), (3, 0), (3, 0))
    hop_6 = core_move(hop_1, (0, 1), (1, 0))
    hop_7 = core_move(jnp.where(first_core, hop_2, hop_1), (0, 1), (3, 0))
    hop_6, context = lax.optimization_barrier((hop_6, context))
    far = jnp.concatenate([far_low, far_high], axis=0)
    cross_low = core_move(jnp.where(first_core, far_low, hop_6[:half]), (0, 1), (1, 0))
    cross_high = core_move(jnp.where(first_core, far_high, hop_7[half:]), (0, 1), (3, 0))
    far_cross = jnp.concatenate([cross_low, cross_high], axis=0)

    arrivals = (
        (got, (0, 0), (0, 0)),
        (hop_1, (3, 0), (0, 1)),
        (hop_2, (1, 0), (3, 0)),
        (hop_3, (0, 1), (1, 0)),
        (far, (2, 0), (2, 0)),
        (hop_6, (3, 1), (3, 1)),
        (hop_7, (1, 1), (1, 1)),
        (far_cross, (2, 1), (2, 1)),
    )
    gate_act = up_act = hidden_grad = 0.0
    for block, dy_from, x_from in arrivals:
        crossed = tp_move(block, dc=1)
        x_rows = jnp.where(first_core, crossed, block)
        dy_rows = jnp.where(first_core, block, crossed)
        x_start = (chunk_of(*x_from, 0) // 2) * width
        dy_start = (chunk_of(*dy_from, 0) // 2) * width
        gate_rows = lax.dynamic_slice_in_dim(gate_w, x_start, width, 0)
        up_rows = lax.dynamic_slice_in_dim(up_w, x_start, width, 0)
        down_cols = lax.dynamic_slice_in_dim(down_w, dy_start, width, 1)
        gate_act = gate_act + jnp.dot(x_rows, gate_rows, preferred_element_type=F32)
        up_act = up_act + jnp.dot(x_rows, up_rows, preferred_element_type=F32)
        hidden_grad = hidden_grad + contract_last(dy_rows, down_cols)
    grad_gate, grad_up = swiglu_grads(gate_act, up_act, hidden_grad)

    def routed(core_0, core_1):
        gate_half = jnp.where(first_core, grad_gate[core_0], grad_gate[core_1])
        up_half = jnp.where(first_core, grad_up[core_0], grad_up[core_1])
        return (contract_last(gate_w, gate_half) + contract_last(up_w, up_half)).astype(BF16)

    lower, upper = slice(None, half), slice(half, None)
    sent = routed(upper, lower)
    arrived = tp_move(sent, dc=1)
    grad_gate, sent = lax.optimization_barrier((grad_gate, sent))
    kept = routed(lower, upper)

    cut = features

    def stack_for(zero, one):
        return jnp.where(first_core, jnp.stack(zero), jnp.stack(one))

    def low(rows):
        return rows[:cut]

    def high(rows):
        return rows[cut:]

    def both(rows):
        return (low(rows), high(rows))

    near, cross = {}, {}
    for dz in (2, 1, 3, 0):

        def chip_rows(dx):
            start = (chunk_of(dz, dx, 0) // 2) * width
            return add_bf16(
                lax.dynamic_slice_in_dim(kept, start, width, 0),
                lax.dynamic_slice_in_dim(arrived, start, width, 0),
            )

        near[dz], cross[dz] = chip_rows(0), chip_rows(1)
        if dz == 2:
            load_1 = stack_for(both(cross[2]), (low(near[2]), low(cross[2])))
            load_1, kept = lax.optimization_barrier((load_1, kept))
    loads = (
        load_1,
        stack_for((high(cross[1]), low(cross[3])), (high(near[2]), high(cross[2]))),
        stack_for((low(cross[1]), high(cross[3])), (high(near[1]), high(cross[1]))),
        stack_for(both(cross[0]), (low(near[3]), low(cross[3]))),
    )
    sum_1 = core_move(loads[0], (0, 1), (1, 0))
    sum_1, context = lax.optimization_barrier((sum_1, context))
    part_context = double_ctx(context, 2)
    sum_2 = core_move(loads[1], (0, 1), (3, 0))
    sum_3 = core_move(loads[2], (0, 1), (1, 0))
    sum_4 = core_move(loads[3], (0, 1), (3, 0))
    over_2 = [add_bf16(low(near[2]), sum_1[0]), add_bf16(high(near[2]), sum_1[1])]
    over_1 = [None, add_bf16(high(near[1]), sum_2[0])]
    over_3 = [add_bf16(low(near[3]), sum_2[1]), None]
    down = [add_bf16(high(near[3]), sum_2[0]), add_bf16(high(cross[3]), sum_2[1])]
    up = [add_bf16(low(near[1]), sum_1[0]), add_bf16(low(cross[1]), sum_1[1])]
    load_5 = stack_for((over_2[0], over_1[1]), down)
    load_6 = stack_for((over_2[1], over_3[0]), up)
    sum_3, sum_4, _, _ = lax.optimization_barrier((sum_3, sum_4, load_5, load_6))
    sum_5 = core_move(load_5, (1, 0), (3, 0))
    sum_5, part_context = lax.optimization_barrier((sum_5, part_context))
    sum_6 = core_move(load_6, (3, 0), (1, 0))
    over_1[0] = add_bf16(low(near[1]), sum_3[0])
    over_3[1] = add_bf16(high(near[3]), sum_3[1])
    z_near = [add_bf16(low(near[0]), sum_4[0], sum_6[0]), add_bf16(high(near[0]), sum_3[0], sum_5[0])]
    z_cross = [
        add_bf16(low(cross[0]), sum_4[1], sum_6[1]),
        add_bf16(high(cross[0]), sum_3[1], sum_5[1]),
    ]
    sum_7 = core_move(jnp.where(first_core, add_bf16(over_1[0], sum_5[0]), z_cross[0]), (1, 0), (0, 1))
    sum_8 = core_move(jnp.where(first_core, add_bf16(over_3[1], sum_6[0]), z_cross[1]), (3, 0), (0, 1))
    zero_low = add_bf16(low(near[0]), sum_4[0], sum_6[1], sum_7)
    zero_high = add_bf16(high(near[0]), sum_4[1], sum_5[1], sum_8)
    one_low, one_high = add_bf16(z_near[0], sum_7), add_bf16(z_near[1], sum_8)
    total = jnp.concatenate(
        [jnp.where(first_core, zero_low, one_low), jnp.where(first_core, zero_high, one_high)], axis=0
    )
    left, right = total[:features], total[features:]
    came = tp_move(jnp.where(first_core, right, left), dc=1)
    own_slice = in_core_order(jnp.where(first_core, left, right), came, 1).T

    returned = lax.all_to_all(
        own_slice.reshape(ctx_count, capacity, features), "ctx", split_axis=0, concat_axis=0, tiled=True
    ).reshape(slot_rows, features)
    part_context = double_ctx(double_ctx(part_context, 0), 1)
    returned, part_context = lax.optimization_barrier((returned, part_context))
    all_context = part_context.reshape(-1, heads_here * HD)
    moe_part = lax.dot_general(
        combine,
        returned.astype(F32),
        (((0,), (0,)), ((), ())),
        precision=lax.Precision.HIGHEST,
        preferred_element_type=F32,
    )
    grad_hidden = (grad_output.astype(F32) + moe_part).astype(BF16)

    one_half, other_half = grad_hidden[: tokens // 2], grad_hidden[tokens // 2 :]
    low_pair = jnp.stack([one_half, tp_move(one_half, dx=1)])
    high_z = jnp.stack([other_half] + [tp_move(other_half, dz=dz) for dz in (1, 2, 3)])
    low_all = jnp.stack([low_pair] + [tp_move(low_pair, dz=dz) for dz in (1, 2, 3)])
    high_all = jnp.stack([high_z, tp_move(high_z, dx=1)], axis=1)
    same_core = jnp.concatenate([low_all, high_all], axis=2)
    swapped = jnp.where(my_x == 0, same_core, same_core[:, ::-1])
    ordered = jnp.stack([swapped[0], swapped[3], swapped[2], swapped[1]])
    ids = jnp.stack([(my_z + i) % Z * 4 + x * 2 for x in (0, 1) for i in range(Z)])
    grad_context = context_grad(
        ids + my_core, ordered, out_proj, jnp.zeros((tokens, features), F32), F32
    )
    grad_context = context_grad(
        ids + 1 - my_core, tp_move(ordered, dc=1), out_proj, grad_context, BF16
    )

    by_owner = rolled(ordered, my_z, 0)
    column_own = lax.all_to_all(
        by_owner.reshape(ctx_count, tokens, features), "ctx", split_axis=0, concat_axis=0, tiled=True
    ).reshape(seq_len, features)

    key_rows, value_rows = all_kv[:, :HD], all_kv[:, HD:]
    grad_heads = grad_context.reshape(tokens, heads_here, HD)
    grad_prob = jnp.einsum("qhd,kd->hqk", grad_heads, value_rows, preferred_element_type=F32)
    row_delta = jnp.sum(grad_heads.astype(F32) * context_heads.astype(F32), axis=2)
    grad_score = (attn_prob * (grad_prob - row_delta.T[:, :, None])).astype(BF16)
    grad_query = (
        jnp.einsum("hqk,kd->qhd", grad_score, key_rows, preferred_element_type=F32) * inv_root
    ).astype(BF16)
    grad_query = grad_query.reshape(tokens, heads_here * HD)
    key_term = (
        jnp.einsum("hqk,qhd->kd", grad_score, query_heads, preferred_element_type=F32) * inv_root
    )
    value_term = jnp.einsum("hqk,qhd->kd", prob_b, grad_heads, preferred_element_type=F32)
    kept_term = jnp.where(my_core == 0, key_term, value_term)
    sent_term = jnp.where(my_core == 0, value_term, key_term).astype(BF16)
    pair_term = (kept_term + tp_move(sent_term, dc=1).astype(F32)).astype(BF16)
    pair_term, column_own = lax.optimization_barrier((pair_term, column_own))
    column_other = tp_move(column_own, dc=1)
    kv_blocks = lax.all_to_all(
        pair_term.reshape(ctx_count, tokens, HD), "ctx", split_axis=0, concat_axis=0, tiled=True
    )

    def over_tokens(left):
        return lax.dot_general(
            left, all_context, (((0,), (0,)), ((), ())), preferred_element_type=F32
        ).astype(BF16)

    grad_out_proj_t = in_core_order(over_tokens(column_own), over_tokens(column_other), 0)
    kv_blocks, grad_out_proj_t = lax.optimization_barrier((kv_blocks, grad_out_proj_t))
    grad_kv = jnp.sum(kv_blocks.astype(F32), axis=0).astype(BF16)
    return (grad_hidden, grad_query, grad_kv, grad_out_proj_t)


def solution(mesh):
    in_specs = (
        P("ctx", "tp"),
        P("ctx", "tp"),
        P("ctx", None),
        P("ctx", None),
        P("ctx", None, "tp"),
        P("ctx", None, "tp"),
        P("ctx", "tp", None),
        P("ctx", "tp"),
        P("ctx", None),
        P("tp", None),
    )
    out_specs = (P("ctx", "tp"), P("ctx", "tp"), P("ctx", "tp"), P("ctx", "tp"))
    return jax.shard_map(
        per_device, mesh=mesh, in_specs=in_specs, out_specs=out_specs, check_vma=False
    )
```

```python
import math

import jax
import jax.numpy as jnp
from jax import lax
from jax.experimental import pallas as pl
from jax.experimental.pallas import tpu as pltpu
from jax.sharding import PartitionSpec as P

HQ = 48
KVH = 8
HD = 128
Z = 4
BF16 = jnp.bfloat16
F32 = jnp.float32


def tp_move(block, dz=0, dx=0, dc=0):
    route = []
    for src in range(Z * 4):
        z, low = src // 4, src % 4
        route.append((src, ((z + dz) % Z) * 4 + (low ^ (dx * 2 + dc))))
    return lax.ppermute(block, "tp", route)


def core_move(block, zero, one):
    route = []
    for src in range(Z * 4):
        z, low = src // 4, src % 4
        dz, dx = (zero, one)[src % 2]
        route.append((src, ((z + dz) % Z) * 4 + (low ^ (dx * 2))))
    return lax.ppermute(block, "tp", route)


def double_ctx(held, bit):
    route = [(c, c ^ (1 << bit)) for c in range(lax.axis_size("ctx"))]
    came = lax.ppermute(held, "ctx", route)
    upper = (lax.axis_index("ctx") >> bit) & 1 == 1
    axis = 0 if bit == 2 else 1
    return jnp.stack([jnp.where(upper, came, held), jnp.where(upper, held, came)], axis=axis)


def rolled(blocks, shift, axis):
    blocks = jnp.where(shift % 2 == 1, jnp.roll(blocks, 1, axis=axis), blocks)
    return jnp.where(shift >= 2, jnp.roll(blocks, 2, axis=axis), blocks)


def route_tables(expert_ids, route_weights, groups, capacity):
    tokens = expert_ids.shape[0]
    flat_ids = expert_ids.reshape(-1)
    numbers = jnp.arange(groups, dtype=jnp.int32)
    hits = (flat_ids[:, None] == numbers[None, :]).astype(jnp.int32)
    earlier = jnp.cumsum(hits, axis=0) - hits
    slot_rank = jnp.sum(earlier * hits, axis=1)
    targets = (flat_ids * capacity + slot_rank).reshape(tokens, 2)
    slot_index = jnp.arange(groups * capacity, dtype=jnp.int32)[:, None]
    first_hit = slot_index == targets[None, :, 0]
    second_hit = slot_index == targets[None, :, 1]
    placing = (first_hit | second_hit).astype(BF16)
    combine = jnp.where(first_hit, route_weights[None, :, 0], 0.0) + jnp.where(
        second_hit, route_weights[None, :, 1], 0.0
    )
    return (placing, combine)


def swiglu_grads(gate_act, up_act, hidden_grad):
    sigmoid_g = jax.nn.sigmoid(gate_act)
    grad_gate = (hidden_grad * up_act * sigmoid_g * (1.0 + gate_act * (1.0 - sigmoid_g))).astype(
        BF16
    )
    grad_up = (hidden_grad * gate_act * sigmoid_g).astype(BF16)
    return (grad_gate, grad_up)


def contract_last(left, right):
    return lax.dot_general(left, right, (((1,), (1,)), ((), ())), preferred_element_type=F32)


def add_bf16(*terms):
    total = terms[0].astype(F32)
    for term in terms[1:]:
        total = total + term.astype(F32)
    return total.astype(BF16)


def context_kernel(ids_ref, pieces_ref, first_ref, second_ref, before_ref, out_ref, total):
    step = pl.program_id(0)

    @pl.when(step == 0)
    def _():
        total[...] = before_ref[...]

    total[...] += contract_last(pieces_ref[0, 0], first_ref[...]) + contract_last(
        pieces_ref[0, 1], second_ref[...]
    )

    @pl.when(step == pl.num_programs(0) - 1)
    def _():
        out_ref[...] = total[...].astype(out_ref.dtype)


def context_grad(ids, pieces, weight, before, dtype):
    count, _, rows, width = pieces.shape
    outs = weight.shape[0]
    whole = pl.BlockSpec((rows, outs), lambda i, ids: (0, 0))
    return pl.pallas_call(
        context_kernel,
        grid_spec=pltpu.PrefetchScalarGridSpec(
            num_scalar_prefetch=1,
            grid=(count,),
            in_specs=[
                pl.BlockSpec((1, 2, rows, width), lambda i, ids: (i, 0, 0, 0)),
                pl.BlockSpec((outs, width), lambda i, ids: (0, ids[i])),
                pl.BlockSpec((outs, width), lambda i, ids: (0, ids[i + count])),
                whole,
            ],
            out_specs=whole,
            scratch_shapes=[pltpu.VMEM((rows, outs), F32)],
        ),
        out_shape=jax.ShapeDtypeStruct((rows, outs), dtype),
        compiler_params=pltpu.CompilerParams(vmem_limit_bytes=8 * 2**20),
        cost_estimate=pl.CostEstimate(
            flops=4 * count * rows * width * outs,
            bytes_accessed=4 * count * width * (outs + rows),
            transcendentals=0,
        ),
    )(ids, pieces, weight, weight, before)


def per_device(
    moe_input,
    grad_output,
    expert_ids,
    route_weights,
    w_gate,
    w_up,
    w_down,
    queries,
    keys_values,
    out_proj,
):
    ctx_count = lax.axis_size("ctx")
    tp_rank = lax.axis_index("tp")
    ctx_rank = lax.axis_index("ctx")
    my_z, my_x, my_core = tp_rank // 4, (tp_rank // 2) % 2, tp_rank % 2
    tokens, features = moe_input.shape
    capacity = tokens // 2
    slot_rows = ctx_count * capacity
    gate_w, up_w, down_w = w_gate[0], w_up[0], w_down[0]

    def chunk_of(dz, dx, dc):
        return ((my_z + dz) % Z) * 4 + (my_x ^ dx) * 2 + (my_core ^ dc)

    placing, combine = route_tables(expert_ids, route_weights, ctx_count, capacity)
    first_core = my_core == 0

    def in_core_order(own, other, axis):
        return jnp.concatenate(
            [jnp.where(first_core, own, other), jnp.where(first_core, other, own)], axis=axis
        )

    came = tp_move(jnp.where(first_core, moe_input, grad_output), dc=1)
    carried = in_core_order(jnp.where(first_core, grad_output, moe_input), came, 1)
    send = jnp.dot(placing, carried, preferred_element_type=F32).astype(BF16)
    got = lax.all_to_all(
        send.reshape(ctx_count, capacity, 2 * features), "ctx", split_axis=0, concat_axis=0, tiled=True
    ).reshape(slot_rows, 2 * features)

    heads_here = queries.shape[1] // HD
    group_size = HQ // KVH
    kv_group = tp_rank * heads_here // group_size
    mine_kv = lax.dynamic_slice_in_dim(keys_values, kv_group * 2 * HD, 2 * HD, 1)
    part_kv, got = lax.optimization_barrier((double_ctx(mine_kv, 2), got))
    all_kv = double_ctx(double_ctx(part_kv, 0), 1).reshape(-1, 2 * HD)
    seq_len = ctx_count * tokens
    query_heads = queries.reshape(tokens, heads_here, HD)
    inv_root = 1.0 / math.sqrt(HD)

    def attention_forward(all_kv):
        key_rows, value_rows = all_kv[:, :HD], all_kv[:, HD:]
        query_pos = ctx_rank * tokens + jnp.arange(tokens, dtype=jnp.int32)
        causal = query_pos[:, None] >= jnp.arange(seq_len, dtype=jnp.int32)[None, :]
        scores = (
            jnp.einsum("qhd,kd->hqk", query_heads, key_rows, preferred_element_type=F32) * inv_root
        )
        scores = jnp.where(causal[None], scores, -1e30)
        row_max = jnp.max(scores, axis=2, keepdims=True)
        exp_scores = jnp.exp(scores - row_max)
        attn_prob = exp_scores / jnp.sum(exp_scores, axis=2, keepdims=True)
        prob_b = attn_prob.astype(BF16)
        context_heads = jnp.einsum(
            "hqk,kd->qhd", prob_b, value_rows, preferred_element_type=F32
        ).astype(BF16)
        return context_heads, attn_prob, prob_b

    half, width = slot_rows // 2, 2 * features
    hop_1 = core_move(got, (1, 0), (0, 1))
    hop_2 = core_move(got, (3, 0), (1, 0))
    hop_3 = core_move(got, (0, 1), (3, 0))
    hop_3, all_kv = lax.optimization_barrier((hop_3, all_kv))
    far_low = core_move(jnp.where(first_core, hop_1[:half], hop_2[:half]), (1, 0), (1, 0))
    far_high = core_move(jnp.where(first_core, hop_2[half:], hop_3[half:]), (3, 0), (3, 0))
    hop_6 = core_move(hop_1, (0, 1), (1, 0))
    hop_7 = core_move(jnp.where(first_core, hop_2, hop_1), (0, 1), (3, 0))
    far = jnp.concatenate([far_low, far_high], axis=0)
    cross_low = core_move(jnp.where(first_core, far_low, hop_6[:half]), (0, 1), (1, 0))
    cross_high = core_move(jnp.where(first_core, far_high, hop_7[half:]), (0, 1), (3, 0))
    far_cross = jnp.concatenate([cross_low, cross_high], axis=0)

    arrivals = (
        (got, (0, 0), (0, 0)),
        (hop_1, (3, 0), (0, 1)),
        (hop_2, (1, 0), (3, 0)),
        (hop_3, (0, 1), (1, 0)),
        (far, (2, 0), (2, 0)),
        (hop_6, (3, 1), (3, 1)),
        (hop_7, (1, 1), (1, 1)),
        (far_cross, (2, 1), (2, 1)),
    )
    gate_act = up_act = hidden_grad = 0.0
    for block, dy_from, x_from in arrivals:
        crossed = tp_move(block, dc=1)
        x_rows = jnp.where(first_core, crossed, block)
        dy_rows = jnp.where(first_core, block, crossed)
        x_start = (chunk_of(*x_from, 0) // 2) * width
        dy_start = (chunk_of(*dy_from, 0) // 2) * width
        gate_rows = lax.dynamic_slice_in_dim(gate_w, x_start, width, 0)
        up_rows = lax.dynamic_slice_in_dim(up_w, x_start, width, 0)
        down_cols = lax.dynamic_slice_in_dim(down_w, dy_start, width, 1)
        gate_act = gate_act + jnp.dot(x_rows, gate_rows, preferred_element_type=F32)
        up_act = up_act + jnp.dot(x_rows, up_rows, preferred_element_type=F32)
        hidden_grad = hidden_grad + contract_last(dy_rows, down_cols)
    grad_gate, grad_up = swiglu_grads(gate_act, up_act, hidden_grad)

    def routed(core_0, core_1):
        gate_half = jnp.where(first_core, grad_gate[core_0], grad_gate[core_1])
        up_half = jnp.where(first_core, grad_up[core_0], grad_up[core_1])
        return (contract_last(gate_w, gate_half) + contract_last(up_w, up_half)).astype(BF16)

    lower, upper = slice(None, half), slice(half, None)
    sent = routed(upper, lower)
    arrived = tp_move(sent, dc=1)
    grad_gate, sent = lax.optimization_barrier((grad_gate, sent))
    kept = routed(lower, upper)

    cut = features

    def stack_for(zero, one):
        return jnp.where(first_core, jnp.stack(zero), jnp.stack(one))

    def low(rows):
        return rows[:cut]

    def high(rows):
        return rows[cut:]

    def both(rows):
        return (low(rows), high(rows))

    near, cross = {}, {}
    for dz in (2, 1, 3, 0):

        def chip_rows(dx):
            start = (chunk_of(dz, dx, 0) // 2) * width
            return add_bf16(
                lax.dynamic_slice_in_dim(kept, start, width, 0),
                lax.dynamic_slice_in_dim(arrived, start, width, 0),
            )

        near[dz], cross[dz] = chip_rows(0), chip_rows(1)
        if dz == 2:
            load_1 = stack_for(both(cross[2]), (low(near[2]), low(cross[2])))
            load_1, kept = lax.optimization_barrier((load_1, kept))
    loads = (
        load_1,
        stack_for((high(cross[1]), low(cross[3])), (high(near[2]), high(cross[2]))),
        stack_for((low(cross[1]), high(cross[3])), (high(near[1]), high(cross[1]))),
        stack_for(both(cross[0]), (low(near[3]), low(cross[3]))),
    )
    sum_1 = core_move(loads[0], (0, 1), (1, 0))
    sum_2 = core_move(loads[1], (0, 1), (3, 0))
    sum_3 = core_move(loads[2], (0, 1), (1, 0))
    sum_4 = core_move(loads[3], (0, 1), (3, 0))
    over_2 = [add_bf16(low(near[2]), sum_1[0]), add_bf16(high(near[2]), sum_1[1])]
    over_1 = [None, add_bf16(high(near[1]), sum_2[0])]
    over_3 = [add_bf16(low(near[3]), sum_2[1]), None]
    down = [add_bf16(high(near[3]), sum_2[0]), add_bf16(high(cross[3]), sum_2[1])]
    up = [add_bf16(low(near[1]), sum_1[0]), add_bf16(low(cross[1]), sum_1[1])]
    load_5 = stack_for((over_2[0], over_1[1]), down)
    load_6 = stack_for((over_2[1], over_3[0]), up)
    sum_3, sum_4, _, _ = lax.optimization_barrier((sum_3, sum_4, load_5, load_6))
    context_heads, attn_prob, prob_b = attention_forward(all_kv)
    context = context_heads.reshape(tokens, heads_here * HD)
    sum_4, context = lax.optimization_barrier((sum_4, context))
    part_context = double_ctx(context, 2)
    sum_5 = core_move(load_5, (1, 0), (3, 0))
    sum_6 = core_move(load_6, (3, 0), (1, 0))
    over_1[0] = add_bf16(low(near[1]), sum_3[0])
    over_3[1] = add_bf16(high(near[3]), sum_3[1])
    z_near = [add_bf16(low(near[0]), sum_4[0], sum_6[0]), add_bf16(high(near[0]), sum_3[0], sum_5[0])]
    z_cross = [
        add_bf16(low(cross[0]), sum_4[1], sum_6[1]),
        add_bf16(high(cross[0]), sum_3[1], sum_5[1]),
    ]
    sum_7 = core_move(jnp.where(first_core, add_bf16(over_1[0], sum_5[0]), z_cross[0]), (1, 0), (0, 1))
    sum_8 = core_move(jnp.where(first_core, add_bf16(over_3[1], sum_6[0]), z_cross[1]), (3, 0), (0, 1))
    zero_low = add_bf16(low(near[0]), sum_4[0], sum_6[1], sum_7)
    zero_high = add_bf16(high(near[0]), sum_4[1], sum_5[1], sum_8)
    one_low, one_high = add_bf16(z_near[0], sum_7), add_bf16(z_near[1], sum_8)
    total = jnp.concatenate(
        [jnp.where(first_core, zero_low, one_low), jnp.where(first_core, zero_high, one_high)], axis=0
    )
    left, right = total[:features], total[features:]
    came = tp_move(jnp.where(first_core, right, left), dc=1)
    own_slice = in_core_order(jnp.where(first_core, left, right), came, 1).T

    returned = lax.all_to_all(
        own_slice.reshape(ctx_count, capacity, features), "ctx", split_axis=0, concat_axis=0, tiled=True
    ).reshape(slot_rows, features)
    part_context = double_ctx(part_context, 0)
    returned, part_context = lax.optimization_barrier((returned, part_context))
    all_context = double_ctx(part_context, 1).reshape(-1, heads_here * HD)
    moe_part = lax.dot_general(
        combine,
        returned.astype(F32),
        (((0,), (0,)), ((), ())),
        precision=lax.Precision.HIGHEST,
        preferred_element_type=F32,
    )
    grad_hidden = (grad_output.astype(F32) + moe_part).astype(BF16)

    one_half, other_half = grad_hidden[: tokens // 2], grad_hidden[tokens // 2 :]
    low_pair = jnp.stack([one_half, tp_move(one_half, dx=1)])
    high_z = jnp.stack([other_half] + [tp_move(other_half, dz=dz) for dz in (1, 2, 3)])
    low_all = jnp.stack([low_pair] + [tp_move(low_pair, dz=dz) for dz in (1, 2, 3)])
    high_all = jnp.stack([high_z, tp_move(high_z, dx=1)], axis=1)
    same_core = jnp.concatenate([low_all, high_all], axis=2)
    swapped = jnp.where(my_x == 0, same_core, same_core[:, ::-1])
    ordered = jnp.stack([swapped[0], swapped[3], swapped[2], swapped[1]])
    ids = jnp.stack([(my_z + i) % Z * 4 + x * 2 for x in (0, 1) for i in range(Z)])
    grad_context = context_grad(
        ids + my_core, ordered, out_proj, jnp.zeros((tokens, features), F32), F32
    )
    grad_context = context_grad(
        ids + 1 - my_core, tp_move(ordered, dc=1), out_proj, grad_context, BF16
    )

    grad_context, all_context = lax.optimization_barrier((grad_context, all_context))

    by_owner = rolled(ordered, my_z, 0)
    column_own = lax.all_to_all(
        by_owner.reshape(ctx_count, tokens, features), "ctx", split_axis=0, concat_axis=0, tiled=True
    ).reshape(seq_len, features)

    key_rows, value_rows = all_kv[:, :HD], all_kv[:, HD:]
    grad_heads = grad_context.reshape(tokens, heads_here, HD)
    grad_prob = jnp.einsum("qhd,kd->hqk", grad_heads, value_rows, preferred_element_type=F32)
    row_delta = jnp.sum(grad_heads.astype(F32) * context_heads.astype(F32), axis=2)
    grad_score = (attn_prob * (grad_prob - row_delta.T[:, :, None])).astype(BF16)
    grad_query = (
        jnp.einsum("hqk,kd->qhd", grad_score, key_rows, preferred_element_type=F32) * inv_root
    ).astype(BF16)
    grad_query = grad_query.reshape(tokens, heads_here * HD)
    key_term = (
        jnp.einsum("hqk,qhd->kd", grad_score, query_heads, preferred_element_type=F32) * inv_root
    )
    value_term = jnp.einsum("hqk,qhd->kd", prob_b, grad_heads, preferred_element_type=F32)
    kept_term = jnp.where(my_core == 0, key_term, value_term)
    sent_term = jnp.where(my_core == 0, value_term, key_term).astype(BF16)
    pair_term = (kept_term + tp_move(sent_term, dc=1).astype(F32)).astype(BF16)
    pair_term, column_own = lax.optimization_barrier((pair_term, column_own))
    column_other = tp_move(column_own, dc=1)
    kv_blocks = lax.all_to_all(
        pair_term.reshape(ctx_count, tokens, HD), "ctx", split_axis=0, concat_axis=0, tiled=True
    )

    def over_tokens(left):
        return lax.dot_general(
            left, all_context, (((0,), (0,)), ((), ())), preferred_element_type=F32
        ).astype(BF16)

    grad_out_proj_t = in_core_order(over_tokens(column_own), over_tokens(column_other), 0)
    kv_blocks, grad_out_proj_t = lax.optimization_barrier((kv_blocks, grad_out_proj_t))
    grad_kv = jnp.sum(kv_blocks.astype(F32), axis=0).astype(BF16)
    return (grad_hidden, grad_query, grad_kv, grad_out_proj_t)


def solution(mesh):
    in_specs = (
        P("ctx", "tp"),
        P("ctx", "tp"),
        P("ctx", None),
        P("ctx", None),
        P("ctx", None, "tp"),
        P("ctx", None, "tp"),
        P("ctx", "tp", None),
        P("ctx", "tp"),
        P("ctx", None),
        P("tp", None),
    )
    out_specs = (P("ctx", "tp"), P("ctx", "tp"), P("ctx", "tp"), P("ctx", "tp"))
    return jax.shard_map(
        per_device, mesh=mesh, in_specs=in_specs, out_specs=out_specs, check_vma=False
    )
```

```python
import math

import jax
import jax.numpy as jnp
from jax import lax
from jax.experimental import pallas as pl
from jax.experimental.pallas import tpu as pltpu
from jax.sharding import PartitionSpec as P

HQ = 48
KVH = 8
HD = 128
Z = 4
BF16 = jnp.bfloat16
F32 = jnp.float32


def tp_move(block, dz=0, dx=0, dc=0):
    route = []
    for src in range(Z * 4):
        z, low = src // 4, src % 4
        route.append((src, ((z + dz) % Z) * 4 + (low ^ (dx * 2 + dc))))
    return lax.ppermute(block, "tp", route)


def core_move(block, zero, one):
    route = []
    for src in range(Z * 4):
        z, low = src // 4, src % 4
        dz, dx = (zero, one)[src % 2]
        route.append((src, ((z + dz) % Z) * 4 + (low ^ (dx * 2))))
    return lax.ppermute(block, "tp", route)


def double_ctx(held, bit):
    route = [(c, c ^ (1 << bit)) for c in range(lax.axis_size("ctx"))]
    came = lax.ppermute(held, "ctx", route)
    upper = (lax.axis_index("ctx") >> bit) & 1 == 1
    axis = 0 if bit == 2 else 1
    return jnp.stack([jnp.where(upper, came, held), jnp.where(upper, held, came)], axis=axis)


def rolled(blocks, shift, axis):
    blocks = jnp.where(shift % 2 == 1, jnp.roll(blocks, 1, axis=axis), blocks)
    return jnp.where(shift >= 2, jnp.roll(blocks, 2, axis=axis), blocks)


def route_tables(expert_ids, route_weights, groups, capacity):
    tokens = expert_ids.shape[0]
    flat_ids = expert_ids.reshape(-1)
    numbers = jnp.arange(groups, dtype=jnp.int32)
    hits = (flat_ids[:, None] == numbers[None, :]).astype(jnp.int32)
    earlier = jnp.cumsum(hits, axis=0) - hits
    slot_rank = jnp.sum(earlier * hits, axis=1)
    targets = (flat_ids * capacity + slot_rank).reshape(tokens, 2)
    slot_index = jnp.arange(groups * capacity, dtype=jnp.int32)[:, None]
    first_hit = slot_index == targets[None, :, 0]
    second_hit = slot_index == targets[None, :, 1]
    placing = (first_hit | second_hit).astype(BF16)
    combine = jnp.where(first_hit, route_weights[None, :, 0], 0.0) + jnp.where(
        second_hit, route_weights[None, :, 1], 0.0
    )
    return (placing, combine)


def swiglu_grads(gate_act, up_act, hidden_grad):
    sigmoid_g = jax.nn.sigmoid(gate_act)
    grad_gate = (hidden_grad * up_act * sigmoid_g * (1.0 + gate_act * (1.0 - sigmoid_g))).astype(
        BF16
    )
    grad_up = (hidden_grad * gate_act * sigmoid_g).astype(BF16)
    return (grad_gate, grad_up)


def contract_last(left, right):
    return lax.dot_general(left, right, (((1,), (1,)), ((), ())), preferred_element_type=F32)


def add_bf16(*terms):
    total = terms[0].astype(F32)
    for term in terms[1:]:
        total = total + term.astype(F32)
    return total.astype(BF16)


def context_kernel(ids_ref, pieces_ref, first_ref, second_ref, before_ref, out_ref, total):
    step = pl.program_id(0)

    @pl.when(step == 0)
    def _():
        total[...] = before_ref[...]

    total[...] += contract_last(pieces_ref[0, 0], first_ref[...]) + contract_last(
        pieces_ref[0, 1], second_ref[...]
    )

    @pl.when(step == pl.num_programs(0) - 1)
    def _():
        out_ref[...] = total[...].astype(out_ref.dtype)


def context_grad(ids, pieces, weight, before, dtype):
    count, _, rows, width = pieces.shape
    outs = weight.shape[0]
    whole = pl.BlockSpec((rows, outs), lambda i, ids: (0, 0))
    return pl.pallas_call(
        context_kernel,
        grid_spec=pltpu.PrefetchScalarGridSpec(
            num_scalar_prefetch=1,
            grid=(count,),
            in_specs=[
                pl.BlockSpec((1, 2, rows, width), lambda i, ids: (i, 0, 0, 0)),
                pl.BlockSpec((outs, width), lambda i, ids: (0, ids[i])),
                pl.BlockSpec((outs, width), lambda i, ids: (0, ids[i + count])),
                whole,
            ],
            out_specs=whole,
            scratch_shapes=[pltpu.VMEM((rows, outs), F32)],
        ),
        out_shape=jax.ShapeDtypeStruct((rows, outs), dtype),
        compiler_params=pltpu.CompilerParams(vmem_limit_bytes=8 * 2**20),
        cost_estimate=pl.CostEstimate(
            flops=4 * count * rows * width * outs,
            bytes_accessed=4 * count * width * (outs + rows),
            transcendentals=0,
        ),
    )(ids, pieces, weight, weight, before)


def per_device(
    moe_input,
    grad_output,
    expert_ids,
    route_weights,
    w_gate,
    w_up,
    w_down,
    queries,
    keys_values,
    out_proj,
):
    ctx_count = lax.axis_size("ctx")
    tp_rank = lax.axis_index("tp")
    ctx_rank = lax.axis_index("ctx")
    my_z, my_x, my_core = tp_rank // 4, (tp_rank // 2) % 2, tp_rank % 2
    tokens, features = moe_input.shape
    capacity = tokens // 2
    slot_rows = ctx_count * capacity
    gate_w, up_w, down_w = w_gate[0], w_up[0], w_down[0]

    def chunk_of(dz, dx, dc):
        return ((my_z + dz) % Z) * 4 + (my_x ^ dx) * 2 + (my_core ^ dc)

    placing, combine = route_tables(expert_ids, route_weights, ctx_count, capacity)
    first_core = my_core == 0

    def in_core_order(own, other, axis):
        return jnp.concatenate(
            [jnp.where(first_core, own, other), jnp.where(first_core, other, own)], axis=axis
        )

    came = tp_move(jnp.where(first_core, moe_input, grad_output), dc=1)
    carried = in_core_order(jnp.where(first_core, grad_output, moe_input), came, 1)
    send = jnp.dot(placing, carried, preferred_element_type=F32).astype(BF16)
    got = lax.all_to_all(
        send.reshape(ctx_count, capacity, 2 * features), "ctx", split_axis=0, concat_axis=0, tiled=True
    ).reshape(slot_rows, 2 * features)

    heads_here = queries.shape[1] // HD
    group_size = HQ // KVH
    kv_group = tp_rank * heads_here // group_size
    mine_kv = lax.dynamic_slice_in_dim(keys_values, kv_group * 2 * HD, 2 * HD, 1)
    part_kv, got = lax.optimization_barrier((double_ctx(mine_kv, 2), got))
    all_kv = double_ctx(double_ctx(part_kv, 0), 1).reshape(-1, 2 * HD)
    seq_len = ctx_count * tokens
    query_heads = queries.reshape(tokens, heads_here, HD)
    inv_root = 1.0 / math.sqrt(HD)

    def attention_forward(all_kv):
        key_rows, value_rows = all_kv[:, :HD], all_kv[:, HD:]
        query_pos = ctx_rank * tokens + jnp.arange(tokens, dtype=jnp.int32)
        causal = query_pos[:, None] >= jnp.arange(seq_len, dtype=jnp.int32)[None, :]
        scores = (
            jnp.einsum("qhd,kd->hqk", query_heads, key_rows, preferred_element_type=F32) * inv_root
        )
        scores = jnp.where(causal[None], scores, -1e30)
        row_max = jnp.max(scores, axis=2, keepdims=True)
        exp_scores = jnp.exp(scores - row_max)
        attn_prob = exp_scores / jnp.sum(exp_scores, axis=2, keepdims=True)
        prob_b = attn_prob.astype(BF16)
        context_heads = jnp.einsum(
            "hqk,kd->qhd", prob_b, value_rows, preferred_element_type=F32
        ).astype(BF16)
        return context_heads, attn_prob, prob_b

    half, width = slot_rows // 2, 2 * features
    hop_1 = core_move(got, (1, 0), (0, 1))
    hop_2 = core_move(got, (3, 0), (1, 0))
    hop_3 = core_move(got, (0, 1), (3, 0))
    hop_3, all_kv = lax.optimization_barrier((hop_3, all_kv))
    far_low = core_move(jnp.where(first_core, hop_1[:half], hop_2[:half]), (1, 0), (1, 0))
    far_high = core_move(jnp.where(first_core, hop_2[half:], hop_3[half:]), (3, 0), (3, 0))
    hop_6 = core_move(hop_1, (0, 1), (1, 0))
    hop_7 = core_move(jnp.where(first_core, hop_2, hop_1), (0, 1), (3, 0))
    far = jnp.concatenate([far_low, far_high], axis=0)
    cross_low = core_move(jnp.where(first_core, far_low, hop_6[:half]), (0, 1), (1, 0))
    cross_high = core_move(jnp.where(first_core, far_high, hop_7[half:]), (0, 1), (3, 0))
    far_cross = jnp.concatenate([cross_low, cross_high], axis=0)

    arrivals = (
        (got, (0, 0), (0, 0)),
        (hop_1, (3, 0), (0, 1)),
        (hop_2, (1, 0), (3, 0)),
        (hop_3, (0, 1), (1, 0)),
        (far, (2, 0), (2, 0)),
        (hop_6, (3, 1), (3, 1)),
        (hop_7, (1, 1), (1, 1)),
        (far_cross, (2, 1), (2, 1)),
    )
    gate_act = up_act = hidden_grad = 0.0
    for block, dy_from, x_from in arrivals:
        crossed = tp_move(block, dc=1)
        x_rows = jnp.where(first_core, crossed, block)
        dy_rows = jnp.where(first_core, block, crossed)
        x_start = (chunk_of(*x_from, 0) // 2) * width
        dy_start = (chunk_of(*dy_from, 0) // 2) * width
        gate_rows = lax.dynamic_slice_in_dim(gate_w, x_start, width, 0)
        up_rows = lax.dynamic_slice_in_dim(up_w, x_start, width, 0)
        down_cols = lax.dynamic_slice_in_dim(down_w, dy_start, width, 1)
        gate_act = gate_act + jnp.dot(x_rows, gate_rows, preferred_element_type=F32)
        up_act = up_act + jnp.dot(x_rows, up_rows, preferred_element_type=F32)
        hidden_grad = hidden_grad + contract_last(dy_rows, down_cols)
    grad_gate, grad_up = swiglu_grads(gate_act, up_act, hidden_grad)

    def routed(core_0, core_1):
        gate_half = jnp.where(first_core, grad_gate[core_0], grad_gate[core_1])
        up_half = jnp.where(first_core, grad_up[core_0], grad_up[core_1])
        gate_part = contract_last(gate_w, gate_half).astype(BF16)
        return gate_part.astype(F32) + contract_last(up_w, up_half)

    lower, upper = slice(None, half), slice(half, None)
    sent = routed(upper, lower).astype(BF16)
    arrived = tp_move(sent, dc=1)
    grad_gate, sent = lax.optimization_barrier((grad_gate, sent))
    own = add_bf16(routed(lower, upper), arrived)

    cut = features

    def stack_for(zero, one):
        return jnp.where(first_core, jnp.stack(zero), jnp.stack(one))

    def low(rows):
        return rows[:cut]

    def high(rows):
        return rows[cut:]

    def both(rows):
        return (low(rows), high(rows))

    def chip_rows(dz, dx):
        return lax.dynamic_slice_in_dim(own, (chunk_of(dz, dx, 0) // 2) * width, width, 0)

    near = {dz: chip_rows(dz, 0) for dz in range(Z)}
    cross = {dz: chip_rows(dz, 1) for dz in range(Z)}
    loads = (
        stack_for(both(cross[2]), (low(near[2]), low(cross[2]))),
        stack_for((high(cross[1]), low(cross[3])), (high(near[2]), high(cross[2]))),
        stack_for((low(cross[1]), high(cross[3])), (high(near[1]), high(cross[1]))),
        stack_for(both(cross[0]), (low(near[3]), low(cross[3]))),
    )
    sum_1 = core_move(loads[0], (0, 1), (1, 0))
    sum_2 = core_move(loads[1], (0, 1), (3, 0))
    sum_3 = core_move(loads[2], (0, 1), (1, 0))
    sum_4 = core_move(loads[3], (0, 1), (3, 0))
    over_2 = [add_bf16(low(near[2]), sum_1[0]), add_bf16(high(near[2]), sum_1[1])]
    over_1 = [None, add_bf16(high(near[1]), sum_2[0])]
    over_3 = [add_bf16(low(near[3]), sum_2[1]), None]
    down = [add_bf16(high(near[3]), sum_2[0]), add_bf16(high(cross[3]), sum_2[1])]
    up = [add_bf16(low(near[1]), sum_1[0]), add_bf16(low(cross[1]), sum_1[1])]
    load_5 = stack_for((over_2[0], over_1[1]), down)
    load_6 = stack_for((over_2[1], over_3[0]), up)
    sum_3, sum_4, _, _ = lax.optimization_barrier((sum_3, sum_4, load_5, load_6))
    all_kv, _ = lax.optimization_barrier((all_kv, load_5))
    context_heads, attn_prob, prob_b = attention_forward(all_kv)
    context = context_heads.reshape(tokens, heads_here * HD)
    sum_4, context = lax.optimization_barrier((sum_4, context))
    part_context = double_ctx(context, 2)
    sum_5 = core_move(load_5, (1, 0), (3, 0))
    sum_6 = core_move(load_6, (3, 0), (1, 0))
    over_1[0] = add_bf16(low(near[1]), sum_3[0])
    over_3[1] = add_bf16(high(near[3]), sum_3[1])
    z_near = [add_bf16(low(near[0]), sum_4[0], sum_6[0]), add_bf16(high(near[0]), sum_3[0], sum_5[0])]
    z_cross = [
        add_bf16(low(cross[0]), sum_4[1], sum_6[1]),
        add_bf16(high(cross[0]), sum_3[1], sum_5[1]),
    ]
    sum_7 = core_move(jnp.where(first_core, add_bf16(over_1[0], sum_5[0]), z_cross[0]), (1, 0), (0, 1))
    sum_8 = core_move(jnp.where(first_core, add_bf16(over_3[1], sum_6[0]), z_cross[1]), (3, 0), (0, 1))
    zero_low = add_bf16(low(near[0]), sum_4[0], sum_6[1], sum_7)
    zero_high = add_bf16(high(near[0]), sum_4[1], sum_5[1], sum_8)
    one_low, one_high = add_bf16(z_near[0], sum_7), add_bf16(z_near[1], sum_8)
    total = jnp.concatenate(
        [jnp.where(first_core, zero_low, one_low), jnp.where(first_core, zero_high, one_high)], axis=0
    )
    left, right = total[:features], total[features:]
    came = tp_move(jnp.where(first_core, right, left), dc=1)
    own_slice = in_core_order(jnp.where(first_core, left, right), came, 1).T

    returned = lax.all_to_all(
        own_slice.reshape(ctx_count, capacity, features), "ctx", split_axis=0, concat_axis=0, tiled=True
    ).reshape(slot_rows, features)
    part_context = double_ctx(part_context, 0)
    returned, part_context = lax.optimization_barrier((returned, part_context))
    all_context = double_ctx(part_context, 1).reshape(-1, heads_here * HD)
    moe_part = lax.dot_general(
        combine,
        returned.astype(F32),
        (((0,), (0,)), ((), ())),
        precision=lax.Precision.HIGHEST,
        preferred_element_type=F32,
    )
    grad_hidden = (grad_output.astype(F32) + moe_part).astype(BF16)

    one_half, other_half = grad_hidden[: tokens // 2], grad_hidden[tokens // 2 :]
    low_pair = jnp.stack([one_half, tp_move(one_half, dx=1)])
    high_z = jnp.stack([other_half] + [tp_move(other_half, dz=dz) for dz in (1, 2, 3)])
    low_all = jnp.stack([low_pair] + [tp_move(low_pair, dz=dz) for dz in (1, 2, 3)])
    high_all = jnp.stack([high_z, tp_move(high_z, dx=1)], axis=1)
    same_core = jnp.concatenate([low_all, high_all], axis=2)
    swapped = jnp.where(my_x == 0, same_core, same_core[:, ::-1])
    ordered = jnp.stack([swapped[0], swapped[3], swapped[2], swapped[1]])
    ids = jnp.stack([(my_z + i) % Z * 4 + x * 2 for x in (0, 1) for i in range(Z)])
    grad_context = context_grad(
        ids + my_core, ordered, out_proj, jnp.zeros((tokens, features), F32), F32
    )
    grad_context = context_grad(
        ids + 1 - my_core, tp_move(ordered, dc=1), out_proj, grad_context, BF16
    )


    by_owner = rolled(ordered, my_z, 0)
    column_own = lax.all_to_all(
        by_owner.reshape(ctx_count, tokens, features), "ctx", split_axis=0, concat_axis=0, tiled=True
    ).reshape(seq_len, features)

    key_rows, value_rows = all_kv[:, :HD], all_kv[:, HD:]
    grad_heads = grad_context.reshape(tokens, heads_here, HD)
    grad_prob = jnp.einsum("qhd,kd->hqk", grad_heads, value_rows, preferred_element_type=F32)
    row_delta = jnp.sum(grad_heads.astype(F32) * context_heads.astype(F32), axis=2)
    grad_score = (attn_prob * (grad_prob - row_delta.T[:, :, None])).astype(BF16)
    grad_query = (
        jnp.einsum("hqk,kd->qhd", grad_score, key_rows, preferred_element_type=F32) * inv_root
    ).astype(BF16)
    grad_query = grad_query.reshape(tokens, heads_here * HD)
    key_term = (
        jnp.einsum("hqk,qhd->kd", grad_score, query_heads, preferred_element_type=F32) * inv_root
    )
    value_term = jnp.einsum("hqk,qhd->kd", prob_b, grad_heads, preferred_element_type=F32)
    kept_term = jnp.where(my_core == 0, key_term, value_term)
    sent_term = jnp.where(my_core == 0, value_term, key_term).astype(BF16)
    pair_term = (kept_term + tp_move(sent_term, dc=1).astype(F32)).astype(BF16)
    pair_term, column_own = lax.optimization_barrier((pair_term, column_own))
    column_other = tp_move(column_own, dc=1)
    kv_blocks = lax.all_to_all(
        pair_term.reshape(ctx_count, tokens, HD), "ctx", split_axis=0, concat_axis=0, tiled=True
    )

    def over_tokens(left):
        return lax.dot_general(
            left, all_context, (((0,), (0,)), ((), ())), preferred_element_type=F32
        ).astype(BF16)

    grad_out_proj_t = in_core_order(over_tokens(column_own), over_tokens(column_other), 0)
    kv_blocks, grad_out_proj_t = lax.optimization_barrier((kv_blocks, grad_out_proj_t))
    grad_kv = jnp.sum(kv_blocks.astype(F32), axis=0).astype(BF16)
    return (grad_hidden, grad_query, grad_kv, grad_out_proj_t)


def solution(mesh):
    in_specs = (
        P("ctx", "tp"),
        P("ctx", "tp"),
        P("ctx", None),
        P("ctx", None),
        P("ctx", None, "tp"),
        P("ctx", None, "tp"),
        P("ctx", "tp", None),
        P("ctx", "tp"),
        P("ctx", None),
        P("tp", None),
    )
    out_specs = (P("ctx", "tp"), P("ctx", "tp"), P("ctx", "tp"), P("ctx", "tp"))
    return jax.shard_map(
        per_device, mesh=mesh, in_specs=in_specs, out_specs=out_specs, check_vma=False
    )
```

```python
import math

import jax
import jax.numpy as jnp
from jax import lax
from jax.experimental import pallas as pl
from jax.experimental.pallas import tpu as pltpu
from jax.sharding import PartitionSpec as P

HQ = 48
KVH = 8
HD = 128
Z = 4
BF16 = jnp.bfloat16
F32 = jnp.float32


def tp_move(block, dz=0, dx=0, dc=0):
    route = []
    for src in range(Z * 4):
        z, low = src // 4, src % 4
        route.append((src, ((z + dz) % Z) * 4 + (low ^ (dx * 2 + dc))))
    return lax.ppermute(block, "tp", route)


def core_move(block, zero, one):
    route = []
    for src in range(Z * 4):
        z, low = src // 4, src % 4
        dz, dx = (zero, one)[src % 2]
        route.append((src, ((z + dz) % Z) * 4 + (low ^ (dx * 2))))
    return lax.ppermute(block, "tp", route)


def from_bit(held, bit):
    return lax.ppermute(
        held, "ctx", [(c, c ^ (1 << bit)) for c in range(lax.axis_size("ctx"))]
    )


def in_bit_order(held, came, bit):
    upper = (lax.axis_index("ctx") >> bit) & 1 == 1
    axis = 0 if bit == 2 else 1
    return jnp.stack([jnp.where(upper, came, held), jnp.where(upper, held, came)], axis=axis)


def double_ctx(held, bit):
    return in_bit_order(held, from_bit(held, bit), bit)


def rolled(blocks, shift, axis):
    blocks = jnp.where(shift % 2 == 1, jnp.roll(blocks, 1, axis=axis), blocks)
    return jnp.where(shift >= 2, jnp.roll(blocks, 2, axis=axis), blocks)


def route_tables(expert_ids, route_weights, groups, capacity):
    tokens = expert_ids.shape[0]
    flat_ids = expert_ids.reshape(-1)
    numbers = jnp.arange(groups, dtype=jnp.int32)
    hits = (flat_ids[:, None] == numbers[None, :]).astype(jnp.int32)
    earlier = jnp.cumsum(hits, axis=0) - hits
    slot_rank = jnp.sum(earlier * hits, axis=1)
    targets = (flat_ids * capacity + slot_rank).reshape(tokens, 2)
    slot_index = jnp.arange(groups * capacity, dtype=jnp.int32)[:, None]
    first_hit = slot_index == targets[None, :, 0]
    second_hit = slot_index == targets[None, :, 1]
    placing = (first_hit | second_hit).astype(BF16)
    combine = jnp.where(first_hit, route_weights[None, :, 0], 0.0) + jnp.where(
        second_hit, route_weights[None, :, 1], 0.0
    )
    return (placing, combine)


def swiglu_grads(gate_act, up_act, hidden_grad):
    sigmoid_g = jax.nn.sigmoid(gate_act)
    grad_gate = (hidden_grad * up_act * sigmoid_g * (1.0 + gate_act * (1.0 - sigmoid_g))).astype(
        BF16
    )
    grad_up = (hidden_grad * gate_act * sigmoid_g).astype(BF16)
    return (grad_gate, grad_up)


def contract_last(left, right):
    return lax.dot_general(left, right, (((1,), (1,)), ((), ())), preferred_element_type=F32)


def add_bf16(*terms):
    total = terms[0].astype(F32)
    for term in terms[1:]:
        total = total + term.astype(F32)
    return total.astype(BF16)


def context_kernel(ids_ref, pieces_ref, first_ref, second_ref, before_ref, out_ref, total):
    step = pl.program_id(0)

    @pl.when(step == 0)
    def _():
        total[...] = before_ref[...]

    total[...] += contract_last(pieces_ref[0, 0], first_ref[...]) + contract_last(
        pieces_ref[0, 1], second_ref[...]
    )

    @pl.when(step == pl.num_programs(0) - 1)
    def _():
        out_ref[...] = total[...].astype(out_ref.dtype)


def context_grad(ids, pieces, weight, before, dtype):
    count, _, rows, width = pieces.shape
    outs = weight.shape[0]
    whole = pl.BlockSpec((rows, outs), lambda i, ids: (0, 0))
    return pl.pallas_call(
        context_kernel,
        grid_spec=pltpu.PrefetchScalarGridSpec(
            num_scalar_prefetch=1,
            grid=(count,),
            in_specs=[
                pl.BlockSpec((1, 2, rows, width), lambda i, ids: (i, 0, 0, 0)),
                pl.BlockSpec((outs, width), lambda i, ids: (0, ids[i])),
                pl.BlockSpec((outs, width), lambda i, ids: (0, ids[i + count])),
                whole,
            ],
            out_specs=whole,
            scratch_shapes=[pltpu.VMEM((rows, outs), F32)],
        ),
        out_shape=jax.ShapeDtypeStruct((rows, outs), dtype),
        compiler_params=pltpu.CompilerParams(vmem_limit_bytes=8 * 2**20),
        cost_estimate=pl.CostEstimate(
            flops=4 * count * rows * width * outs,
            bytes_accessed=4 * count * width * (outs + rows),
            transcendentals=0,
        ),
    )(ids, pieces, weight, weight, before)


def per_device(
    moe_input,
    grad_output,
    expert_ids,
    route_weights,
    w_gate,
    w_up,
    w_down,
    queries,
    keys_values,
    out_proj,
):
    ctx_count = lax.axis_size("ctx")
    tp_rank = lax.axis_index("tp")
    ctx_rank = lax.axis_index("ctx")
    my_z, my_x, my_core = tp_rank // 4, (tp_rank // 2) % 2, tp_rank % 2
    tokens, features = moe_input.shape
    capacity = tokens // 2
    slot_rows = ctx_count * capacity
    gate_w, up_w, down_w = w_gate[0], w_up[0], w_down[0]

    def chunk_of(dz, dx, dc):
        return ((my_z + dz) % Z) * 4 + (my_x ^ dx) * 2 + (my_core ^ dc)

    placing, combine = route_tables(expert_ids, route_weights, ctx_count, capacity)
    first_core = my_core == 0

    def in_core_order(own, other, axis):
        return jnp.concatenate(
            [jnp.where(first_core, own, other), jnp.where(first_core, other, own)], axis=axis
        )

    came = tp_move(jnp.where(first_core, moe_input, grad_output), dc=1)
    carried = in_core_order(jnp.where(first_core, grad_output, moe_input), came, 1)
    send = jnp.dot(placing, carried, preferred_element_type=F32).astype(BF16)
    got = lax.all_to_all(
        send.reshape(ctx_count, capacity, 2 * features), "ctx", split_axis=0, concat_axis=0, tiled=True
    ).reshape(slot_rows, 2 * features)

    heads_here = queries.shape[1] // HD
    group_size = HQ // KVH
    kv_group = tp_rank * heads_here // group_size
    mine_kv = lax.dynamic_slice_in_dim(keys_values, kv_group * 2 * HD, 2 * HD, 1)
    part_kv, got = lax.optimization_barrier((double_ctx(mine_kv, 2), got))
    all_kv = double_ctx(double_ctx(part_kv, 0), 1).reshape(-1, 2 * HD)
    seq_len = ctx_count * tokens
    query_heads = queries.reshape(tokens, heads_here, HD)
    inv_root = 1.0 / math.sqrt(HD)

    def attention_forward(all_kv):
        key_rows, value_rows = all_kv[:, :HD], all_kv[:, HD:]
        query_pos = ctx_rank * tokens + jnp.arange(tokens, dtype=jnp.int32)
        causal = query_pos[:, None] >= jnp.arange(seq_len, dtype=jnp.int32)[None, :]
        scores = (
            jnp.einsum("qhd,kd->hqk", query_heads, key_rows, preferred_element_type=F32) * inv_root
        )
        scores = jnp.where(causal[None], scores, -1e30)
        row_max = jnp.max(scores, axis=2, keepdims=True)
        exp_scores = jnp.exp(scores - row_max)
        attn_prob = exp_scores / jnp.sum(exp_scores, axis=2, keepdims=True)
        prob_b = attn_prob.astype(BF16)
        context_heads = jnp.einsum(
            "hqk,kd->qhd", prob_b, value_rows, preferred_element_type=F32
        ).astype(BF16)
        return context_heads, attn_prob, prob_b

    half, width = slot_rows // 2, 2 * features
    hop_1 = core_move(got, (1, 0), (0, 1))
    hop_2 = core_move(got, (3, 0), (1, 0))
    hop_3 = core_move(got, (0, 1), (3, 0))
    hop_3, all_kv = lax.optimization_barrier((hop_3, all_kv))
    far_low = core_move(jnp.where(first_core, hop_1[:half], hop_2[:half]), (1, 0), (1, 0))
    far_high = core_move(jnp.where(first_core, hop_2[half:], hop_3[half:]), (3, 0), (3, 0))
    hop_6 = core_move(hop_1, (0, 1), (1, 0))
    hop_7 = core_move(jnp.where(first_core, hop_2, hop_1), (0, 1), (3, 0))
    far = jnp.concatenate([far_low, far_high], axis=0)
    cross_low = core_move(jnp.where(first_core, far_low, hop_6[:half]), (0, 1), (1, 0))
    cross_high = core_move(jnp.where(first_core, far_high, hop_7[half:]), (0, 1), (3, 0))
    far_cross = jnp.concatenate([cross_low, cross_high], axis=0)

    arrivals = (
        (got, (0, 0), (0, 0)),
        (hop_1, (3, 0), (0, 1)),
        (hop_2, (1, 0), (3, 0)),
        (hop_3, (0, 1), (1, 0)),
        (far, (2, 0), (2, 0)),
        (hop_6, (3, 1), (3, 1)),
        (hop_7, (1, 1), (1, 1)),
        (far_cross, (2, 1), (2, 1)),
    )
    gate_act = up_act = hidden_grad = 0.0
    for block, dy_from, x_from in arrivals:
        crossed = tp_move(block, dc=1)
        x_rows = jnp.where(first_core, crossed, block)
        dy_rows = jnp.where(first_core, block, crossed)
        x_start = (chunk_of(*x_from, 0) // 2) * width
        dy_start = (chunk_of(*dy_from, 0) // 2) * width
        gate_rows = lax.dynamic_slice_in_dim(gate_w, x_start, width, 0)
        up_rows = lax.dynamic_slice_in_dim(up_w, x_start, width, 0)
        down_cols = lax.dynamic_slice_in_dim(down_w, dy_start, width, 1)
        gate_act = gate_act + jnp.dot(x_rows, gate_rows, preferred_element_type=F32)
        up_act = up_act + jnp.dot(x_rows, up_rows, preferred_element_type=F32)
        hidden_grad = hidden_grad + contract_last(dy_rows, down_cols)
    grad_gate, grad_up = swiglu_grads(gate_act, up_act, hidden_grad)

    def routed(core_0, core_1):
        gate_half = jnp.where(first_core, grad_gate[core_0], grad_gate[core_1])
        up_half = jnp.where(first_core, grad_up[core_0], grad_up[core_1])
        gate_part = contract_last(gate_w, gate_half).astype(BF16)
        return gate_part.astype(F32) + contract_last(up_w, up_half)

    lower, upper = slice(None, half), slice(half, None)
    sent = routed(upper, lower).astype(BF16)
    arrived = tp_move(sent, dc=1)
    grad_gate, sent = lax.optimization_barrier((grad_gate, sent))
    own = add_bf16(routed(lower, upper), arrived)

    cut = features

    def stack_for(zero, one):
        return jnp.where(first_core, jnp.stack(zero), jnp.stack(one))

    def low(rows):
        return rows[:cut]

    def high(rows):
        return rows[cut:]

    def both(rows):
        return (low(rows), high(rows))

    def chip_rows(dz, dx):
        return lax.dynamic_slice_in_dim(own, (chunk_of(dz, dx, 0) // 2) * width, width, 0)

    near = {dz: chip_rows(dz, 0) for dz in range(Z)}
    cross = {dz: chip_rows(dz, 1) for dz in range(Z)}
    loads = (
        stack_for(both(cross[2]), (low(near[2]), low(cross[2]))),
        stack_for((high(cross[1]), low(cross[3])), (high(near[2]), high(cross[2]))),
        stack_for((low(cross[1]), high(cross[3])), (high(near[1]), high(cross[1]))),
        stack_for(both(cross[0]), (low(near[3]), low(cross[3]))),
    )
    sum_1 = core_move(loads[0], (0, 1), (1, 0))
    sum_2 = core_move(loads[1], (0, 1), (3, 0))
    sum_3 = core_move(loads[2], (0, 1), (1, 0))
    sum_4 = core_move(loads[3], (0, 1), (3, 0))
    over_2 = [add_bf16(low(near[2]), sum_1[0]), add_bf16(high(near[2]), sum_1[1])]
    over_1 = [None, add_bf16(high(near[1]), sum_2[0])]
    over_3 = [add_bf16(low(near[3]), sum_2[1]), None]
    down = [add_bf16(high(near[3]), sum_2[0]), add_bf16(high(cross[3]), sum_2[1])]
    up = [add_bf16(low(near[1]), sum_1[0]), add_bf16(low(cross[1]), sum_1[1])]
    load_5 = stack_for((over_2[0], over_1[1]), down)
    load_6 = stack_for((over_2[1], over_3[0]), up)
    sum_3, sum_4, _, _ = lax.optimization_barrier((sum_3, sum_4, load_5, load_6))
    context_heads, attn_prob, prob_b = attention_forward(all_kv)
    context = context_heads.reshape(tokens, heads_here * HD)
    sum_4, context = lax.optimization_barrier((sum_4, context))
    part_context = double_ctx(context, 2)
    sum_5 = core_move(load_5, (1, 0), (3, 0))
    sum_6 = core_move(load_6, (3, 0), (1, 0))
    over_1[0] = add_bf16(low(near[1]), sum_3[0])
    over_3[1] = add_bf16(high(near[3]), sum_3[1])
    z_near = [add_bf16(low(near[0]), sum_4[0], sum_6[0]), add_bf16(high(near[0]), sum_3[0], sum_5[0])]
    z_cross = [
        add_bf16(low(cross[0]), sum_4[1], sum_6[1]),
        add_bf16(high(cross[0]), sum_3[1], sum_5[1]),
    ]
    sum_7 = core_move(jnp.where(first_core, add_bf16(over_1[0], sum_5[0]), z_cross[0]), (1, 0), (0, 1))
    sum_8 = core_move(jnp.where(first_core, add_bf16(over_3[1], sum_6[0]), z_cross[1]), (3, 0), (0, 1))
    zero_low = add_bf16(low(near[0]), sum_4[0], sum_6[1], sum_7)
    zero_high = add_bf16(high(near[0]), sum_4[1], sum_5[1], sum_8)
    one_low, one_high = add_bf16(z_near[0], sum_7), add_bf16(z_near[1], sum_8)
    total = jnp.concatenate(
        [jnp.where(first_core, zero_low, one_low), jnp.where(first_core, zero_high, one_high)], axis=0
    )
    left, right = total[:features], total[features:]
    came = tp_move(jnp.where(first_core, right, left), dc=1)
    own_slice = in_core_order(jnp.where(first_core, left, right), came, 1).T

    returned = lax.all_to_all(
        own_slice.reshape(ctx_count, capacity, features), "ctx", split_axis=0, concat_axis=0, tiled=True
    ).reshape(slot_rows, features)
    part_context = double_ctx(part_context, 0)
    returned, part_context = lax.optimization_barrier((returned, part_context))
    moe_part = lax.dot_general(
        combine,
        returned.astype(F32),
        (((0,), (0,)), ((), ())),
        precision=lax.Precision.HIGHEST,
        preferred_element_type=F32,
    )
    grad_hidden = (grad_output.astype(F32) + moe_part).astype(BF16)

    one_half, other_half = grad_hidden[: tokens // 2], grad_hidden[tokens // 2 :]
    low_pair = jnp.stack([one_half, tp_move(one_half, dx=1)])
    high_z = jnp.stack([other_half] + [tp_move(other_half, dz=dz) for dz in (1, 2, 3)])
    low_all = jnp.stack([low_pair] + [tp_move(low_pair, dz=dz) for dz in (1, 2, 3)])
    high_all = jnp.stack([high_z, tp_move(high_z, dx=1)], axis=1)
    same_core = jnp.concatenate([low_all, high_all], axis=2)
    swapped = jnp.where(my_x == 0, same_core, same_core[:, ::-1])
    ordered = jnp.stack([swapped[0], swapped[3], swapped[2], swapped[1]])
    ids = jnp.stack([(my_z + i) % Z * 4 + x * 2 for x in (0, 1) for i in range(Z)])
    grad_context = context_grad(
        ids + my_core, ordered, out_proj, jnp.zeros((tokens, features), F32), F32
    )
    grad_context, last_context = lax.optimization_barrier(
        (grad_context, from_bit(part_context, 1))
    )
    grad_context = context_grad(
        ids + 1 - my_core, tp_move(ordered, dc=1), out_proj, grad_context, BF16
    )


    all_context = in_bit_order(part_context, last_context, 1).reshape(-1, heads_here * HD)

    by_owner = rolled(ordered, my_z, 0)
    column_own = lax.all_to_all(
        by_owner.reshape(ctx_count, tokens, features), "ctx", split_axis=0, concat_axis=0, tiled=True
    ).reshape(seq_len, features)

    key_rows, value_rows = all_kv[:, :HD], all_kv[:, HD:]
    grad_heads = grad_context.reshape(tokens, heads_here, HD)
    grad_prob = jnp.einsum("qhd,kd->hqk", grad_heads, value_rows, preferred_element_type=F32)
    row_delta = jnp.sum(grad_heads.astype(F32) * context_heads.astype(F32), axis=2)
    grad_score = (attn_prob * (grad_prob - row_delta.T[:, :, None])).astype(BF16)
    grad_query = (
        jnp.einsum("hqk,kd->qhd", grad_score, key_rows, preferred_element_type=F32) * inv_root
    ).astype(BF16)
    grad_query = grad_query.reshape(tokens, heads_here * HD)
    key_term = (
        jnp.einsum("hqk,qhd->kd", grad_score, query_heads, preferred_element_type=F32) * inv_root
    )
    value_term = jnp.einsum("hqk,qhd->kd", prob_b, grad_heads, preferred_element_type=F32)
    kept_term = jnp.where(my_core == 0, key_term, value_term)
    sent_term = jnp.where(my_core == 0, value_term, key_term).astype(BF16)
    pair_term = (kept_term + tp_move(sent_term, dc=1).astype(F32)).astype(BF16)
    pair_term, column_own = lax.optimization_barrier((pair_term, column_own))
    column_other = tp_move(column_own, dc=1)
    kv_blocks = lax.all_to_all(
        pair_term.reshape(ctx_count, tokens, HD), "ctx", split_axis=0, concat_axis=0, tiled=True
    )

    def over_tokens(left):
        return lax.dot_general(
            left, all_context, (((0,), (0,)), ((), ())), preferred_element_type=F32
        ).astype(BF16)

    grad_out_proj_t = in_core_order(over_tokens(column_own), over_tokens(column_other), 0)
    kv_blocks, grad_out_proj_t = lax.optimization_barrier((kv_blocks, grad_out_proj_t))
    grad_kv = jnp.sum(kv_blocks.astype(F32), axis=0).astype(BF16)
    return (grad_hidden, grad_query, grad_kv, grad_out_proj_t)


def solution(mesh):
    in_specs = (
        P("ctx", "tp"),
        P("ctx", "tp"),
        P("ctx", None),
        P("ctx", None),
        P("ctx", None, "tp"),
        P("ctx", None, "tp"),
        P("ctx", "tp", None),
        P("ctx", "tp"),
        P("ctx", None),
        P("tp", None),
    )
    out_specs = (P("ctx", "tp"), P("ctx", "tp"), P("ctx", "tp"), P("ctx", "tp"))
    return jax.shard_map(
        per_device, mesh=mesh, in_specs=in_specs, out_specs=out_specs, check_vma=False
    )
```

```python
import math

import jax
import jax.numpy as jnp
from jax import lax
from jax.experimental import pallas as pl
from jax.experimental.pallas import tpu as pltpu
from jax.sharding import PartitionSpec as P

HQ = 48
KVH = 8
HD = 128
Z = 4
BF16 = jnp.bfloat16
F32 = jnp.float32


def tp_move(block, dz=0, dx=0, dc=0):
    route = []
    for src in range(Z * 4):
        z, low = src // 4, src % 4
        route.append((src, ((z + dz) % Z) * 4 + (low ^ (dx * 2 + dc))))
    return lax.ppermute(block, "tp", route)


def core_move(block, zero, one):
    route = []
    for src in range(Z * 4):
        z, low = src // 4, src % 4
        dz, dx = (zero, one)[src % 2]
        route.append((src, ((z + dz) % Z) * 4 + (low ^ (dx * 2))))
    return lax.ppermute(block, "tp", route)


def from_bit(held, bit):
    return lax.ppermute(
        held, "ctx", [(c, c ^ (1 << bit)) for c in range(lax.axis_size("ctx"))]
    )


def in_bit_order(held, came, bit):
    upper = (lax.axis_index("ctx") >> bit) & 1 == 1
    axis = 0 if bit == 2 else 1
    return jnp.stack([jnp.where(upper, came, held), jnp.where(upper, held, came)], axis=axis)


def double_ctx(held, bit):
    return in_bit_order(held, from_bit(held, bit), bit)


def rolled(blocks, shift, axis):
    blocks = jnp.where(shift % 2 == 1, jnp.roll(blocks, 1, axis=axis), blocks)
    return jnp.where(shift >= 2, jnp.roll(blocks, 2, axis=axis), blocks)


def route_tables(expert_ids, route_weights, groups, capacity):
    tokens = expert_ids.shape[0]
    flat_ids = expert_ids.reshape(-1)
    numbers = jnp.arange(groups, dtype=jnp.int32)
    hits = (flat_ids[:, None] == numbers[None, :]).astype(jnp.int32)
    earlier = jnp.cumsum(hits, axis=0) - hits
    slot_rank = jnp.sum(earlier * hits, axis=1)
    targets = (flat_ids * capacity + slot_rank).reshape(tokens, 2)
    slot_index = jnp.arange(groups * capacity, dtype=jnp.int32)[:, None]
    first_hit = slot_index == targets[None, :, 0]
    second_hit = slot_index == targets[None, :, 1]
    placing = (first_hit | second_hit).astype(BF16)
    combine = jnp.where(first_hit, route_weights[None, :, 0], 0.0) + jnp.where(
        second_hit, route_weights[None, :, 1], 0.0
    )
    return (placing, combine)


def swiglu_grads(gate_act, up_act, hidden_grad):
    sigmoid_g = jax.nn.sigmoid(gate_act)
    grad_gate = (hidden_grad * up_act * sigmoid_g * (1.0 + gate_act * (1.0 - sigmoid_g))).astype(
        BF16
    )
    grad_up = (hidden_grad * gate_act * sigmoid_g).astype(BF16)
    return (grad_gate, grad_up)


def contract_last(left, right):
    return lax.dot_general(left, right, (((1,), (1,)), ((), ())), preferred_element_type=F32)


def add_bf16(*terms):
    total = terms[0].astype(F32)
    for term in terms[1:]:
        total = total + term.astype(F32)
    return total.astype(BF16)


def context_kernel(ids_ref, pieces_ref, first_ref, second_ref, before_ref, out_ref, total):
    step = pl.program_id(0)

    @pl.when(step == 0)
    def _():
        total[...] = before_ref[...]

    total[...] += contract_last(pieces_ref[0, 0], first_ref[...]) + contract_last(
        pieces_ref[0, 1], second_ref[...]
    )

    @pl.when(step == pl.num_programs(0) - 1)
    def _():
        out_ref[...] = total[...].astype(out_ref.dtype)


def context_grad(ids, pieces, weight, before, dtype):
    count, _, rows, width = pieces.shape
    outs = weight.shape[0]
    whole = pl.BlockSpec((rows, outs), lambda i, ids: (0, 0))
    return pl.pallas_call(
        context_kernel,
        grid_spec=pltpu.PrefetchScalarGridSpec(
            num_scalar_prefetch=1,
            grid=(count,),
            in_specs=[
                pl.BlockSpec((1, 2, rows, width), lambda i, ids: (i, 0, 0, 0)),
                pl.BlockSpec((outs, width), lambda i, ids: (0, ids[i])),
                pl.BlockSpec((outs, width), lambda i, ids: (0, ids[i + count])),
                whole,
            ],
            out_specs=whole,
            scratch_shapes=[pltpu.VMEM((rows, outs), F32)],
        ),
        out_shape=jax.ShapeDtypeStruct((rows, outs), dtype),
        compiler_params=pltpu.CompilerParams(vmem_limit_bytes=8 * 2**20),
        cost_estimate=pl.CostEstimate(
            flops=4 * count * rows * width * outs,
            bytes_accessed=4 * count * width * (outs + rows),
            transcendentals=0,
        ),
    )(ids, pieces, weight, weight, before)


def per_device(
    moe_input,
    grad_output,
    expert_ids,
    route_weights,
    w_gate,
    w_up,
    w_down,
    queries,
    keys_values,
    out_proj,
):
    ctx_count = lax.axis_size("ctx")
    tp_rank = lax.axis_index("tp")
    ctx_rank = lax.axis_index("ctx")
    my_z, my_x, my_core = tp_rank // 4, (tp_rank // 2) % 2, tp_rank % 2
    tokens, features = moe_input.shape
    capacity = tokens // 2
    slot_rows = ctx_count * capacity
    gate_w, up_w, down_w = w_gate[0], w_up[0], w_down[0]

    def chunk_of(dz, dx, dc):
        return ((my_z + dz) % Z) * 4 + (my_x ^ dx) * 2 + (my_core ^ dc)

    placing, combine = route_tables(expert_ids, route_weights, ctx_count, capacity)
    first_core = my_core == 0

    def in_core_order(own, other, axis):
        return jnp.concatenate(
            [jnp.where(first_core, own, other), jnp.where(first_core, other, own)], axis=axis
        )

    came = tp_move(jnp.where(first_core, moe_input, grad_output), dc=1)
    carried = in_core_order(jnp.where(first_core, grad_output, moe_input), came, 1)
    send = jnp.dot(placing, carried, preferred_element_type=F32).astype(BF16)
    got = lax.all_to_all(
        send.reshape(ctx_count, capacity, 2 * features), "ctx", split_axis=0, concat_axis=0, tiled=True
    ).reshape(slot_rows, 2 * features)

    heads_here = queries.shape[1] // HD
    group_size = HQ // KVH
    kv_group = tp_rank * heads_here // group_size
    mine_kv = lax.dynamic_slice_in_dim(keys_values, kv_group * 2 * HD, 2 * HD, 1)
    part_kv, got = lax.optimization_barrier((double_ctx(mine_kv, 2), got))
    all_kv = double_ctx(double_ctx(part_kv, 0), 1).reshape(-1, 2 * HD)
    seq_len = ctx_count * tokens
    query_heads = queries.reshape(tokens, heads_here, HD)
    inv_root = 1.0 / math.sqrt(HD)

    def attention_forward(all_kv):
        key_rows, value_rows = all_kv[:, :HD], all_kv[:, HD:]
        query_pos = ctx_rank * tokens + jnp.arange(tokens, dtype=jnp.int32)
        causal = query_pos[:, None] >= jnp.arange(seq_len, dtype=jnp.int32)[None, :]
        scores = (
            jnp.einsum("qhd,kd->hqk", query_heads, key_rows, preferred_element_type=F32) * inv_root
        )
        scores = jnp.where(causal[None], scores, -1e30)
        row_max = jnp.max(scores, axis=2, keepdims=True)
        exp_scores = jnp.exp(scores - row_max)
        attn_prob = exp_scores / jnp.sum(exp_scores, axis=2, keepdims=True)
        prob_b = attn_prob.astype(BF16)
        context_heads = jnp.einsum(
            "hqk,kd->qhd", prob_b, value_rows, preferred_element_type=F32
        ).astype(BF16)
        return context_heads, attn_prob, prob_b

    half, width = slot_rows // 2, 2 * features
    hop_1 = core_move(got, (1, 0), (0, 1))
    hop_2 = core_move(got, (3, 0), (1, 0))
    hop_3 = core_move(got, (0, 1), (3, 0))
    hop_3, all_kv = lax.optimization_barrier((hop_3, all_kv))
    far_low = core_move(jnp.where(first_core, hop_1[:half], hop_2[:half]), (1, 0), (1, 0))
    far_high = core_move(jnp.where(first_core, hop_2[half:], hop_3[half:]), (3, 0), (3, 0))
    hop_6 = core_move(hop_1, (0, 1), (1, 0))
    hop_7 = core_move(jnp.where(first_core, hop_2, hop_1), (0, 1), (3, 0))
    far = jnp.concatenate([far_low, far_high], axis=0)
    cross_low = core_move(jnp.where(first_core, far_low, hop_6[:half]), (0, 1), (1, 0))
    cross_high = core_move(jnp.where(first_core, far_high, hop_7[half:]), (0, 1), (3, 0))
    far_cross = jnp.concatenate([cross_low, cross_high], axis=0)

    arrivals = (
        (got, (0, 0), (0, 0)),
        (hop_1, (3, 0), (0, 1)),
        (hop_2, (1, 0), (3, 0)),
        (hop_3, (0, 1), (1, 0)),
        (far, (2, 0), (2, 0)),
        (hop_6, (3, 1), (3, 1)),
        (hop_7, (1, 1), (1, 1)),
        (far_cross, (2, 1), (2, 1)),
    )
    gate_act = up_act = hidden_grad = 0.0
    for block, dy_from, x_from in arrivals:
        crossed = tp_move(block, dc=1)
        x_rows = jnp.where(first_core, crossed, block)
        dy_rows = jnp.where(first_core, block, crossed)
        x_start = (chunk_of(*x_from, 0) // 2) * width
        dy_start = (chunk_of(*dy_from, 0) // 2) * width
        gate_rows = lax.dynamic_slice_in_dim(gate_w, x_start, width, 0)
        up_rows = lax.dynamic_slice_in_dim(up_w, x_start, width, 0)
        down_cols = lax.dynamic_slice_in_dim(down_w, dy_start, width, 1)
        gate_act = gate_act + jnp.dot(x_rows, gate_rows, preferred_element_type=F32)
        up_act = up_act + jnp.dot(x_rows, up_rows, preferred_element_type=F32)
        hidden_grad = hidden_grad + contract_last(dy_rows, down_cols)
    grad_gate, grad_up = swiglu_grads(gate_act, up_act, hidden_grad)

    def routed(core_0, core_1):
        gate_half = jnp.where(first_core, grad_gate[core_0], grad_gate[core_1])
        up_half = jnp.where(first_core, grad_up[core_0], grad_up[core_1])
        gate_part = contract_last(gate_w, gate_half).astype(BF16)
        return gate_part.astype(F32) + contract_last(up_w, up_half)

    lower, upper = slice(None, half), slice(half, None)
    sent = routed(upper, lower).astype(BF16)
    arrived = tp_move(sent, dc=1)
    grad_gate, sent = lax.optimization_barrier((grad_gate, sent))
    own = add_bf16(routed(lower, upper), arrived)

    cut = features

    def stack_for(zero, one):
        return jnp.where(first_core, jnp.stack(zero), jnp.stack(one))

    def low(rows):
        return rows[:cut]

    def high(rows):
        return rows[cut:]

    def both(rows):
        return (low(rows), high(rows))

    def chip_rows(dz, dx):
        return lax.dynamic_slice_in_dim(own, (chunk_of(dz, dx, 0) // 2) * width, width, 0)

    near = {dz: chip_rows(dz, 0) for dz in range(Z)}
    cross = {dz: chip_rows(dz, 1) for dz in range(Z)}
    loads = (
        stack_for(both(cross[2]), (low(near[2]), low(cross[2]))),
        stack_for((high(cross[1]), low(cross[3])), (high(near[2]), high(cross[2]))),
        stack_for((low(cross[1]), high(cross[3])), (high(near[1]), high(cross[1]))),
        stack_for(both(cross[0]), (low(near[3]), low(cross[3]))),
    )
    sum_1 = core_move(loads[0], (0, 1), (1, 0))
    sum_2 = core_move(loads[1], (0, 1), (3, 0))
    sum_3 = core_move(loads[2], (0, 1), (1, 0))
    sum_4 = core_move(loads[3], (0, 1), (3, 0))
    over_2 = [add_bf16(low(near[2]), sum_1[0]), add_bf16(high(near[2]), sum_1[1])]
    over_1 = [None, add_bf16(high(near[1]), sum_2[0])]
    over_3 = [add_bf16(low(near[3]), sum_2[1]), None]
    down = [add_bf16(high(near[3]), sum_2[0]), add_bf16(high(cross[3]), sum_2[1])]
    up = [add_bf16(low(near[1]), sum_1[0]), add_bf16(low(cross[1]), sum_1[1])]
    load_5 = stack_for((over_2[0], over_1[1]), down)
    load_6 = stack_for((over_2[1], over_3[0]), up)
    sum_3, sum_4, _, _ = lax.optimization_barrier((sum_3, sum_4, load_5, load_6))
    context_heads, attn_prob, prob_b = attention_forward(all_kv)
    context = context_heads.reshape(tokens, heads_here * HD)
    sum_4, context = lax.optimization_barrier((sum_4, context))
    part_context = double_ctx(context, 2)
    sum_5 = core_move(load_5, (1, 0), (3, 0))
    sum_6 = core_move(load_6, (3, 0), (1, 0))
    over_1[0] = add_bf16(low(near[1]), sum_3[0])
    over_3[1] = add_bf16(high(near[3]), sum_3[1])
    z_near = [add_bf16(low(near[0]), sum_4[0], sum_6[0]), add_bf16(high(near[0]), sum_3[0], sum_5[0])]
    z_cross = [
        add_bf16(low(cross[0]), sum_4[1], sum_6[1]),
        add_bf16(high(cross[0]), sum_3[1], sum_5[1]),
    ]
    sum_7 = core_move(jnp.where(first_core, add_bf16(over_1[0], sum_5[0]), z_cross[0]), (1, 0), (0, 1))
    sum_8 = core_move(jnp.where(first_core, add_bf16(over_3[1], sum_6[0]), z_cross[1]), (3, 0), (0, 1))
    zero_low = add_bf16(low(near[0]), sum_4[0], sum_6[1], sum_7)
    zero_high = add_bf16(high(near[0]), sum_4[1], sum_5[1], sum_8)
    one_low, one_high = add_bf16(z_near[0], sum_7), add_bf16(z_near[1], sum_8)
    total = jnp.concatenate(
        [jnp.where(first_core, zero_low, one_low), jnp.where(first_core, zero_high, one_high)], axis=0
    )
    left, right = total[:features], total[features:]
    came = tp_move(jnp.where(first_core, right, left), dc=1)
    own_slice = in_core_order(jnp.where(first_core, left, right), came, 1).T

    returned = lax.all_to_all(
        own_slice.reshape(ctx_count, capacity, features), "ctx", split_axis=0, concat_axis=0, tiled=True
    ).reshape(slot_rows, features)
    part_context = double_ctx(part_context, 0)
    moe_part = lax.dot_general(
        combine,
        returned.astype(F32),
        (((0,), (0,)), ((), ())),
        precision=lax.Precision.HIGHEST,
        preferred_element_type=F32,
    )
    grad_hidden = (grad_output.astype(F32) + moe_part).astype(BF16)
    grad_hidden, part_context = lax.optimization_barrier((grad_hidden, part_context))

    one_half, other_half = grad_hidden[: tokens // 2], grad_hidden[tokens // 2 :]
    low_pair = jnp.stack([one_half, tp_move(one_half, dx=1)])
    high_z = jnp.stack([other_half] + [tp_move(other_half, dz=dz) for dz in (1, 2, 3)])
    low_all = jnp.stack([low_pair] + [tp_move(low_pair, dz=dz) for dz in (1, 2, 3)])
    high_all = jnp.stack([high_z, tp_move(high_z, dx=1)], axis=1)
    same_core = jnp.concatenate([low_all, high_all], axis=2)
    swapped = jnp.where(my_x == 0, same_core, same_core[:, ::-1])
    ordered = jnp.stack([swapped[0], swapped[3], swapped[2], swapped[1]])
    ids = jnp.stack([(my_z + i) % Z * 4 + x * 2 for x in (0, 1) for i in range(Z)])
    grad_context = context_grad(
        ids + my_core, ordered, out_proj, jnp.zeros((tokens, features), F32), F32
    )
    grad_context, last_context = lax.optimization_barrier(
        (grad_context, from_bit(part_context, 1))
    )
    grad_context = context_grad(
        ids + 1 - my_core, tp_move(ordered, dc=1), out_proj, grad_context, BF16
    )


    all_context = in_bit_order(part_context, last_context, 1).reshape(-1, heads_here * HD)

    by_owner = rolled(ordered, my_z, 0)
    column_own = lax.all_to_all(
        by_owner.reshape(ctx_count, tokens, features), "ctx", split_axis=0, concat_axis=0, tiled=True
    ).reshape(seq_len, features)

    key_rows, value_rows = all_kv[:, :HD], all_kv[:, HD:]
    grad_heads = grad_context.reshape(tokens, heads_here, HD)
    grad_prob = jnp.einsum("qhd,kd->hqk", grad_heads, value_rows, preferred_element_type=F32)
    row_delta = jnp.sum(grad_heads.astype(F32) * context_heads.astype(F32), axis=2)
    grad_score = (attn_prob * (grad_prob - row_delta.T[:, :, None])).astype(BF16)
    grad_query = (
        jnp.einsum("hqk,kd->qhd", grad_score, key_rows, preferred_element_type=F32) * inv_root
    ).astype(BF16)
    grad_query = grad_query.reshape(tokens, heads_here * HD)
    key_term = (
        jnp.einsum("hqk,qhd->kd", grad_score, query_heads, preferred_element_type=F32) * inv_root
    )
    value_term = jnp.einsum("hqk,qhd->kd", prob_b, grad_heads, preferred_element_type=F32)
    kept_term = jnp.where(my_core == 0, key_term, value_term)
    sent_term = jnp.where(my_core == 0, value_term, key_term).astype(BF16)
    pair_term = (kept_term + tp_move(sent_term, dc=1).astype(F32)).astype(BF16)
    pair_term, column_own = lax.optimization_barrier((pair_term, column_own))
    column_other = tp_move(column_own, dc=1)
    kv_blocks = lax.all_to_all(
        pair_term.reshape(ctx_count, tokens, HD), "ctx", split_axis=0, concat_axis=0, tiled=True
    )

    def over_tokens(left):
        return lax.dot_general(
            left, all_context, (((0,), (0,)), ((), ())), preferred_element_type=F32
        ).astype(BF16)

    grad_out_proj_t = in_core_order(over_tokens(column_own), over_tokens(column_other), 0)
    kv_blocks, grad_out_proj_t = lax.optimization_barrier((kv_blocks, grad_out_proj_t))
    grad_kv = jnp.sum(kv_blocks.astype(F32), axis=0).astype(BF16)
    return (grad_hidden, grad_query, grad_kv, grad_out_proj_t)


def solution(mesh):
    in_specs = (
        P("ctx", "tp"),
        P("ctx", "tp"),
        P("ctx", None),
        P("ctx", None),
        P("ctx", None, "tp"),
        P("ctx", None, "tp"),
        P("ctx", "tp", None),
        P("ctx", "tp"),
        P("ctx", None),
        P("tp", None),
    )
    out_specs = (P("ctx", "tp"), P("ctx", "tp"), P("ctx", "tp"), P("ctx", "tp"))
    return jax.shard_map(
        per_device, mesh=mesh, in_specs=in_specs, out_specs=out_specs, check_vma=False
    )
```

```python
import math

import jax
import jax.numpy as jnp
from jax import lax
from jax.experimental import pallas as pl
from jax.experimental.pallas import tpu as pltpu
from jax.sharding import PartitionSpec as P

HQ = 48
KVH = 8
HD = 128
Z = 4
BF16 = jnp.bfloat16
F32 = jnp.float32


def tp_move(block, dz=0, dx=0, dc=0):
    route = []
    for src in range(Z * 4):
        z, low = src // 4, src % 4
        route.append((src, ((z + dz) % Z) * 4 + (low ^ (dx * 2 + dc))))
    return lax.ppermute(block, "tp", route)


def core_move(block, zero, one):
    route = []
    for src in range(Z * 4):
        z, low = src // 4, src % 4
        dz, dx = (zero, one)[src % 2]
        route.append((src, ((z + dz) % Z) * 4 + (low ^ (dx * 2))))
    return lax.ppermute(block, "tp", route)


def from_bit(held, bit):
    return lax.ppermute(
        held, "ctx", [(c, c ^ (1 << bit)) for c in range(lax.axis_size("ctx"))]
    )


def in_bit_order(held, came, bit):
    upper = (lax.axis_index("ctx") >> bit) & 1 == 1
    axis = 0 if bit == 2 else 1
    return jnp.stack([jnp.where(upper, came, held), jnp.where(upper, held, came)], axis=axis)


def double_ctx(held, bit):
    return in_bit_order(held, from_bit(held, bit), bit)


def rolled(blocks, shift, axis):
    blocks = jnp.where(shift % 2 == 1, jnp.roll(blocks, 1, axis=axis), blocks)
    return jnp.where(shift >= 2, jnp.roll(blocks, 2, axis=axis), blocks)


def route_tables(expert_ids, route_weights, groups, capacity):
    tokens = expert_ids.shape[0]
    flat_ids = expert_ids.reshape(-1)
    numbers = jnp.arange(groups, dtype=jnp.int32)
    hits = (flat_ids[:, None] == numbers[None, :]).astype(jnp.int32)
    earlier = jnp.cumsum(hits, axis=0) - hits
    slot_rank = jnp.sum(earlier * hits, axis=1)
    targets = (flat_ids * capacity + slot_rank).reshape(tokens, 2)
    slot_index = jnp.arange(groups * capacity, dtype=jnp.int32)[:, None]
    first_hit = slot_index == targets[None, :, 0]
    second_hit = slot_index == targets[None, :, 1]
    placing = (first_hit | second_hit).astype(BF16)
    combine = jnp.where(first_hit, route_weights[None, :, 0], 0.0) + jnp.where(
        second_hit, route_weights[None, :, 1], 0.0
    )
    return (placing, combine)


def swiglu_grads(gate_act, up_act, hidden_grad):
    sigmoid_g = jax.nn.sigmoid(gate_act)
    grad_gate = (hidden_grad * up_act * sigmoid_g * (1.0 + gate_act * (1.0 - sigmoid_g))).astype(
        BF16
    )
    grad_up = (hidden_grad * gate_act * sigmoid_g).astype(BF16)
    return (grad_gate, grad_up)


def contract_last(left, right):
    return lax.dot_general(left, right, (((1,), (1,)), ((), ())), preferred_element_type=F32)


def add_bf16(*terms):
    total = terms[0].astype(F32)
    for term in terms[1:]:
        total = total + term.astype(F32)
    return total.astype(BF16)


def context_kernel(ids_ref, pieces_ref, first_ref, second_ref, before_ref, out_ref, total):
    step = pl.program_id(0)

    @pl.when(step == 0)
    def _():
        total[...] = before_ref[...]

    total[...] += contract_last(pieces_ref[0, 0], first_ref[...]) + contract_last(
        pieces_ref[0, 1], second_ref[...]
    )

    @pl.when(step == pl.num_programs(0) - 1)
    def _():
        out_ref[...] = total[...].astype(out_ref.dtype)


def context_grad(ids, pieces, weight, before, dtype):
    count, _, rows, width = pieces.shape
    outs = weight.shape[0]
    whole = pl.BlockSpec((rows, outs), lambda i, ids: (0, 0))
    return pl.pallas_call(
        context_kernel,
        grid_spec=pltpu.PrefetchScalarGridSpec(
            num_scalar_prefetch=1,
            grid=(count,),
            in_specs=[
                pl.BlockSpec((1, 2, rows, width), lambda i, ids: (i, 0, 0, 0)),
                pl.BlockSpec((outs, width), lambda i, ids: (0, ids[i])),
                pl.BlockSpec((outs, width), lambda i, ids: (0, ids[i + count])),
                whole,
            ],
            out_specs=whole,
            scratch_shapes=[pltpu.VMEM((rows, outs), F32)],
        ),
        out_shape=jax.ShapeDtypeStruct((rows, outs), dtype),
        compiler_params=pltpu.CompilerParams(vmem_limit_bytes=8 * 2**20),
        cost_estimate=pl.CostEstimate(
            flops=4 * count * rows * width * outs,
            bytes_accessed=4 * count * width * (outs + rows),
            transcendentals=0,
        ),
    )(ids, pieces, weight, weight, before)


def per_device(
    moe_input,
    grad_output,
    expert_ids,
    route_weights,
    w_gate,
    w_up,
    w_down,
    queries,
    keys_values,
    out_proj,
):
    ctx_count = lax.axis_size("ctx")
    tp_rank = lax.axis_index("tp")
    ctx_rank = lax.axis_index("ctx")
    my_z, my_x, my_core = tp_rank // 4, (tp_rank // 2) % 2, tp_rank % 2
    tokens, features = moe_input.shape
    capacity = tokens // 2
    slot_rows = ctx_count * capacity
    gate_w, up_w, down_w = w_gate[0], w_up[0], w_down[0]

    def chunk_of(dz, dx, dc):
        return ((my_z + dz) % Z) * 4 + (my_x ^ dx) * 2 + (my_core ^ dc)

    placing, combine = route_tables(expert_ids, route_weights, ctx_count, capacity)
    first_core = my_core == 0

    def in_core_order(own, other, axis):
        return jnp.concatenate(
            [jnp.where(first_core, own, other), jnp.where(first_core, other, own)], axis=axis
        )

    came = tp_move(jnp.where(first_core, moe_input, grad_output), dc=1)
    carried = in_core_order(jnp.where(first_core, grad_output, moe_input), came, 1)
    send = jnp.dot(placing, carried, preferred_element_type=F32).astype(BF16)
    got = lax.all_to_all(
        send.reshape(ctx_count, capacity, 2 * features), "ctx", split_axis=0, concat_axis=0, tiled=True
    ).reshape(slot_rows, 2 * features)

    heads_here = queries.shape[1] // HD
    group_size = HQ // KVH
    kv_group = tp_rank * heads_here // group_size
    mine_kv = lax.dynamic_slice_in_dim(keys_values, kv_group * 2 * HD, 2 * HD, 1)
    part_kv, got = lax.optimization_barrier((double_ctx(mine_kv, 2), got))
    all_kv = double_ctx(double_ctx(part_kv, 0), 1).reshape(-1, 2 * HD)
    seq_len = ctx_count * tokens
    query_heads = queries.reshape(tokens, heads_here, HD)
    inv_root = 1.0 / math.sqrt(HD)

    def attention_forward(all_kv):
        key_rows, value_rows = all_kv[:, :HD], all_kv[:, HD:]
        query_pos = ctx_rank * tokens + jnp.arange(tokens, dtype=jnp.int32)
        causal = query_pos[:, None] >= jnp.arange(seq_len, dtype=jnp.int32)[None, :]
        scores = (
            jnp.einsum("qhd,kd->hqk", query_heads, key_rows, preferred_element_type=F32) * inv_root
        )
        scores = jnp.where(causal[None], scores, -1e30)
        row_max = jnp.max(scores, axis=2, keepdims=True)
        exp_scores = jnp.exp(scores - row_max)
        attn_prob = exp_scores / jnp.sum(exp_scores, axis=2, keepdims=True)
        prob_b = attn_prob.astype(BF16)
        context_heads = jnp.einsum(
            "hqk,kd->qhd", prob_b, value_rows, preferred_element_type=F32
        ).astype(BF16)
        return context_heads, attn_prob, prob_b

    half, width = slot_rows // 2, 2 * features
    hop_1 = core_move(got, (1, 0), (0, 1))
    hop_2 = core_move(got, (3, 0), (1, 0))
    hop_3 = core_move(got, (0, 1), (3, 0))
    hop_3, all_kv = lax.optimization_barrier((hop_3, all_kv))
    far_low = core_move(jnp.where(first_core, hop_1[:half], hop_2[:half]), (1, 0), (1, 0))
    far_high = core_move(jnp.where(first_core, hop_2[half:], hop_3[half:]), (3, 0), (3, 0))
    hop_6 = core_move(hop_1, (0, 1), (1, 0))
    hop_7 = core_move(jnp.where(first_core, hop_2, hop_1), (0, 1), (3, 0))
    far = jnp.concatenate([far_low, far_high], axis=0)
    cross_low = core_move(jnp.where(first_core, far_low, hop_6[:half]), (0, 1), (1, 0))
    cross_high = core_move(jnp.where(first_core, far_high, hop_7[half:]), (0, 1), (3, 0))
    far_cross = jnp.concatenate([cross_low, cross_high], axis=0)

    arrivals = (
        (got, (0, 0), (0, 0)),
        (hop_1, (3, 0), (0, 1)),
        (hop_2, (1, 0), (3, 0)),
        (hop_3, (0, 1), (1, 0)),
        (far, (2, 0), (2, 0)),
        (hop_6, (3, 1), (3, 1)),
        (hop_7, (1, 1), (1, 1)),
        (far_cross, (2, 1), (2, 1)),
    )
    gate_act = up_act = hidden_grad = 0.0
    for block, dy_from, x_from in arrivals:
        crossed = tp_move(block, dc=1)
        x_rows = jnp.where(first_core, crossed, block)
        dy_rows = jnp.where(first_core, block, crossed)
        x_start = (chunk_of(*x_from, 0) // 2) * width
        dy_start = (chunk_of(*dy_from, 0) // 2) * width
        gate_rows = lax.dynamic_slice_in_dim(gate_w, x_start, width, 0)
        up_rows = lax.dynamic_slice_in_dim(up_w, x_start, width, 0)
        down_cols = lax.dynamic_slice_in_dim(down_w, dy_start, width, 1)
        gate_act = gate_act + jnp.dot(x_rows, gate_rows, preferred_element_type=F32)
        up_act = up_act + jnp.dot(x_rows, up_rows, preferred_element_type=F32)
        hidden_grad = hidden_grad + contract_last(dy_rows, down_cols)
    grad_gate, grad_up = swiglu_grads(gate_act, up_act, hidden_grad)

    def routed(core_0, core_1):
        gate_half = jnp.where(first_core, grad_gate[core_0], grad_gate[core_1])
        up_half = jnp.where(first_core, grad_up[core_0], grad_up[core_1])
        return (contract_last(gate_w, gate_half) + contract_last(up_w, up_half)).astype(BF16)

    lower, upper = slice(None, half), slice(half, None)
    sent = routed(upper, lower)
    arrived = tp_move(sent, dc=1)
    grad_gate, sent = lax.optimization_barrier((grad_gate, sent))
    kept = routed(lower, upper)

    cut = features

    def stack_for(zero, one):
        return jnp.where(first_core, jnp.stack(zero), jnp.stack(one))

    def low(rows):
        return rows[:cut]

    def high(rows):
        return rows[cut:]

    def both(rows):
        return (low(rows), high(rows))

    near, cross = {}, {}
    for dz in (2, 1, 3, 0):

        def chip_rows(dx):
            start = (chunk_of(dz, dx, 0) // 2) * width
            return add_bf16(
                lax.dynamic_slice_in_dim(kept, start, width, 0),
                lax.dynamic_slice_in_dim(arrived, start, width, 0),
            )

        near[dz], cross[dz] = chip_rows(0), chip_rows(1)
        if dz == 2:
            load_1 = stack_for(both(cross[2]), (low(near[2]), low(cross[2])))
            load_1, kept = lax.optimization_barrier((load_1, kept))
    loads = (
        load_1,
        stack_for((high(cross[1]), low(cross[3])), (high(near[2]), high(cross[2]))),
        stack_for((low(cross[1]), high(cross[3])), (high(near[1]), high(cross[1]))),
        stack_for(both(cross[0]), (low(near[3]), low(cross[3]))),
    )
    sum_1 = core_move(loads[0], (0, 1), (1, 0))
    sum_2 = core_move(loads[1], (0, 1), (3, 0))
    sum_3 = core_move(loads[2], (0, 1), (1, 0))
    sum_4 = core_move(loads[3], (0, 1), (3, 0))
    over_2 = [add_bf16(low(near[2]), sum_1[0]), add_bf16(high(near[2]), sum_1[1])]
    over_1 = [None, add_bf16(high(near[1]), sum_2[0])]
    over_3 = [add_bf16(low(near[3]), sum_2[1]), None]
    down = [add_bf16(high(near[3]), sum_2[0]), add_bf16(high(cross[3]), sum_2[1])]
    up = [add_bf16(low(near[1]), sum_1[0]), add_bf16(low(cross[1]), sum_1[1])]
    load_5 = stack_for((over_2[0], over_1[1]), down)
    load_6 = stack_for((over_2[1], over_3[0]), up)
    sum_3, sum_4, _, _ = lax.optimization_barrier((sum_3, sum_4, load_5, load_6))
    context_heads, attn_prob, prob_b = attention_forward(all_kv)
    context = context_heads.reshape(tokens, heads_here * HD)
    sum_4, context = lax.optimization_barrier((sum_4, context))
    part_context = double_ctx(context, 2)
    sum_5 = core_move(load_5, (1, 0), (3, 0))
    sum_6 = core_move(load_6, (3, 0), (1, 0))
    over_1[0] = add_bf16(low(near[1]), sum_3[0])
    over_3[1] = add_bf16(high(near[3]), sum_3[1])
    z_near = [add_bf16(low(near[0]), sum_4[0], sum_6[0]), add_bf16(high(near[0]), sum_3[0], sum_5[0])]
    z_cross = [
        add_bf16(low(cross[0]), sum_4[1], sum_6[1]),
        add_bf16(high(cross[0]), sum_3[1], sum_5[1]),
    ]
    sum_7 = core_move(jnp.where(first_core, add_bf16(over_1[0], sum_5[0]), z_cross[0]), (1, 0), (0, 1))
    sum_8 = core_move(jnp.where(first_core, add_bf16(over_3[1], sum_6[0]), z_cross[1]), (3, 0), (0, 1))
    zero_low = add_bf16(low(near[0]), sum_4[0], sum_6[1], sum_7)
    zero_high = add_bf16(high(near[0]), sum_4[1], sum_5[1], sum_8)
    one_low, one_high = add_bf16(z_near[0], sum_7), add_bf16(z_near[1], sum_8)
    total = jnp.concatenate(
        [jnp.where(first_core, zero_low, one_low), jnp.where(first_core, zero_high, one_high)], axis=0
    )
    left, right = total[:features], total[features:]
    came = tp_move(jnp.where(first_core, right, left), dc=1)
    own_slice = in_core_order(jnp.where(first_core, left, right), came, 1).T

    returned = lax.all_to_all(
        own_slice.reshape(ctx_count, capacity, features), "ctx", split_axis=0, concat_axis=0, tiled=True
    ).reshape(slot_rows, features)
    part_context = double_ctx(part_context, 0)
    returned, part_context = lax.optimization_barrier((returned, part_context))
    moe_part = lax.dot_general(
        combine,
        returned.astype(F32),
        (((0,), (0,)), ((), ())),
        precision=lax.Precision.HIGHEST,
        preferred_element_type=F32,
    )
    grad_hidden = (grad_output.astype(F32) + moe_part).astype(BF16)

    one_half, other_half = grad_hidden[: tokens // 2], grad_hidden[tokens // 2 :]
    low_pair = jnp.stack([one_half, tp_move(one_half, dx=1)])
    high_z = jnp.stack([other_half] + [tp_move(other_half, dz=dz) for dz in (1, 2, 3)])
    low_all = jnp.stack([low_pair] + [tp_move(low_pair, dz=dz) for dz in (1, 2, 3)])
    high_all = jnp.stack([high_z, tp_move(high_z, dx=1)], axis=1)
    same_core = jnp.concatenate([low_all, high_all], axis=2)
    swapped = jnp.where(my_x == 0, same_core, same_core[:, ::-1])
    ordered = jnp.stack([swapped[0], swapped[3], swapped[2], swapped[1]])
    ids = jnp.stack([(my_z + i) % Z * 4 + x * 2 for x in (0, 1) for i in range(Z)])
    grad_context = context_grad(
        ids + my_core, ordered, out_proj, jnp.zeros((tokens, features), F32), F32
    )
    grad_context, last_context = lax.optimization_barrier(
        (grad_context, from_bit(part_context, 1))
    )
    grad_context = context_grad(
        ids + 1 - my_core, tp_move(ordered, dc=1), out_proj, grad_context, BF16
    )

    all_context = in_bit_order(part_context, last_context, 1).reshape(-1, heads_here * HD)

    by_owner = rolled(ordered, my_z, 0)
    column_own = lax.all_to_all(
        by_owner.reshape(ctx_count, tokens, features), "ctx", split_axis=0, concat_axis=0, tiled=True
    ).reshape(seq_len, features)

    key_rows, value_rows = all_kv[:, :HD], all_kv[:, HD:]
    grad_heads = grad_context.reshape(tokens, heads_here, HD)
    grad_prob = jnp.einsum("qhd,kd->hqk", grad_heads, value_rows, preferred_element_type=F32)
    row_delta = jnp.sum(grad_heads.astype(F32) * context_heads.astype(F32), axis=2)
    grad_score = (attn_prob * (grad_prob - row_delta.T[:, :, None])).astype(BF16)
    grad_query = (
        jnp.einsum("hqk,kd->qhd", grad_score, key_rows, preferred_element_type=F32) * inv_root
    ).astype(BF16)
    grad_query = grad_query.reshape(tokens, heads_here * HD)
    key_term = (
        jnp.einsum("hqk,qhd->kd", grad_score, query_heads, preferred_element_type=F32) * inv_root
    )
    value_term = jnp.einsum("hqk,qhd->kd", prob_b, grad_heads, preferred_element_type=F32)
    kept_term = jnp.where(my_core == 0, key_term, value_term)
    sent_term = jnp.where(my_core == 0, value_term, key_term).astype(BF16)
    pair_term = (kept_term + tp_move(sent_term, dc=1).astype(F32)).astype(BF16)
    pair_term, column_own = lax.optimization_barrier((pair_term, column_own))
    column_other = tp_move(column_own, dc=1)
    kv_blocks = lax.all_to_all(
        pair_term.reshape(ctx_count, tokens, HD), "ctx", split_axis=0, concat_axis=0, tiled=True
    )

    def over_tokens(left):
        return lax.dot_general(
            left, all_context, (((0,), (0,)), ((), ())), preferred_element_type=F32
        ).astype(BF16)

    grad_out_proj_t = in_core_order(over_tokens(column_own), over_tokens(column_other), 0)
    kv_blocks, grad_out_proj_t = lax.optimization_barrier((kv_blocks, grad_out_proj_t))
    grad_kv = jnp.sum(kv_blocks.astype(F32), axis=0).astype(BF16)
    return (grad_hidden, grad_query, grad_kv, grad_out_proj_t)


def solution(mesh):
    in_specs = (
        P("ctx", "tp"),
        P("ctx", "tp"),
        P("ctx", None),
        P("ctx", None),
        P("ctx", None, "tp"),
        P("ctx", None, "tp"),
        P("ctx", "tp", None),
        P("ctx", "tp"),
        P("ctx", None),
        P("tp", None),
    )
    out_specs = (P("ctx", "tp"), P("ctx", "tp"), P("ctx", "tp"), P("ctx", "tp"))
    return jax.shard_map(
        per_device, mesh=mesh, in_specs=in_specs, out_specs=out_specs, check_vma=False
    )
```
